32 devices in a mesh: row: 8 (over y, x, core), col: 4 (over z).
Axes of the slice: x: 2, y: 2, z: 4, core: 2. Of those that a mesh axis runs over, the one named last changes fastest.
Arguments:
- block_values: bfloat16 [8, 4, 192, 128, 128], P('row', 'col'), may hold values from -0.0625 to 0.0625
- block_rows: int32 [8, 4, 192], P('row', 'col'), may hold values from 0 to 511, as said below
- block_cols: int32 [8, 4, 192], P('row', 'col'), may hold values from 0 to 511, as said below
- block_counts: int32 [8, 4], P('row', 'col'), may hold values from 48 to 192, as said below
- precond: float32 [4, 128, 128, 128], P('col', 'row')
- right_side: float32 [4, 128, 32, 128], P('col', 'row'), may hold values from -6 to 6
Outputs:
- solution: float32 [4, 128, 32, 128], P('col', 'row')
The draws below stay inside these ranges and needn't reach their ends.
Inputs may be any that keep to these rules, and one draw needn't show every extreme that they name: `block_rows`: the block rows of device (r, c) lie in [c * 128, (c + 1) * 128); positions may repeat; for each j, at most 36 of a device's 192 slots have (row mod 128) // 16 == j, and in every index of col some j has exactly 36 such slots on every device. `block_cols`: every block column q of device (r, c) has (q mod 128) // 16 == r; positions may repeat. `block_counts`: slots at or past a device's count are unused; some device uses all 192 slots.
All inputs are finite; a program needn't handle non-finite values.
Results may differ from the reference program's by a relative error of at most 0.00073.
Values may be sent and summed in bfloat16 or wider, within the bound.
No kernel may reach another device: no remote copies, remote signals or barrier semaphores. Data moves between devices by JAX's collectives and lax.ppermute only.
A program may use at most 64 MiB of HBM per device.

```python
import jax
import jax.numpy as jnp
from jax import lax

BS = 128
OWN_DEV = 16
BLK_DEV = 192
RHS = 32
ITERS = 3
RGRP = 128
CSET = 64
NB = 512
CAP = 36
N_ROW = 8
N_COL = 4


def draw_block_rows(key, part):
    total_devices = N_ROW * N_COL
    entries = N_ROW * CAP
    dest_of_entry = jnp.arange(entries, dtype=jnp.int32) // CAP
    hot_dest = jax.random.randint(jax.random.fold_in(key, 13), (N_COL,), 0, N_ROW).astype(jnp.int32)
    device_keys = jax.random.split(jax.random.fold_in(key, 17), total_devices)
    ranks = jax.vmap(lambda one_key: jax.random.permutation(one_key, entries))(device_keys).astype(jnp.int32)
    col_of_device = jnp.arange(total_devices, dtype=jnp.int32) % N_COL
    is_hot = (dest_of_entry[None, :] == hot_dest[col_of_device][:, None]).astype(jnp.int32)
    scores = ranks - entries * is_hot
    order = jnp.argsort(scores, axis=1, stable=True)[:, :BLK_DEV]
    dests = dest_of_entry[order]
    inner = jax.random.randint(jax.random.fold_in(key, 11), (total_devices, BLK_DEV), 0, OWN_DEV).astype(jnp.int32)
    local_rows = dests * OWN_DEV + inner
    result = col_of_device[:, None] * RGRP + local_rows
    return result.reshape(N_ROW, N_COL, BLK_DEV).astype(jnp.int32)


def draw_block_cols(key, part):
    local_cols = jax.random.randint(jax.random.fold_in(key, 23), (N_ROW, N_COL, BLK_DEV), 0, CSET)
    owner = jnp.arange(N_ROW, dtype=jnp.int32)[:, None, None]
    return (local_cols // OWN_DEV * RGRP + owner * OWN_DEV + local_cols % OWN_DEV).astype(jnp.int32)


def draw_block_counts(key, part):
    total_devices = N_ROW * N_COL
    base = jax.random.randint(jax.random.fold_in(key, 31), (total_devices,), BLK_DEV // 4, BLK_DEV + 1)
    fullest = jax.random.randint(jax.random.fold_in(key, 37), (), 0, total_devices)
    base = jnp.where(jnp.arange(total_devices) == fullest, BLK_DEV, base)
    return base.reshape(N_ROW, N_COL).astype(jnp.int32)


def draw_precond(key, part):
    eye = jnp.eye(BS, dtype=jnp.float32)
    noise = jax.random.normal(jax.random.fold_in(key, 47), (N_COL, RGRP, BS, BS), jnp.float32)
    return (0.8 * eye + 0.15 * noise / jnp.sqrt(BS * 1.0)).astype(jnp.float32)


def shard_levels(own_key, shape, cuts, smallest, largest):
    gain = 1.0
    for position, parts in cuts:
        draws = jax.random.uniform(jax.random.fold_in(jax.random.fold_in(own_key, 6), position), (parts,), jnp.float32, smallest / len(cuts), largest / len(cuts))
        gain = gain * jnp.repeat(jnp.exp(draws), shape[position] // parts).reshape((-1,) + (1,) * (len(shape) - 1 - position))
    return gain


def scatter_about(stream_key, shape, width, bound, pieces=(), kind=jnp.bfloat16):
    array = width * jax.random.normal(stream_key, shape, jnp.float32)
    if pieces:
        array = array * shard_levels(stream_key, shape, pieces, -0.22, 0.18)
    return jnp.clip(array, -bound, bound).astype(kind)


def setup_inputs(seed: int = 0) -> dict:
    arg_keys = jax.random.split(jax.random.key(seed), 7)
    block_values = scatter_about(arg_keys[0], (N_ROW, N_COL, BLK_DEV, BS, BS), (7 * BS * BLK_DEV // OWN_DEV) ** -0.5, 0.0625, ((0, 8), (1, 4)))
    block_rows = draw_block_rows(jax.random.fold_in(arg_keys[6], 71), 0)
    block_cols = draw_block_cols(jax.random.fold_in(arg_keys[6], 71), 0)
    block_counts = draw_block_counts(jax.random.fold_in(arg_keys[6], 71), 0)
    precond = draw_precond(jax.random.fold_in(arg_keys[6], 71), 0)
    right_side = scatter_about(arg_keys[5], (N_COL, RGRP, RHS, BS), 1.0, 6.0, ((0, 4), (1, 8)), jnp.float32)
    return {"block_values": block_values, "block_rows": block_rows, "block_cols": block_cols, "block_counts": block_counts, "precond": precond, "right_side": right_side}


def apply_blocks(matrix, field):
    return jnp.einsum("poi,pki->pko", matrix.astype(jnp.float32), field.astype(jnp.float32), precision=lax.Precision.HIGHEST)


def reference(block_values, block_rows, block_cols, block_counts, precond, right_side):
    total_devices = N_ROW * N_COL
    rhs_flat = right_side.reshape(NB, RHS, BS).astype(jnp.float32)
    inverse = precond.reshape(NB, BS, BS).astype(jnp.float32)
    values = block_values.reshape(total_devices, BLK_DEV, BS, BS)
    rows = block_rows.reshape(total_devices, BLK_DEV).astype(jnp.int32)
    cols = block_cols.reshape(total_devices, BLK_DEV).astype(jnp.int32)
    counts = block_counts.reshape(total_devices).astype(jnp.int32)
    slot_ids = jnp.arange(BLK_DEV, dtype=jnp.int32)
    solution = apply_blocks(inverse, rhs_flat)
    for step in range(ITERS):
        rounded = lax.optimization_barrier(solution.astype(jnp.bfloat16)).astype(jnp.float32)

        def add_device(accum, inputs):
            vals, rr, cc, count = inputs
            xg = rounded[cc]
            contrib = jnp.einsum("soi,ski->sko", vals.astype(jnp.float32), xg)
            contrib = jnp.where((slot_ids < count)[:, None, None], contrib, jnp.zeros_like(contrib))
            return accum.at[rr].add(contrib), None

        product, _ = lax.scan(add_device, jnp.zeros((NB, RHS, BS), jnp.float32), (values, rows, cols, counts))
        residual = rhs_flat - solution - product
        solution = solution + apply_blocks(inverse, residual)
    return solution.reshape(N_COL, RGRP, RHS, BS)
```

```python
import functools

import jax
import jax.numpy as jnp
from jax import lax
from jax.experimental import pallas as pl
from jax.experimental.pallas import tpu as pltpu
from jax.sharding import PartitionSpec as P

ITERS = 3
UNROLL = 8
CORES = 2
VMEM_LIMIT = 48 * 1024 * 1024

NT = (((1,), (1,)), ((), ()))


def in_vmem():
    return pl.BlockSpec(memory_space=pltpu.VMEM)


def in_smem():
    return pl.BlockSpec(memory_space=pltpu.SMEM)


def params():
    return pltpu.CompilerParams(vmem_limit_bytes=VMEM_LIMIT)


def split(value):
    high = value.astype(jnp.bfloat16)
    low = (value - high.astype(jnp.float32)).astype(jnp.bfloat16)
    return high, low


def times_block(field, high, low):
    field_high, field_low = split(field)
    rhs = field.shape[0]
    both = jnp.concatenate([field_high, field_low], axis=0)
    first = lax.dot_general(both, high, NT, preferred_element_type=jnp.float32)
    second = lax.dot_general(field_high, low, NT, preferred_element_type=jnp.float32)
    return first[:rhs] + (first[rhs:] + second)


def start_kernel(precond_ref, rhs_ref, high_ref, low_ref, sol_ref, rounded_ref):
    for p in range(rhs_ref.shape[0]):
        high, low = split(precond_ref[p])
        high_ref[p] = high
        low_ref[p] = low
        value = times_block(rhs_ref[p], high, low)
        sol_ref[p] = value
        rounded_ref[p] = value.astype(jnp.bfloat16)


def apply_kernel(pieces, high_ref, low_ref, rhs_ref, sol_ref, own_ref, *refs):
    piece_refs, (new_ref, rounded_ref) = refs[:pieces], refs[pieces:]
    for p in range(rhs_ref.shape[0]):
        product = own_ref[p]
        for piece_ref in piece_refs:
            product = product + piece_ref[p].astype(jnp.float32)
        before = sol_ref[p]
        residual = rhs_ref[p] - before - product
        value = before + times_block(residual, high_ref[p], low_ref[p])
        new_ref[p] = value
        rounded_ref[p] = value.astype(jnp.bfloat16)


def order_kernel(group, owned, groups, position_ref, count_ref, rows_ref, cols_ref,
                 slot_out, row_out, col_out, total_out):
    used = count_ref[0]
    core = lax.rem(position_ref[0], CORES)
    mine = position_ref[1]
    trash = group // CORES

    def fill(at, carry):
        for half in range(CORES):
            slot_out[half, at] = 0
            row_out[half, at] = trash
            col_out[half, at] = 0
        return carry

    lax.fori_loop(0, slot_out.shape[1], fill, 0)

    def place(slot, counts):
        row = lax.rem(rows_ref[slot], group)
        owner = lax.div(row, owned)
        half = jnp.where(lax.rem(owner, CORES) == core, 1, 0)
        at = jnp.where(half == 1, counts[1], counts[0])
        column = cols_ref[slot]
        source = lax.div(column, group)
        away = lax.rem(mine - source + groups, groups)
        slot_out[half, at] = slot
        row_out[half, at] = lax.div(owner, CORES) * owned + lax.rem(row, owned)
        col_out[half, at] = away * owned + lax.rem(column, owned)
        return counts[0] + (1 - half), counts[1] + half

    zero = jnp.int32(0)
    first, second = lax.fori_loop(0, used, place, (zero, zero))
    total_out[0] = first
    total_out[1] = second


def product_kernel(half, pieces, slot_ref, row_ref, col_ref, total_ref, values_ref, *refs):
    piece_refs, (out_ref, field, total) = refs[:pieces], refs[pieces:]
    owned = piece_refs[0].shape[0]
    for index, piece_ref in enumerate(piece_refs):
        field[pl.ds(index * owned, owned)] = piece_ref[...]
    total[...] = jnp.zeros_like(total)

    def step(chunk, carry):
        terms = []
        for lane in range(UNROLL):
            at = chunk * UNROLL + lane
            term = lax.dot_general(
                field[col_ref[half, at]], values_ref[slot_ref[half, at]], NT,
                preferred_element_type=jnp.float32)
            terms.append((row_ref[half, at], term))
        for row, term in terms:
            total[row] += term
        return carry

    chunks = lax.div(total_ref[half] + UNROLL - 1, UNROLL)
    lax.fori_loop(0, chunks, step, 0)
    out_ref[...] = total[pl.ds(0, out_ref.shape[0])].astype(out_ref.dtype)


def combine_kernel(chips, position_ref, own_ref, other_ref, keep_ref, *send_refs):
    chip = lax.div(position_ref[0], CORES)
    owned = keep_ref.shape[0]
    for shift in range(chips):
        dest = partner(chip, shift, chips)
        at = pl.ds(dest * owned, owned)
        value = own_ref[at] + other_ref[at].astype(jnp.float32)
        if shift == 0:
            keep_ref[...] = value
        else:
            send_refs[shift - 1][...] = value.astype(jnp.bfloat16)


def partner(chip, shift, chips):
    if chips & (chips - 1) == 0:
        return chip ^ shift
    return (chip + shift) % chips


def per_device(block_values, block_rows, block_cols, block_counts, precond, right_side):
    owned, rhs, size = right_side.shape[1:]
    row_devices = lax.axis_size("row")
    groups = lax.axis_size("col")
    chips = row_devices // CORES
    group = owned * row_devices
    half_rows = chips * owned
    slots = block_values.shape[2]
    padded = (slots + UNROLL - 1) // UNROLL * UNROLL
    values = block_values[0, 0]
    inverse = precond[0]
    rhs_own = right_side[0]
    position = jnp.stack([lax.axis_index("row"), lax.axis_index("col")]).astype(jnp.int32)

    field_type = jax.ShapeDtypeStruct((owned, rhs, size), jnp.float32)
    rounded_type = jax.ShapeDtypeStruct((owned, rhs, size), jnp.bfloat16)
    matrix_type = jax.ShapeDtypeStruct((owned, size, size), jnp.bfloat16)

    high, low, sol, rounded = pl.pallas_call(
        start_kernel,
        out_shape=[matrix_type, matrix_type, field_type, rounded_type],
        in_specs=[in_vmem()] * 2,
        out_specs=[in_vmem()] * 4,
        compiler_params=params(),
        name="start",
    )(inverse, rhs_own)

    index_type = jax.ShapeDtypeStruct((CORES, padded), jnp.int32)
    lists = pl.pallas_call(
        functools.partial(order_kernel, group, owned, groups),
        out_shape=[index_type] * 3 + [jax.ShapeDtypeStruct((CORES,), jnp.int32)],
        in_specs=[in_smem()] * 4,
        out_specs=[in_smem()] * 4,
        compiler_params=params(),
        name="order",
    )(position, block_counts[0], block_rows[0, 0], block_cols[0, 0])

    def product(half, dtype, fields):
        return pl.pallas_call(
            functools.partial(product_kernel, half, len(fields)),
            out_shape=jax.ShapeDtypeStruct((half_rows, rhs, size), dtype),
            in_specs=[in_smem()] * 4 + [in_vmem()] * (1 + len(fields)),
            out_specs=in_vmem(),
            scratch_shapes=[
                pltpu.VMEM((groups * owned, rhs, size), jnp.bfloat16),
                pltpu.VMEM((half_rows + 1, rhs, size), jnp.float32),
            ],
            compiler_params=params(),
            name="product%d" % half,
            cost_estimate=pl.CostEstimate(
                flops=slots * rhs * size * size, bytes_accessed=slots * size * size, transcendentals=0),
        )(*lists, values, *fields)

    swap = [(r, r ^ 1) for r in range(row_devices)]
    for step in range(ITERS):
        fields = [rounded]
        for shift in range(1, groups):
            ring = [(c, (c + shift) % groups) for c in range(groups)]
            fields.append(lax.ppermute(rounded, "col", ring))
        outgoing = product(0, jnp.bfloat16, fields)
        incoming = lax.ppermute(outgoing, "row", swap)
        own = product(1, jnp.float32, fields)
        keep, *sends = pl.pallas_call(
            functools.partial(combine_kernel, chips),
            out_shape=[field_type] + [rounded_type] * (chips - 1),
            in_specs=[in_smem()] + [in_vmem()] * 2,
            out_specs=[in_vmem()] * chips,
            compiler_params=params(),
            name="combine",
        )(position, own, incoming)
        pieces = []
        for shift in range(1, chips):
            pairs = [
                (chip * CORES + core, partner(chip, shift, chips) * CORES + core)
                for chip in range(chips) for core in range(CORES)
            ]
            pieces.append(lax.ppermute(sends[shift - 1], "row", pairs))
        sol, rounded = pl.pallas_call(
            functools.partial(apply_kernel, len(pieces)),
            out_shape=[field_type, rounded_type],
            in_specs=[in_vmem()] * (5 + len(pieces)),
            out_specs=[in_vmem()] * 2,
            compiler_params=params(),
            name="apply",
        )(high, low, rhs_own, sol, keep, *pieces)
    return sol[None]


def solution(mesh):
    placed = (
        P("row", "col", None, None, None),
        P("row", "col", None),
        P("row", "col", None),
        P("row", "col"),
        P("col", "row", None, None),
        P("col", "row", None, None),
    )
    return jax.shard_map(
        per_device,
        mesh=mesh,
        in_specs=placed,
        out_specs=P("col", "row", None, None),
        check_vma=False,
    )
```

```python
import functools

import jax
import jax.numpy as jnp
import numpy as np
from jax import lax
from jax.experimental import pallas as pl
from jax.experimental.pallas import tpu as pltpu
from jax.sharding import PartitionSpec as P

ITERS = 3
UNROLL = 8
CORES = 2
VMEM_LIMIT = 24 * 1024 * 1024

NT = (((1,), (1,)), ((), ()))


def in_vmem():
    return pl.BlockSpec(memory_space=pltpu.VMEM)


def in_hbm():
    return pl.BlockSpec(memory_space=pltpu.HBM)


def in_smem():
    return pl.BlockSpec(memory_space=pltpu.SMEM)


def stay_in_hbm(array):
    return pltpu.with_memory_space_constraint(array, pltpu.HBM)


def params():
    return pltpu.CompilerParams(vmem_limit_bytes=VMEM_LIMIT)


def split(value):
    high = value.astype(jnp.bfloat16)
    low = (value - high.astype(jnp.float32)).astype(jnp.bfloat16)
    return high, low


def times_block(field, high, low):
    field_high, field_low = split(field)
    rhs = field.shape[0]
    both = jnp.concatenate([field_high, field_low], axis=0)
    first = lax.dot_general(both, high, NT, preferred_element_type=jnp.float32)
    second = lax.dot_general(field_high, low, NT, preferred_element_type=jnp.float32)
    return first[:rhs] + (first[rhs:] + second)


def partner(chip, shift, chips):
    if chips & (chips - 1) == 0:
        return chip ^ shift
    return (chip + shift) % chips


def halves(value, size):
    if size & (size - 1) == 0:
        return lax.shift_right_logical(value, size.bit_length() - 1), value & (size - 1)
    return lax.div(value, size), lax.rem(value, size)


def gather_stages(groups, parts):
    near = sorted({shift for shift in (1, groups - 1) if 0 < shift < groups})
    far = [shift for shift in range(1, groups) if shift not in near]
    stages = [[(part, 0) for part in range(parts)]]
    for part in range(parts - 1):
        stages.append([(part, shift) for shift in near + far])
    stages.append([(parts - 1, shift) for shift in near])
    stages.append([(parts - 1, shift) for shift in far])
    return [stage for stage in stages if stage]


def start_kernel(parts, precond_hbm, rhs_hbm, high_ref, low_ref, *refs):
    sol_refs, refs = refs[:parts], refs[parts:]
    left_refs, refs = refs[:parts], refs[parts:]
    rounded_refs, (precond_ref, rhs_ref, sems) = refs[:parts], refs[parts:]
    owned = rhs_ref.shape[0]
    loads_total = sems.shape[0] - 1
    each = owned // loads_total
    loads = [pltpu.make_async_copy(rhs_hbm, rhs_ref, sems.at[loads_total])]
    for load in range(loads_total):
        at = pl.ds(load * each, each)
        loads.append(pltpu.make_async_copy(precond_hbm.at[at], precond_ref.at[at], sems.at[load]))
    for load in loads:
        load.start()
    loads[0].wait()
    for load in range(loads_total):
        loads[1 + load].wait()
        for p in range(load * each, (load + 1) * each):
            part, inner = divmod(p, owned // parts)
            high, low = split(precond_ref[p])
            high_ref[p] = high
            low_ref[p] = low
            value = times_block(rhs_ref[p], high, low)
            sol_refs[part][inner] = value
            left_refs[part][inner] = rhs_ref[p]
            rounded_refs[part][inner] = value.astype(jnp.bfloat16)


def updated(p, inner, pieces, high_ref, low_ref, left_ref, sol_ref, keep_ref):
    left = left_ref[inner]
    for piece_ref in pieces:
        left = left - piece_ref[inner].astype(jnp.float32)
    before = sol_ref[inner]
    residual = left - before - keep_ref[inner]
    return before + times_block(residual, high_ref[p], low_ref[p]), left


def apply_kernel(base, pieces, high_ref, low_ref, left_ref, sol_ref, keep_ref, *refs):
    piece_refs, (new_ref, new_left_ref, rounded_ref) = refs[:pieces], refs[pieces:]
    for inner in range(sol_ref.shape[0]):
        value, left = updated(base + inner, inner, piece_refs, high_ref, low_ref, left_ref, sol_ref, keep_ref)
        new_ref[inner] = value
        new_left_ref[inner] = left
        rounded_ref[inner] = value.astype(jnp.bfloat16)


def finish_kernel(base, pieces, earlier, high_ref, low_ref, left_ref, sol_ref, keep_ref, *refs):
    piece_refs, refs = refs[:pieces], refs[pieces:]
    done_refs, (out_hbm, value_ref, sems) = refs[:earlier], refs[earlier:]
    each = sol_ref.shape[0]
    stores = [
        pltpu.make_async_copy(done, out_hbm.at[pl.ds(part * each, each)], sems.at[part])
        for part, done in enumerate(done_refs)
    ]
    for store in stores:
        store.start()
    for inner in range(each):
        value_ref[inner], _ = updated(
            base + inner, inner, piece_refs, high_ref, low_ref, left_ref, sol_ref, keep_ref)
    last = pltpu.make_async_copy(value_ref, out_hbm.at[pl.ds(base, each)], sems.at[earlier])
    last.start()
    for store in stores:
        store.wait()
    last.wait()


def order_kernel(group, owned, groups, parts, bits, table_ref, position_ref, count_ref, rows_ref, cols_ref,
                 values_hbm, list_out, total_out, values_out, sem):
    load = pltpu.make_async_copy(values_hbm, values_out, sem)
    load.start()
    core = position_ref[0] & (CORES - 1)
    mine = position_ref[1]
    each = owned // parts
    row_bits, col_bits = bits
    lists = total_out.shape[0]
    trash = (group // CORES // parts) << col_bits

    def clear(index, carry):
        total_out[index] = 0
        return carry

    lax.fori_loop(0, lists, clear, 0)

    def place(slot, carry):
        owner, row_owned = halves(halves(rows_ref[0, 0, slot], group)[1], owned)
        row_part, row_inner = halves(row_owned, each)
        source, rest = halves(cols_ref[0, 0, slot], group)
        col_part, col_inner = halves(halves(rest, owned)[1], each)
        half = 1 - ((owner & (CORES - 1)) ^ core)
        shift = mine - source
        shift = jnp.where(shift < 0, shift + groups, shift)
        stage, base = halves(table_ref[col_part * groups + shift], 1 << col_bits)
        which = (stage * parts + row_part) * CORES + half
        row = lax.shift_right_logical(owner, 1) * each + row_inner
        at = total_out[which]
        list_out[which, at] = (((slot << row_bits) | row) << col_bits) | (base + col_inner)
        total_out[which] = at + 1
        return carry

    lax.fori_loop(0, count_ref[0, 0], place, 0)

    def close(index, carry):
        for extra in range(UNROLL):
            list_out[index, total_out[index] + extra] = trash
        return carry

    lax.fori_loop(0, lists, close, 0)
    load.wait()


def add_products(which, bits, list_ref, total_ref, values_ref, field_ref, total):
    row_bits, col_bits = bits

    def step(chunk, carry):
        terms = []
        for lane in range(UNROLL):
            entry = list_ref[which, chunk * UNROLL + lane]
            col = entry & ((1 << col_bits) - 1)
            row = lax.shift_right_logical(entry, col_bits) & ((1 << row_bits) - 1)
            slot = lax.shift_right_logical(entry, col_bits + row_bits)
            term = lax.dot_general(
                field_ref[col], values_ref[slot], NT, preferred_element_type=jnp.float32)
            terms.append((row, term))
        for row, term in terms:
            total[row] += term
        return carry

    lax.fori_loop(0, lax.div(total_ref[which] + UNROLL - 1, UNROLL), step, 0)


def join(pieces, field):
    each = pieces[0].shape[0]
    for index, piece in enumerate(pieces):
        field[pl.ds(index * each, each)] = piece[...]


def first_kernel(steps, parts, chips, bits, position_ref, list_ref, total_ref, values_ref, *refs):
    lists = parts * CORES
    piece_refs, refs = refs[:parts], refs[parts:]
    out_refs, refs = refs[:steps], refs[steps:]
    in_refs, refs = refs[:steps], refs[steps:]
    sent_refs, totals, field = refs[:-lists - 1], refs[-lists - 1:-1], refs[-1]
    chip = lax.shift_right_logical(position_ref[0], 1)
    join(piece_refs, field)
    for index, total in enumerate(totals):
        part, half = divmod(index, CORES)
        rows = total.shape[0] - 1
        each = rows // chips
        if steps == 0:
            total[...] = jnp.zeros(total.shape, jnp.float32)
        elif half == 0:
            at = pl.ds(part * rows, rows)
            total[pl.ds(0, rows)] = -sum(out_ref[at].astype(jnp.float32) for out_ref in out_refs)
        else:
            for shift in range(chips):
                at = partner(chip, shift, chips) * each
                value = sum(in_ref[pl.ds(part * rows + at, each)].astype(jnp.float32) for in_ref in in_refs)
                if shift > 0:
                    for step in range(steps):
                        value -= sent_refs[(step * parts + part) * (chips - 1) + shift - 1][...].astype(jnp.float32)
                total[pl.ds(at, each)] = value
        add_products(index, bits, list_ref, total_ref, values_ref, field, total)


def stage_kernel(stage, bits, pieces, lists, list_ref, total_ref, values_ref, *refs):
    piece_refs, refs = refs[:pieces], refs[pieces:]
    totals, field = refs[-lists - 1:-1], refs[-1]
    join(piece_refs, field)
    for index, total in enumerate(totals):
        add_products(stage * lists + index, bits, list_ref, total_ref, values_ref, field, total)


def last_kernel(stage, half, bits, pieces, parts, list_ref, total_ref, values_ref, *refs):
    piece_refs, refs = refs[:pieces], refs[pieces + parts:]
    totals, outs, field = refs[:parts], refs[parts:-1], refs[-1]
    join(piece_refs, field)
    for part, total in enumerate(totals):
        add_products(
            (stage * parts + part) * CORES + half, bits, list_ref, total_ref, values_ref, field, total)
        for out_ref in outs:
            rows = total.shape[0] - 1
            out_ref[pl.ds(part * rows, rows)] = total[pl.ds(0, rows)].astype(out_ref.dtype)


def combine_kernel(part, chips, position_ref, own_ref, other_ref, keep_ref, *send_refs):
    chip = lax.shift_right_logical(position_ref[0], 1)
    each = keep_ref.shape[0]
    for shift in range(chips):
        at = partner(chip, shift, chips) * each
        value = own_ref[pl.ds(at, each)] + other_ref[pl.ds(part * chips * each + at, each)].astype(jnp.float32)
        if shift == 0:
            keep_ref[...] = value
        else:
            send_refs[shift - 1][...] = value.astype(jnp.bfloat16)


def per_device(block_values, block_rows, block_cols, block_counts, precond, right_side):
    owned, rhs, size = right_side.shape[1:]
    row_devices = lax.axis_size("row")
    groups = lax.axis_size("col")
    chips = row_devices // CORES
    group = owned * row_devices
    slots = block_values.shape[2]
    parts = 2 if owned % 2 == 0 else 1
    each = owned // parts
    part_rows = chips * each
    position = jnp.stack([lax.axis_index("row"), lax.axis_index("col")]).astype(jnp.int32)

    stages = gather_stages(groups, parts)
    final = len(stages) - 1
    lists_each = parts * CORES
    widest = max(len(stage) for stage in stages) * each
    row_bits, col_bits = bits = part_rows.bit_length(), (widest - 1).bit_length()
    assert (slots - 1).bit_length() + row_bits + col_bits <= 31
    table = np.zeros(parts * groups, np.int32)
    for index, stage in enumerate(stages):
        for place, (part, shift) in enumerate(stage):
            table[part * groups + shift] = (index << col_bits) + place * each

    part_type = jax.ShapeDtypeStruct((each, rhs, size), jnp.float32)
    rounded_type = jax.ShapeDtypeStruct((each, rhs, size), jnp.bfloat16)
    matrix_type = jax.ShapeDtypeStruct((owned, size, size), jnp.bfloat16)
    total_type = jax.ShapeDtypeStruct((part_rows + 1, rhs, size), jnp.float32)

    loads = next(count for count in (4, 2, 1) if owned % count == 0)
    high, low, *fields = pl.pallas_call(
        functools.partial(start_kernel, parts),
        out_shape=[matrix_type] * 2 + [part_type] * (2 * parts) + [rounded_type] * parts,
        in_specs=[in_hbm()] * 2,
        out_specs=[in_vmem()] * (2 + 3 * parts),
        scratch_shapes=[
            pltpu.VMEM((owned, size, size), jnp.float32),
            pltpu.VMEM((owned, rhs, size), jnp.float32),
            pltpu.SemaphoreType.DMA((loads + 1,)),
        ],
        compiler_params=params(),
        name="start",
    )(stay_in_hbm(precond[0]), stay_in_hbm(right_side[0]))
    sols, lefts, rounded = fields[:parts], fields[parts:2 * parts], fields[2 * parts:]

    *lists, values = pl.pallas_call(
        functools.partial(order_kernel, group, owned, groups, parts, bits),
        out_shape=[
            jax.ShapeDtypeStruct((len(stages) * lists_each, slots + UNROLL), jnp.int32),
            jax.ShapeDtypeStruct((len(stages) * lists_each,), jnp.int32),
            pltpu.VMEM(block_values.shape[2:], block_values.dtype),
        ],
        in_specs=[in_smem()] * 5 + [in_hbm()],
        out_specs=[in_smem()] * 2 + [in_vmem()],
        scratch_shapes=[pltpu.SemaphoreType.DMA],
        compiler_params=params(),
        name="order",
    )(table, position, block_counts, block_rows, block_cols, stay_in_hbm(block_values[0, 0]))

    def cost(share):
        return pl.CostEstimate(
            flops=int(slots * share) * 2 * rhs * size * size,
            bytes_accessed=int(slots * share) * 2 * size * size, transcendentals=0)

    def field_scratch(pieces):
        return pltpu.VMEM((len(pieces) * each, rhs, size), jnp.bfloat16)

    def product_first(pieces, outs, ins, sent):
        return pl.pallas_call(
            functools.partial(first_kernel, len(outs), parts, chips, bits),
            out_shape=[total_type] * lists_each,
            in_specs=[in_smem()] * 3 + [in_vmem()] * (1 + len(pieces) + len(outs) + len(ins) + len(sent)),
            out_specs=[in_vmem()] * lists_each,
            scratch_shapes=[field_scratch(pieces)],
            compiler_params=params(),
            cost_estimate=cost(len(pieces) / groups / parts),
            name="stage0",
        )(position, *lists, values, *pieces, *outs, *ins, *sent)

    def product_stage(stage, pieces, totals):
        inputs = 3 + len(pieces)
        return pl.pallas_call(
            functools.partial(stage_kernel, stage, bits, len(pieces), lists_each),
            out_shape=[total_type] * lists_each,
            in_specs=[in_smem()] * 2 + [in_vmem()] * (1 + len(pieces) + len(totals)),
            out_specs=[in_vmem()] * lists_each,
            scratch_shapes=[field_scratch(pieces)],
            input_output_aliases={inputs + index: index for index in range(len(totals))},
            compiler_params=params(),
            cost_estimate=cost(len(pieces) / groups / parts),
            name="stage%d" % stage,
        )(*lists, values, *pieces, *totals)

    def product_last(half, pieces, totals):
        send = [jax.ShapeDtypeStruct((parts * part_rows, rhs, size), jnp.bfloat16)] if half == 0 else []
        inputs = 3 + len(pieces)
        return pl.pallas_call(
            functools.partial(last_kernel, final, half, bits, len(pieces), parts),
            out_shape=[total_type] * parts + send,
            in_specs=[in_smem()] * 2 + [in_vmem()] * (1 + len(pieces) + parts),
            out_specs=[in_vmem()] * (parts + len(send)),
            scratch_shapes=[field_scratch(pieces)],
            input_output_aliases={inputs + part: part for part in range(parts)},
            compiler_params=params(),
            cost_estimate=cost(len(pieces) / groups / parts / CORES),
            name="last%d" % half,
        )(*lists, values, *pieces, *totals)

    swap = [(r, r ^ 1) for r in range(row_devices)]
    outs, ins, sent = [], [], []
    for step in range(ITERS):
        gathered = {}
        for part in range(parts):
            gathered[part, 0] = rounded[part]
            for _, shift in [entry for stage in stages[1:] for entry in stage if entry[0] == part]:
                ring = [(c, (c + shift) % groups) for c in range(groups)]
                gathered[part, shift] = lax.ppermute(rounded[part], "col", ring)
        totals = product_first([gathered[entry] for entry in stages[0]], outs, ins, sent)
        for stage in range(1, final):
            totals = product_stage(stage, [gathered[entry] for entry in stages[stage]], totals)
        tail = [gathered[entry] for entry in stages[final]]
        outgoing = product_last(0, tail, totals[0::CORES])[-1]
        incoming = lax.ppermute(outgoing, "row", swap)
        own = product_last(1, tail, totals[1::CORES])
        outs.append(outgoing)
        ins.append(incoming)
        received = []
        for part in range(parts):
            keep, *sends = pl.pallas_call(
                functools.partial(combine_kernel, part, chips),
                out_shape=[part_type] + [rounded_type] * (chips - 1),
                in_specs=[in_smem()] + [in_vmem()] * 2,
                out_specs=[in_vmem()] * chips,
                compiler_params=params(),
                name="combine%d" % part,
            )(position, own[part], incoming)
            sent += sends
            pieces = []
            for shift in reversed(range(1, chips)):
                pairs = [
                    (chip * CORES + core, partner(chip, shift, chips) * CORES + core)
                    for chip in range(chips) for core in range(CORES)
                ]
                pieces.append(lax.ppermute(sends[shift - 1], "row", pairs))
            received.append([keep] + pieces)
        results = []
        for part in range(parts):
            base, inputs = part * each, received[part]
            if step == ITERS - 1 and part == parts - 1:
                return pl.pallas_call(
                    functools.partial(finish_kernel, base, len(inputs) - 1, parts - 1),
                    out_shape=jax.ShapeDtypeStruct((owned, rhs, size), jnp.float32),
                    in_specs=[in_vmem()] * (4 + len(inputs) + parts - 1),
                    out_specs=in_hbm(),
                    scratch_shapes=[
                        pltpu.VMEM((each, rhs, size), jnp.float32),
                        pltpu.SemaphoreType.DMA((parts,)),
                    ],
                    compiler_params=params(),
                    name="finish",
                )(high, low, lefts[part], sols[part], *inputs, *[result[0] for result in results])[None]
            results.append(pl.pallas_call(
                functools.partial(apply_kernel, base, len(inputs) - 1),
                out_shape=[part_type, part_type, rounded_type],
                in_specs=[in_vmem()] * (4 + len(inputs)),
                out_specs=[in_vmem()] * 3,
                compiler_params=params(),
                name="apply%d" % part,
            )(high, low, lefts[part], sols[part], *inputs))
        sols, lefts, rounded = [list(column) for column in zip(*results)]


def solution(mesh):
    placed = (
        P("row", "col", None, None, None),
        P("row", "col", None),
        P("row", "col", None),
        P("row", "col"),
        P("col", "row", None, None),
        P("col", "row", None, None),
    )
    return jax.shard_map(
        per_device,
        mesh=mesh,
        in_specs=placed,
        out_specs=P("col", "row", None, None),
        check_vma=False,
    )
```

```python
import functools

import jax
import jax.numpy as jnp
from jax import lax
from jax.experimental import pallas as pl
from jax.experimental.pallas import tpu as pltpu
from jax.sharding import PartitionSpec as P

ITERS = 3
UNROLL = 16
LANES = 4
DEPTH = 6
CORES = 2
VMEM_LIMIT = 24 * 1024 * 1024

NT = (((1,), (1,)), ((), ()))


def in_vmem():
    return pl.BlockSpec(memory_space=pltpu.VMEM)


def in_hbm():
    return pl.BlockSpec(memory_space=pltpu.HBM)


def in_smem():
    return pl.BlockSpec(memory_space=pltpu.SMEM)


def stay_in_hbm(array):
    return pltpu.with_memory_space_constraint(array, pltpu.HBM)


def params():
    return pltpu.CompilerParams(vmem_limit_bytes=VMEM_LIMIT)


def split(value):
    high = value.astype(jnp.bfloat16)
    low = (value - high.astype(jnp.float32)).astype(jnp.bfloat16)
    return high, low


def times_block(field, high, low):
    field_high, field_low = split(field)
    rhs = field.shape[0]
    both = jnp.concatenate([field_high, field_low], axis=0)
    first = lax.dot_general(both, high, NT, preferred_element_type=jnp.float32)
    second = lax.dot_general(field_high, low, NT, preferred_element_type=jnp.float32)
    return first[:rhs] + (first[rhs:] + second)


def partner(chip, shift, chips):
    if chips & (chips - 1) == 0:
        return chip ^ shift
    return (chip + shift) % chips


def halves(value, size):
    if size & (size - 1) == 0:
        return lax.shift_right_logical(value, size.bit_length() - 1), value & (size - 1)
    return lax.div(value, size), lax.rem(value, size)


def relative(mine, source, groups):
    if groups % 2:
        away = mine - source
        return jnp.where(away < 0, away + groups, away)
    other = (mine ^ source) & 1
    away = (mine ^ other) - source
    away = jnp.where(away < 0, away + groups, away)
    return other * (groups // 2) + lax.shift_right_logical(away, 1)


def gather_stages(groups):
    if groups % 2:
        return [[0], list(range(1, groups))]
    pairs = groups // 2
    stages = [[0], [pairs], list(range(1, pairs)), list(range(pairs + 1, groups))]
    return [stage for stage in stages if stage]


def gather(rounded, groups):
    def ring(step):
        return [(c, (c + step) % groups) for c in range(groups)]

    if groups % 2:
        return [rounded] + [lax.ppermute(rounded, "col", ring(step)) for step in range(1, groups)]
    far = [lax.ppermute(rounded, "col", ring(2 * step)) for step in range(1, groups // 2)]
    return [rounded] + far + [lax.ppermute(rounded, "col", neighbours(groups))]


def neighbours(count):
    return [(index, index ^ 1) for index in range(count)]


def hold_kernel(piece_ref, token_ref, out_ref):
    pass


def start_kernel(precond_hbm, rhs_hbm, high_ref, low_ref, sol_ref, left_ref, rounded_ref, precond_ref, sems):
    owned = left_ref.shape[0]
    parts = sems.shape[0] - 1
    each = owned // parts
    loads = [pltpu.make_async_copy(rhs_hbm, left_ref, sems.at[parts])]
    for part in range(parts):
        at = pl.ds(part * each, each)
        loads.append(pltpu.make_async_copy(precond_hbm.at[at], precond_ref.at[at], sems.at[part]))
    for load in loads:
        load.start()
    loads[0].wait()
    for part in range(parts):
        loads[1 + part].wait()
        for p in range(part * each, (part + 1) * each):
            high, low = split(precond_ref[p])
            high_ref[p] = high
            low_ref[p] = low
            value = times_block(left_ref[p], high, low)
            sol_ref[p] = value
            rounded_ref[p] = value.astype(jnp.bfloat16)


def apply_kernel(pieces, high_ref, low_ref, left_ref, sol_ref, base_ref, *refs):
    piece_refs, (new_ref, new_left_ref, rounded_ref) = refs[:pieces], refs[pieces:]
    for p in range(sol_ref.shape[0]):
        received = sum(piece_ref[p].astype(jnp.float32) for piece_ref in piece_refs)
        value = sol_ref[p] + times_block(base_ref[p] - received, high_ref[p], low_ref[p])
        new_ref[p] = value
        new_left_ref[p] = left_ref[p] - received
        rounded_ref[p] = value.astype(jnp.bfloat16)


def finish_kernel(pieces, high_ref, low_ref, sol_ref, base_ref, *refs):
    piece_refs, (out_hbm, value_ref, sems) = refs[:pieces], refs[pieces:]
    owned = sol_ref.shape[0]
    parts = sems.shape[0]
    each = owned // parts
    stores = []
    for part in range(parts):
        for p in range(part * each, (part + 1) * each):
            received = sum(piece_ref[p].astype(jnp.float32) for piece_ref in piece_refs)
            value_ref[p] = sol_ref[p] + times_block(base_ref[p] - received, high_ref[p], low_ref[p])
        at = pl.ds(part * each, each)
        stores.append(pltpu.make_async_copy(value_ref.at[at], out_hbm.at[at], sems.at[part]))
        stores[-1].start()
    for store in stores:
        store.wait()


def order_kernel(group, owned, groups, stages, bits, position_ref, count_ref, rows_hbm, cols_hbm, values_hbm,
                 list_out, total_out, values_out, rows_ref, cols_ref, table_ref, total_ref, sems):
    loads = [
        pltpu.make_async_copy(rows_hbm, rows_ref, sems.at[0]),
        pltpu.make_async_copy(cols_hbm, cols_ref, sems.at[1]),
        pltpu.make_async_copy(values_hbm, values_out, sems.at[2]),
    ]
    for load in loads:
        load.start()
    core = position_ref[0] & (CORES - 1)
    mine = position_ref[1]
    used = count_ref[0, 0]
    row_bits, col_bits = bits
    lists = len(stages) * CORES
    trash = (group // CORES) << col_bits
    for index, stage in enumerate(stages):
        for place, piece in enumerate(stage):
            table_ref[piece] = ((index * CORES) << col_bits) + place * owned
    for index in range(lists + 1):
        total_ref[index] = 0
    loads[0].wait()
    loads[1].wait()

    def place(chunk, carry):
        entries = []
        for lane in range(LANES):
            slot = chunk * LANES + lane
            owner, row_inner = halves(halves(rows_ref[0, 0, slot], group)[1], owned)
            source, rest = halves(cols_ref[0, 0, slot], group)
            half = 1 - ((owner & (CORES - 1)) ^ core)
            first, base = halves(table_ref[relative(mine, source, groups)], 1 << col_bits)
            which = jnp.where(slot < used, first + half, lists)
            row = lax.shift_right_logical(owner, 1) * owned + row_inner
            col = base + halves(rest, owned)[1]
            entries.append((which, (((slot << row_bits) | row) << col_bits) | col))
        for which, entry in entries:
            at = total_ref[which]
            list_out[which, at] = entry
            total_ref[which] = at + 1
        return carry

    lax.fori_loop(0, lax.div(used + LANES - 1, LANES), place, 0)
    for index in range(lists):
        total_out[index] = total_ref[index]

    def close(index, carry):
        for extra in range(UNROLL):
            list_out[index, total_ref[index] + extra] = trash
        return carry

    lax.fori_loop(0, lists, close, 0)
    loads[2].wait()


def add_products(which, bits, list_ref, total_ref, values_ref, field_ref, total):
    row_bits, col_bits = bits

    def step(chunk, carry):
        terms = []

        def store(row, term):
            total[row] += term

        for lane in range(UNROLL):
            entry = list_ref[which, chunk * UNROLL + lane]
            col = entry & ((1 << col_bits) - 1)
            row = lax.shift_right_logical(entry, col_bits) & ((1 << row_bits) - 1)
            slot = lax.shift_right_logical(entry, col_bits + row_bits)
            term = lax.dot_general(
                field_ref[col], values_ref[slot], NT, preferred_element_type=jnp.float32)
            terms.append((row, term))
            if len(terms) > DEPTH:
                store(*terms.pop(0))
        for row, term in terms:
            store(row, term)
        return carry

    lax.fori_loop(0, lax.div(total_ref[which] + UNROLL - 1, UNROLL), step, 0)


def join(pieces, field):
    each = pieces[0].shape[0]
    for index, piece in enumerate(pieces):
        field[pl.ds(index * each, each)] = piece[...]


def first_kernel(steps, chips, bits, position_ref, list_ref, total_ref, values_ref, field_ref, *refs):
    out_refs, refs = refs[:steps], refs[steps:]
    in_refs, refs = refs[:steps], refs[steps:]
    sent_refs, totals, token_ref = refs[:-CORES - 1], refs[-CORES - 1:-1], refs[-1]
    token_ref[...] = jnp.zeros_like(token_ref)
    chip = lax.shift_right_logical(position_ref[0], 1)
    for half, total in enumerate(totals):
        rows = total.shape[0] - 1
        owned = rows // chips
        if steps == 0:
            total[...] = jnp.zeros(total.shape, jnp.float32)
        elif half == 0:
            total[pl.ds(0, rows)] = -sum(out_ref[...].astype(jnp.float32) for out_ref in out_refs)
        else:
            for shift in range(chips):
                at = pl.ds(partner(chip, shift, chips) * owned, owned)
                value = sum(in_ref[at].astype(jnp.float32) for in_ref in in_refs)
                if shift > 0:
                    for step in range(steps):
                        value -= sent_refs[step * (chips - 1) + shift - 1][...].astype(jnp.float32)
                total[at] = value
        add_products(half, bits, list_ref, total_ref, values_ref, field_ref, total)


def stage_kernel(stage, bits, pieces, list_ref, total_ref, values_ref, *refs):
    piece_refs, refs = refs[:pieces], refs[pieces + CORES:]
    totals, field = refs[:CORES], refs[-1]
    join(piece_refs, field)
    for half, total in enumerate(totals):
        add_products(stage * CORES + half, bits, list_ref, total_ref, values_ref, field, total)


def last_kernel(stage, half, bits, pieces, list_ref, total_ref, values_ref, *refs):
    piece_refs, refs = refs[:pieces], refs[pieces + 1:]
    total, outs, field = refs[0], refs[1:-1], refs[-1]
    join(piece_refs, field)
    add_products(stage * CORES + half, bits, list_ref, total_ref, values_ref, field, total)
    for out_ref in outs:
        out_ref[...] = total[pl.ds(0, out_ref.shape[0])].astype(out_ref.dtype)


def chip_rows(shift, chips, position_ref, own_ref, other_ref, owned):
    chip = lax.shift_right_logical(position_ref[0], 1)
    at = pl.ds(partner(chip, shift, chips) * owned, owned)
    return own_ref[at] + other_ref[at].astype(jnp.float32)


def combine_kernel(shift, chips, position_ref, own_ref, other_ref, send_ref):
    send_ref[...] = chip_rows(
        shift, chips, position_ref, own_ref, other_ref, send_ref.shape[0]).astype(send_ref.dtype)


def keep_kernel(chips, position_ref, own_ref, other_ref, left_ref, sol_ref, base_ref):
    keep = chip_rows(0, chips, position_ref, own_ref, other_ref, base_ref.shape[0])
    base_ref[...] = left_ref[...] - sol_ref[...] - keep


def per_device(block_values, block_rows, block_cols, block_counts, precond, right_side):
    owned, rhs, size = right_side.shape[1:]
    row_devices = lax.axis_size("row")
    groups = lax.axis_size("col")
    chips = row_devices // CORES
    group = owned * row_devices
    half_rows = chips * owned
    slots = block_values.shape[2]
    position = jnp.stack([lax.axis_index("row"), lax.axis_index("col")]).astype(jnp.int32)

    stages = gather_stages(groups)
    final = len(stages) - 1
    lists_total = len(stages) * CORES
    widest = max(len(stage) for stage in stages) * owned
    row_bits, col_bits = bits = half_rows.bit_length(), (widest - 1).bit_length()
    assert (slots - 1).bit_length() + row_bits + col_bits <= 31
    assert slots % LANES == 0

    field_type = jax.ShapeDtypeStruct((owned, rhs, size), jnp.float32)
    rounded_type = jax.ShapeDtypeStruct((owned, rhs, size), jnp.bfloat16)
    matrix_type = jax.ShapeDtypeStruct((owned, size, size), jnp.bfloat16)
    total_type = jax.ShapeDtypeStruct((half_rows + 1, rhs, size), jnp.float32)
    index_type = pltpu.SMEM(block_rows.shape, jnp.int32)
    token_type = jax.ShapeDtypeStruct((8, 128), jnp.float32)
    parts = next(count for count in (4, 2, 1) if owned % count == 0)

    high, low, sol, left, rounded = pl.pallas_call(
        start_kernel,
        out_shape=[matrix_type] * 2 + [field_type] * 2 + [rounded_type],
        in_specs=[in_hbm()] * 2,
        out_specs=[in_vmem()] * 5,
        scratch_shapes=[
            pltpu.VMEM((owned, size, size), jnp.float32),
            pltpu.SemaphoreType.DMA((parts + 1,)),
        ],
        compiler_params=params(),
        name="start",
    )(stay_in_hbm(precond[0]), stay_in_hbm(right_side[0]))

    *lists, values = pl.pallas_call(
        functools.partial(order_kernel, group, owned, groups, stages, bits),
        out_shape=[
            jax.ShapeDtypeStruct((lists_total + 1, slots + UNROLL), jnp.int32),
            jax.ShapeDtypeStruct((lists_total,), jnp.int32),
            pltpu.VMEM(block_values.shape[2:], block_values.dtype),
        ],
        in_specs=[in_smem()] * 2 + [in_hbm()] * 3,
        out_specs=[in_smem()] * 2 + [in_vmem()],
        scratch_shapes=[
            index_type, index_type,
            pltpu.SMEM((groups,), jnp.int32), pltpu.SMEM((lists_total + 1,), jnp.int32),
            pltpu.SemaphoreType.DMA((3,)),
        ],
        compiler_params=params(),
        name="order",
    )(position, block_counts, *[stay_in_hbm(array) for array in (block_rows, block_cols, block_values[0, 0])])

    def cost(share):
        return pl.CostEstimate(
            flops=int(slots * share) * 2 * rhs * size * size,
            bytes_accessed=int(slots * share) * 2 * size * size, transcendentals=0)

    def field_scratch(pieces):
        return pltpu.VMEM((len(pieces) * owned, rhs, size), jnp.bfloat16)

    def product_first(field, outs, ins, sent):
        return pl.pallas_call(
            functools.partial(first_kernel, len(outs), chips, bits),
            out_shape=[total_type] * CORES + [token_type],
            in_specs=[in_smem()] * 3 + [in_vmem()] * (2 + len(outs) + len(ins) + len(sent)),
            out_specs=[in_vmem()] * (CORES + 1),
            compiler_params=params(),
            cost_estimate=cost(1 / groups),
            name="stage0",
        )(position, *lists, values, field, *outs, *ins, *sent)

    def product_stage(stage, pieces, totals):
        inputs = 3 + len(pieces)
        return pl.pallas_call(
            functools.partial(stage_kernel, stage, bits, len(pieces)),
            out_shape=[total_type] * CORES,
            in_specs=[in_smem()] * 2 + [in_vmem()] * (1 + len(pieces) + CORES),
            out_specs=[in_vmem()] * CORES,
            scratch_shapes=[field_scratch(pieces)],
            input_output_aliases={inputs + half: half for half in range(CORES)},
            compiler_params=params(),
            cost_estimate=cost(len(pieces) / groups),
            name="stage%d" % stage,
        )(*lists, values, *pieces, *totals)

    def product_last(half, pieces, total):
        send = [jax.ShapeDtypeStruct((half_rows, rhs, size), jnp.bfloat16)] if half == 0 else []
        return pl.pallas_call(
            functools.partial(last_kernel, final, half, bits, len(pieces)),
            out_shape=[total_type] + send,
            in_specs=[in_smem()] * 2 + [in_vmem()] * (2 + len(pieces)),
            out_specs=[in_vmem()] * (1 + len(send)),
            scratch_shapes=[field_scratch(pieces)],
            input_output_aliases={3 + len(pieces): 0},
            compiler_params=params(),
            cost_estimate=cost(len(pieces) / groups / CORES),
            name="last%d" % half,
        )(*lists, values, *pieces, total)[-1]

    def hold(piece, token):
        return pl.pallas_call(
            hold_kernel,
            out_shape=rounded_type,
            in_specs=[in_vmem()] * 2,
            out_specs=in_vmem(),
            input_output_aliases={0: 0},
            compiler_params=params(),
            name="hold",
        )(piece, token)

    outs, ins, sent = [], [], []
    for step in range(ITERS):
        fields = gather(rounded, groups)
        *totals, token = product_first(rounded, outs, ins, sent)
        if groups % 2 == 0:
            for index in range(1, groups // 2):
                fields[index] = hold(fields[index], token)
                fields.append(lax.ppermute(fields[index], "col", neighbours(groups)))
        for stage in range(1, final):
            totals = product_stage(stage, [fields[piece] for piece in stages[stage]], totals)
        tail = [fields[piece] for piece in stages[final]]
        outgoing = product_last(0, tail, totals[0])
        incoming = lax.ppermute(outgoing, "row", neighbours(row_devices))
        own = product_last(1, tail, totals[1])
        outs.append(outgoing)
        ins.append(incoming)
        sends = {}
        pieces = []
        for shift in range(1, chips):
            pairs = [
                (chip * CORES + core, partner(chip, shift, chips) * CORES + core)
                for chip in range(chips) for core in range(CORES)
            ]
            sends[shift] = pl.pallas_call(
                functools.partial(combine_kernel, shift, chips),
                out_shape=rounded_type,
                in_specs=[in_smem()] + [in_vmem()] * 2,
                out_specs=in_vmem(),
                compiler_params=params(),
                name="combine%d" % shift,
            )(position, own, incoming)
            pieces.append(lax.ppermute(sends[shift], "row", pairs))
        sent += [sends[shift] for shift in range(1, chips)]
        base = pl.pallas_call(
            functools.partial(keep_kernel, chips),
            out_shape=field_type,
            in_specs=[in_smem()] + [in_vmem()] * 4,
            out_specs=in_vmem(),
            compiler_params=params(),
            name="keep",
        )(position, own, incoming, left, sol)
        if step < ITERS - 1:
            sol, left, rounded = pl.pallas_call(
                functools.partial(apply_kernel, len(pieces)),
                out_shape=[field_type, field_type, rounded_type],
                in_specs=[in_vmem()] * (5 + len(pieces)),
                out_specs=[in_vmem()] * 3,
                compiler_params=params(),
                name="apply",
            )(high, low, left, sol, base, *pieces)
    return pl.pallas_call(
        functools.partial(finish_kernel, len(pieces)),
        out_shape=field_type,
        in_specs=[in_vmem()] * (4 + len(pieces)),
        out_specs=in_hbm(),
        scratch_shapes=[
            pltpu.VMEM((owned, rhs, size), jnp.float32),
            pltpu.SemaphoreType.DMA((2 if owned % 2 == 0 else 1,)),
        ],
        compiler_params=params(),
        name="finish",
    )(high, low, sol, base, *pieces)[None]


def solution(mesh):
    placed = (
        P("row", "col", None, None, None),
        P("row", "col", None),
        P("row", "col", None),
        P("row", "col"),
        P("col", "row", None, None),
        P("col", "row", None, None),
    )
    return jax.shard_map(
        per_device,
        mesh=mesh,
        in_specs=placed,
        out_specs=P("col", "row", None, None),
        check_vma=False,
    )
```

```python
import functools

import jax
import jax.numpy as jnp
from jax import lax
from jax.experimental import pallas as pl
from jax.experimental.pallas import tpu as pltpu
from jax.sharding import PartitionSpec as P

ITERS = 3
UNROLL = 16
LANES = 4
DEPTH = 6
CORES = 2
VMEM_LIMIT = 24 * 1024 * 1024

NT = (((1,), (1,)), ((), ()))


def in_vmem():
    return pl.BlockSpec(memory_space=pltpu.VMEM)


def in_hbm():
    return pl.BlockSpec(memory_space=pltpu.HBM)


def in_smem():
    return pl.BlockSpec(memory_space=pltpu.SMEM)


def stay_in_hbm(array):
    return pltpu.with_memory_space_constraint(array, pltpu.HBM)


def params():
    return pltpu.CompilerParams(vmem_limit_bytes=VMEM_LIMIT)


def split(value):
    high = value.astype(jnp.bfloat16)
    low = (value - high.astype(jnp.float32)).astype(jnp.bfloat16)
    return high, low


def times_block(field, high, low):
    field_high, field_low = split(field)
    rhs = field.shape[0]
    both = jnp.concatenate([field_high, field_low], axis=0)
    first = lax.dot_general(both, high, NT, preferred_element_type=jnp.float32)
    second = lax.dot_general(field_high, low, NT, preferred_element_type=jnp.float32)
    return first[:rhs] + (first[rhs:] + second)


def partner(chip, shift, chips):
    if chips & (chips - 1) == 0:
        return chip ^ shift
    return (chip + shift) % chips


def halves(value, size):
    if size & (size - 1) == 0:
        return lax.shift_right_logical(value, size.bit_length() - 1), value & (size - 1)
    return lax.div(value, size), lax.rem(value, size)


def relative(mine, source, groups):
    if groups % 2:
        away = mine - source
        return jnp.where(away < 0, away + groups, away)
    other = (mine ^ source) & 1
    away = (mine ^ other) - source
    away = jnp.where(away < 0, away + groups, away)
    return other * (groups // 2) + lax.shift_right_logical(away, 1)


def gather_stages(groups):
    if groups % 2:
        return [[0], list(range(1, groups))]
    pairs = groups // 2
    stages = [[0], [pairs], list(range(1, pairs)), list(range(pairs + 1, groups))]
    return [stage for stage in stages if stage]


def gather(rounded, groups):
    def ring(step):
        return [(c, (c + step) % groups) for c in range(groups)]

    if groups % 2:
        return [rounded] + [lax.ppermute(rounded, "col", ring(step)) for step in range(1, groups)]
    far = [lax.ppermute(rounded, "col", ring(2 * step)) for step in range(1, groups // 2)]
    return [rounded] + far + [lax.ppermute(rounded, "col", neighbours(groups))]


def neighbours(count):
    return [(index, index ^ 1) for index in range(count)]


def hold_kernel(piece_ref, token_ref, out_ref):
    pass


def start_kernel(precond_hbm, rhs_hbm, high_ref, low_ref, sol_ref, left_ref, rounded_ref, precond_ref, sems):
    owned = left_ref.shape[0]
    parts = sems.shape[0] - 1
    each = owned // parts
    loads = [pltpu.make_async_copy(rhs_hbm, left_ref, sems.at[parts])]
    for part in range(parts):
        at = pl.ds(part * each, each)
        loads.append(pltpu.make_async_copy(precond_hbm.at[at], precond_ref.at[at], sems.at[part]))
    for load in loads:
        load.start()
    loads[0].wait()
    for part in range(parts):
        loads[1 + part].wait()
        for p in range(part * each, (part + 1) * each):
            high, low = split(precond_ref[p])
            high_ref[p] = high
            low_ref[p] = low
            value = times_block(left_ref[p], high, low)
            sol_ref[p] = value
            rounded_ref[p] = value.astype(jnp.bfloat16)


def apply_kernel(pieces, high_ref, low_ref, left_ref, sol_ref, base_ref, *refs):
    piece_refs, (new_ref, new_left_ref, rounded_ref) = refs[:pieces], refs[pieces:]
    for p in range(sol_ref.shape[0]):
        received = sum(piece_ref[p].astype(jnp.float32) for piece_ref in piece_refs)
        value = sol_ref[p] + times_block(base_ref[p] - received, high_ref[p], low_ref[p])
        new_ref[p] = value
        new_left_ref[p] = left_ref[p] - received
        rounded_ref[p] = value.astype(jnp.bfloat16)


def finish_kernel(pieces, high_ref, low_ref, sol_ref, base_ref, *refs):
    piece_refs, (out_hbm, value_ref, sems) = refs[:pieces], refs[pieces:]
    owned = sol_ref.shape[0]
    parts = sems.shape[0]
    each = owned // parts
    stores = []
    for part in range(parts):
        for p in range(part * each, (part + 1) * each):
            received = sum(piece_ref[p].astype(jnp.float32) for piece_ref in piece_refs)
            value_ref[p] = sol_ref[p] + times_block(base_ref[p] - received, high_ref[p], low_ref[p])
        at = pl.ds(part * each, each)
        stores.append(pltpu.make_async_copy(value_ref.at[at], out_hbm.at[at], sems.at[part]))
        stores[-1].start()
    for store in stores:
        store.wait()


def order_kernel(group, owned, groups, stages, bits, count_ref, rows_hbm, cols_hbm, values_hbm,
                 list_out, total_out, values_out, rows_ref, cols_ref, table_ref, total_ref, sems):
    loads = [
        pltpu.make_async_copy(rows_hbm, rows_ref, sems.at[0]),
        pltpu.make_async_copy(cols_hbm, cols_ref, sems.at[1]),
        pltpu.make_async_copy(values_hbm, values_out, sems.at[2]),
    ]
    for load in loads:
        load.start()
    core = lax.axis_index("row") & (CORES - 1)
    mine = lax.axis_index("col")
    row_bits, col_bits = bits
    lists = len(stages) * CORES
    trash = (group // CORES) << col_bits
    for index, stage in enumerate(stages):
        for place, piece in enumerate(stage):
            table_ref[piece] = ((index * CORES) << col_bits) + place * owned
    for index in range(lists + 1):
        total_ref[index] = 0
    for load in loads[:2]:
        load.wait()
    used = count_ref[0, 0]

    def place(chunk, carry):
        entries = []
        for lane in range(LANES):
            slot = chunk * LANES + lane
            owner, row_inner = halves(halves(rows_ref[0, 0, slot], group)[1], owned)
            source, rest = halves(cols_ref[0, 0, slot], group)
            half = 1 - ((owner & (CORES - 1)) ^ core)
            first, base = halves(table_ref[relative(mine, source, groups)], 1 << col_bits)
            which = jnp.where(slot < used, first + half, lists)
            row = lax.shift_right_logical(owner, 1) * owned + row_inner
            col = base + halves(rest, owned)[1]
            entries.append((which, (((slot << row_bits) | row) << col_bits) | col))
        for which, entry in entries:
            at = total_ref[which]
            list_out[which, at] = entry
            total_ref[which] = at + 1
        return carry

    lax.fori_loop(0, lax.div(used + LANES - 1, LANES), place, 0)
    for index in range(lists):
        total_out[index] = total_ref[index]

    def close(index, carry):
        for extra in range(UNROLL):
            list_out[index, total_ref[index] + extra] = trash
        return carry

    lax.fori_loop(0, lists, close, 0)
    loads[2].wait()


def add_products(which, bits, list_ref, total_ref, values_ref, field_ref, total):
    row_bits, col_bits = bits

    def step(chunk, carry):
        terms = []

        def store(row, term):
            total[row] += term

        for lane in range(UNROLL):
            entry = list_ref[which, chunk * UNROLL + lane]
            col = entry & ((1 << col_bits) - 1)
            row = lax.shift_right_logical(entry, col_bits) & ((1 << row_bits) - 1)
            slot = lax.shift_right_logical(entry, col_bits + row_bits)
            term = lax.dot_general(
                field_ref[col], values_ref[slot], NT, preferred_element_type=jnp.float32)
            terms.append((row, term))
            if len(terms) > DEPTH:
                store(*terms.pop(0))
        for row, term in terms:
            store(row, term)
        return carry

    lax.fori_loop(0, lax.div(total_ref[which] + UNROLL - 1, UNROLL), step, 0)


def join(pieces, field):
    if len(pieces) == 1:
        return pieces[0]
    each = pieces[0].shape[0]
    for index, piece in enumerate(pieces):
        field[pl.ds(index * each, each)] = piece[...]
    return field


def first_kernel(steps, chips, bits, list_ref, total_ref, values_ref, field_ref, *refs):
    out_refs, refs = refs[:steps], refs[steps:]
    in_refs, refs = refs[:steps], refs[steps:]
    sent_refs, totals, token_ref = refs[:-CORES - 1], refs[-CORES - 1:-1], refs[-1]
    token_ref[...] = jnp.zeros_like(token_ref)
    chip = lax.axis_index("row") // CORES
    for half, total in enumerate(totals):
        rows = total.shape[0] - 1
        owned = rows // chips
        if steps == 0:
            total[...] = jnp.zeros(total.shape, jnp.float32)
        elif half == 0:
            total[pl.ds(0, rows)] = -sum(out_ref[...].astype(jnp.float32) for out_ref in out_refs)
        else:
            for shift in range(chips):
                at = pl.ds(partner(chip, shift, chips) * owned, owned)
                value = sum(in_ref[at].astype(jnp.float32) for in_ref in in_refs)
                if shift > 0:
                    for step in range(steps):
                        value -= sent_refs[step * (chips - 1) + shift - 1][...].astype(jnp.float32)
                total[at] = value
        add_products(half, bits, list_ref, total_ref, values_ref, field_ref, total)


def stage_kernel(stage, bits, pieces, list_ref, total_ref, values_ref, *refs):
    piece_refs, refs = refs[:pieces], refs[pieces + CORES:]
    totals, field = refs[:CORES], refs[-1]
    field_ref = join(piece_refs, field)
    for half, total in enumerate(totals):
        add_products(stage * CORES + half, bits, list_ref, total_ref, values_ref, field_ref, total)


def last_kernel(stage, half, bits, pieces, list_ref, total_ref, values_ref, *refs):
    piece_refs, refs = refs[:pieces], refs[pieces + 1:]
    total, outs, field = refs[0], refs[1:-1], refs[-1]
    field_ref = join(piece_refs, field)
    add_products(stage * CORES + half, bits, list_ref, total_ref, values_ref, field_ref, total)
    for out_ref in outs:
        out_ref[...] = total[pl.ds(0, out_ref.shape[0])].astype(out_ref.dtype)


def chip_rows(shift, chips, own_ref, other_ref, owned):
    chip = lax.axis_index("row") // CORES
    at = pl.ds(partner(chip, shift, chips) * owned, owned)
    return own_ref[at] + other_ref[at].astype(jnp.float32)


def combine_kernel(shift, chips, own_ref, other_ref, send_ref):
    send_ref[...] = chip_rows(
        shift, chips, own_ref, other_ref, send_ref.shape[0]).astype(send_ref.dtype)


def keep_kernel(chips, own_ref, other_ref, left_ref, sol_ref, base_ref):
    keep = chip_rows(0, chips, own_ref, other_ref, base_ref.shape[0])
    base_ref[...] = left_ref[...] - sol_ref[...] - keep


def per_device(block_values, block_rows, block_cols, block_counts, precond, right_side):
    owned, rhs, size = right_side.shape[1:]
    row_devices = lax.axis_size("row")
    groups = lax.axis_size("col")
    chips = row_devices // CORES
    group = owned * row_devices
    half_rows = chips * owned
    slots = block_values.shape[2]

    stages = gather_stages(groups)
    final = len(stages) - 1
    lists_total = len(stages) * CORES
    widest = max(len(stage) for stage in stages) * owned
    row_bits, col_bits = bits = half_rows.bit_length(), (widest - 1).bit_length()
    assert (slots - 1).bit_length() + row_bits + col_bits <= 31
    assert slots % LANES == 0

    field_type = jax.ShapeDtypeStruct((owned, rhs, size), jnp.float32)
    rounded_type = jax.ShapeDtypeStruct((owned, rhs, size), jnp.bfloat16)
    matrix_type = jax.ShapeDtypeStruct((owned, size, size), jnp.bfloat16)
    total_type = jax.ShapeDtypeStruct((half_rows + 1, rhs, size), jnp.float32)
    index_type = pltpu.SMEM(block_rows.shape, jnp.int32)
    token_type = jax.ShapeDtypeStruct((8, 128), jnp.float32)
    parts = next(count for count in (4, 2, 1) if owned % count == 0)

    high, low, sol, left, rounded = pl.pallas_call(
        start_kernel,
        out_shape=[matrix_type] * 2 + [field_type] * 2 + [rounded_type],
        in_specs=[in_hbm()] * 2,
        out_specs=[in_vmem()] * 5,
        scratch_shapes=[
            pltpu.VMEM((owned, size, size), jnp.float32),
            pltpu.SemaphoreType.DMA((parts + 1,)),
        ],
        compiler_params=params(),
        name="start",
    )(stay_in_hbm(precond[0]), stay_in_hbm(right_side[0]))

    *lists, values = pl.pallas_call(
        functools.partial(order_kernel, group, owned, groups, stages, bits),
        out_shape=[
            pltpu.SMEM((lists_total + 1, slots + UNROLL), jnp.int32),
            pltpu.SMEM((lists_total,), jnp.int32),
            pltpu.VMEM(block_values.shape[2:], block_values.dtype),
        ],
        in_specs=[in_smem()] + [in_hbm()] * 3,
        out_specs=[in_smem()] * 2 + [in_vmem()],
        scratch_shapes=[
            index_type, index_type,
            pltpu.SMEM((groups,), jnp.int32), pltpu.SMEM((lists_total + 1,), jnp.int32),
            pltpu.SemaphoreType.DMA((3,)),
        ],
        compiler_params=params(),
        name="order",
    )(block_counts, *[stay_in_hbm(array) for array in (block_rows, block_cols, block_values[0, 0])])

    def cost(share):
        return pl.CostEstimate(
            flops=int(slots * share) * 2 * rhs * size * size,
            bytes_accessed=int(slots * share) * 2 * size * size, transcendentals=0)

    def field_scratch(pieces):
        return pltpu.VMEM((len(pieces) * owned, rhs, size), jnp.bfloat16)

    def product_first(field, outs, ins, sent):
        return pl.pallas_call(
            functools.partial(first_kernel, len(outs), chips, bits),
            out_shape=[total_type] * CORES + [token_type],
            in_specs=[in_smem()] * 2 + [in_vmem()] * (2 + len(outs) + len(ins) + len(sent)),
            out_specs=[in_vmem()] * (CORES + 1),
            compiler_params=params(),
            cost_estimate=cost(1 / groups),
            name="stage0",
        )(*lists, values, field, *outs, *ins, *sent)

    def product_stage(stage, pieces, totals):
        inputs = 3 + len(pieces)
        return pl.pallas_call(
            functools.partial(stage_kernel, stage, bits, len(pieces)),
            out_shape=[total_type] * CORES,
            in_specs=[in_smem()] * 2 + [in_vmem()] * (1 + len(pieces) + CORES),
            out_specs=[in_vmem()] * CORES,
            scratch_shapes=[field_scratch(pieces)],
            input_output_aliases={inputs + half: half for half in range(CORES)},
            compiler_params=params(),
            cost_estimate=cost(len(pieces) / groups),
            name="stage%d" % stage,
        )(*lists, values, *pieces, *totals)

    def product_last(half, pieces, total):
        send = [jax.ShapeDtypeStruct((half_rows, rhs, size), jnp.bfloat16)] if half == 0 else []
        return pl.pallas_call(
            functools.partial(last_kernel, final, half, bits, len(pieces)),
            out_shape=[total_type] + send,
            in_specs=[in_smem()] * 2 + [in_vmem()] * (2 + len(pieces)),
            out_specs=[in_vmem()] * (1 + len(send)),
            scratch_shapes=[field_scratch(pieces)],
            input_output_aliases={3 + len(pieces): 0},
            compiler_params=params(),
            cost_estimate=cost(len(pieces) / groups / CORES),
            name="last%d" % half,
        )(*lists, values, *pieces, total)[-1]

    def hold(piece, token):
        return pl.pallas_call(
            hold_kernel,
            out_shape=rounded_type,
            in_specs=[in_vmem()] * 2,
            out_specs=in_vmem(),
            input_output_aliases={0: 0},
            compiler_params=params(),
            name="hold",
        )(piece, token)

    outs, ins, sent = [], [], []
    for step in range(ITERS):
        fields = gather(rounded, groups)
        *totals, token = product_first(rounded, outs, ins, sent)
        if groups % 2 == 0:
            for index in range(1, groups // 2):
                fields[index] = hold(fields[index], token)
                fields.append(lax.ppermute(fields[index], "col", neighbours(groups)))
        for stage in range(1, final):
            totals = product_stage(stage, [fields[piece] for piece in stages[stage]], totals)
        tail = [fields[piece] for piece in stages[final]]
        outgoing = product_last(0, tail, totals[0])
        incoming = lax.ppermute(outgoing, "row", neighbours(row_devices))
        own = product_last(1, tail, totals[1])
        outs.append(outgoing)
        ins.append(incoming)
        sends = {}
        pieces = []
        for shift in range(1, chips):
            pairs = [
                (chip * CORES + core, partner(chip, shift, chips) * CORES + core)
                for chip in range(chips) for core in range(CORES)
            ]
            sends[shift] = pl.pallas_call(
                functools.partial(combine_kernel, shift, chips),
                out_shape=rounded_type,
                in_specs=[in_vmem()] * 2,
                out_specs=in_vmem(),
                compiler_params=params(),
                name="combine%d" % shift,
            )(own, incoming)
            pieces.append(lax.ppermute(sends[shift], "row", pairs))
        sent += [sends[shift] for shift in range(1, chips)]
        base = pl.pallas_call(
            functools.partial(keep_kernel, chips),
            out_shape=field_type,
            in_specs=[in_vmem()] * 4,
            out_specs=in_vmem(),
            compiler_params=params(),
            name="keep",
        )(own, incoming, left, sol)
        if step < ITERS - 1:
            sol, left, rounded = pl.pallas_call(
                functools.partial(apply_kernel, len(pieces)),
                out_shape=[field_type, field_type, rounded_type],
                in_specs=[in_vmem()] * (5 + len(pieces)),
                out_specs=[in_vmem()] * 3,
                compiler_params=params(),
                name="apply",
            )(high, low, left, sol, base, *pieces)
    return pl.pallas_call(
        functools.partial(finish_kernel, len(pieces)),
        out_shape=field_type,
        in_specs=[in_vmem()] * (4 + len(pieces)),
        out_specs=in_hbm(),
        scratch_shapes=[
            pltpu.VMEM((owned, rhs, size), jnp.float32),
            pltpu.SemaphoreType.DMA((2 if owned % 2 == 0 else 1,)),
        ],
        compiler_params=params(),
        name="finish",
    )(high, low, sol, base, *pieces)[None]


def solution(mesh):
    placed = (
        P("row", "col", None, None, None),
        P("row", "col", None),
        P("row", "col", None),
        P("row", "col"),
        P("col", "row", None, None),
        P("col", "row", None, None),
    )
    return jax.shard_map(
        per_device,
        mesh=mesh,
        in_specs=placed,
        out_specs=P("col", "row", None, None),
        check_vma=False,
    )
```

```python
import functools

import jax
import jax.numpy as jnp
from jax import lax
from jax.experimental import pallas as pl
from jax.experimental.pallas import tpu as pltpu
from jax.sharding import PartitionSpec as P

ITERS = 3
UNROLL = 16
LANES = 4
DEPTH = 6
APPLY_FLOPS = 20_000_000_000
CORES = 2
VMEM_LIMIT = 24 * 1024 * 1024

NT = (((1,), (1,)), ((), ()))


def in_vmem():
    return pl.BlockSpec(memory_space=pltpu.VMEM)


def in_hbm():
    return pl.BlockSpec(memory_space=pltpu.HBM)


def in_smem():
    return pl.BlockSpec(memory_space=pltpu.SMEM)


def stay_in_hbm(array):
    return pltpu.with_memory_space_constraint(array, pltpu.HBM)


def params():
    return pltpu.CompilerParams(vmem_limit_bytes=VMEM_LIMIT)


def split(value):
    high = value.astype(jnp.bfloat16)
    low = (value - high.astype(jnp.float32)).astype(jnp.bfloat16)
    return high, low


def times_block(field, high, low):
    field_high, field_low = split(field)
    rhs = field.shape[0]
    both = jnp.concatenate([field_high, field_low], axis=0)
    first = lax.dot_general(both, high, NT, preferred_element_type=jnp.float32)
    second = lax.dot_general(field_high, low, NT, preferred_element_type=jnp.float32)
    return first[:rhs] + (first[rhs:] + second)


def partner(chip, shift, chips):
    if chips & (chips - 1) == 0:
        return chip ^ shift
    return (chip + shift) % chips


def halves(value, size):
    if size & (size - 1) == 0:
        return lax.shift_right_logical(value, size.bit_length() - 1), value & (size - 1)
    return lax.div(value, size), lax.rem(value, size)


def relative(mine, source, groups):
    if groups % 2:
        away = mine - source
        return jnp.where(away < 0, away + groups, away)
    other = (mine ^ source) & 1
    away = (mine ^ other) - source
    away = jnp.where(away < 0, away + groups, away)
    return other * (groups // 2) + lax.shift_right_logical(away, 1)


def gather_stages(groups):
    if groups % 2:
        return [[0], list(range(1, groups))]
    pairs = groups // 2
    stages = [[0], list(range(1, pairs + 1)), list(range(pairs + 1, groups))]
    return [stage for stage in stages if stage]


def ring(groups, step):
    return [(c, (c + step) % groups) for c in range(groups)]


def gather(whole, rounded, groups):
    if groups % 2:
        return {step: [lax.ppermute(whole, "col", ring(groups, step))] for step in range(1, groups)}
    sets = {
        step: [lax.ppermute(piece, "col", ring(groups, 2 * step)) for piece in rounded]
        for step in range(1, groups // 2)
    }
    sets[groups // 2] = [lax.ppermute(piece, "col", neighbours(groups)) for piece in rounded]
    return sets


def neighbours(count):
    return [(index, index ^ 1) for index in range(count)]


def hold_kernel(piece_ref, token_ref, out_ref):
    pass


def start_kernel(precond_hbm, rhs_hbm, high_ref, low_ref, sol_ref, left_ref, rounded_ref, *refs):
    part_refs, (precond_ref, sems) = refs[:-2], refs[-2:]
    owned = left_ref.shape[0]
    parts = sems.shape[0] - 1
    each = owned // parts
    loads = [pltpu.make_async_copy(rhs_hbm, left_ref, sems.at[parts])]
    for part in range(parts):
        at = pl.ds(part * each, each)
        loads.append(pltpu.make_async_copy(precond_hbm.at[at], precond_ref.at[at], sems.at[part]))
    for load in loads:
        load.start()
    loads[0].wait()
    for part in range(parts):
        loads[1 + part].wait()
        for p in range(part * each, (part + 1) * each):
            high, low = split(precond_ref[p])
            high_ref[p] = high
            low_ref[p] = low
            value = times_block(left_ref[p], high, low)
            sol_ref[p] = value
            rounded = value.astype(jnp.bfloat16)
            rounded_ref[p] = rounded
            part_refs[p * len(part_refs) // owned][p % (owned // len(part_refs))] = rounded


def apply_kernel(part, earlier, pieces, high_ref, low_ref, left_ref, sol_ref, base_ref, *refs):
    piece_refs, refs = refs[:pieces], refs[pieces:]
    earlier_refs, refs = refs[:earlier], refs[earlier:]
    new_ref, new_left_ref, rounded_ref = refs[:3]
    each = rounded_ref.shape[0]
    for whole_ref in refs[3:]:
        for index, done_ref in enumerate(earlier_refs):
            whole_ref[pl.ds(index * each, each)] = done_ref[...]
    for inner in range(each):
        p = part * each + inner
        received = sum(piece_ref[inner].astype(jnp.float32) for piece_ref in piece_refs)
        value = sol_ref[p] + times_block(base_ref[p] - received, high_ref[p], low_ref[p])
        new_ref[p] = value
        new_left_ref[p] = left_ref[p] - received
        rounded_ref[inner] = value.astype(jnp.bfloat16)
        for whole_ref in refs[3:]:
            whole_ref[p] = value.astype(jnp.bfloat16)


def finish_kernel(pieces, high_ref, low_ref, sol_ref, base_ref, *refs):
    piece_refs, (out_hbm, value_ref, sems) = refs[:pieces], refs[pieces:]
    owned = sol_ref.shape[0]
    parts = sems.shape[0]
    each = owned // parts
    stores = []
    for part in range(parts):
        for p in range(part * each, (part + 1) * each):
            received = sum(piece_ref[p].astype(jnp.float32) for piece_ref in piece_refs)
            value_ref[p] = sol_ref[p] + times_block(base_ref[p] - received, high_ref[p], low_ref[p])
        at = pl.ds(part * each, each)
        stores.append(pltpu.make_async_copy(value_ref.at[at], out_hbm.at[at], sems.at[part]))
        stores[-1].start()
    for store in stores:
        store.wait()


def order_kernel(group, owned, groups, stages, bits, count_ref, rows_hbm, cols_hbm, values_hbm,
                 list_out, total_out, values_out, rows_ref, cols_ref, table_ref, total_ref, sems):
    loads = [
        pltpu.make_async_copy(rows_hbm, rows_ref, sems.at[0]),
        pltpu.make_async_copy(cols_hbm, cols_ref, sems.at[1]),
        pltpu.make_async_copy(values_hbm, values_out, sems.at[2]),
    ]
    for load in loads:
        load.start()
    core = lax.axis_index("row") & (CORES - 1)
    mine = lax.axis_index("col")
    row_bits, col_bits = bits
    lists = len(stages) * CORES
    trash = (group // CORES) << col_bits
    for index, stage in enumerate(stages):
        for place, piece in enumerate(stage):
            table_ref[piece] = ((index * CORES) << col_bits) + place * owned
    for index in range(lists + 1):
        total_ref[index] = 0
    for load in loads[:2]:
        load.wait()
    used = count_ref[0, 0]

    def place(chunk, carry):
        entries = []
        for lane in range(LANES):
            slot = chunk * LANES + lane
            owner, row_inner = halves(halves(rows_ref[0, 0, slot], group)[1], owned)
            source, rest = halves(cols_ref[0, 0, slot], group)
            half = 1 - ((owner & (CORES - 1)) ^ core)
            first, base = halves(table_ref[relative(mine, source, groups)], 1 << col_bits)
            which = jnp.where(slot < used, first + half, lists)
            row = lax.shift_right_logical(owner, 1) * owned + row_inner
            col = base + halves(rest, owned)[1]
            entries.append((which, (((slot << row_bits) | row) << col_bits) | col))
        for which, entry in entries:
            at = total_ref[which]
            list_out[which, at] = entry
            total_ref[which] = at + 1
        return carry

    lax.fori_loop(0, lax.div(used + LANES - 1, LANES), place, 0)
    for index in range(lists):
        total_out[index] = total_ref[index]

    def close(index, carry):
        for extra in range(UNROLL):
            list_out[index, total_ref[index] + extra] = trash
        return carry

    lax.fori_loop(0, lists, close, 0)
    loads[2].wait()


def add_products(which, bits, list_ref, total_ref, values_ref, field_ref, total):
    row_bits, col_bits = bits

    def step(chunk, carry):
        terms = []

        def store(row, term):
            total[row] += term

        for lane in range(UNROLL):
            entry = list_ref[which, chunk * UNROLL + lane]
            col = entry & ((1 << col_bits) - 1)
            row = lax.shift_right_logical(entry, col_bits) & ((1 << row_bits) - 1)
            slot = lax.shift_right_logical(entry, col_bits + row_bits)
            term = lax.dot_general(
                field_ref[col], values_ref[slot], NT, preferred_element_type=jnp.float32)
            terms.append((row, term))
            if len(terms) > DEPTH:
                store(*terms.pop(0))
        for row, term in terms:
            store(row, term)
        return carry

    lax.fori_loop(0, lax.div(total_ref[which] + UNROLL - 1, UNROLL), step, 0)


def join(pieces, field):
    if len(pieces) == 1:
        return pieces[0]
    at = 0
    for piece in pieces:
        field[pl.ds(at, piece.shape[0])] = piece[...]
        at += piece.shape[0]
    return field


def first_kernel(steps, parts, chips, bits, list_ref, total_ref, values_ref, field_ref, *refs):
    out_refs, refs = refs[:steps], refs[steps:]
    in_refs, refs = refs[:steps], refs[steps:]
    sent_refs, totals, token_ref = refs[:-CORES - 1], refs[-CORES - 1:-1], refs[-1]
    token_ref[...] = jnp.zeros_like(token_ref)
    chip = lax.axis_index("row") // CORES
    for half, total in enumerate(totals):
        rows = total.shape[0] - 1
        owned = rows // chips
        if steps == 0:
            total[...] = jnp.zeros(total.shape, jnp.float32)
        elif half == 0:
            total[pl.ds(0, rows)] = -sum(out_ref[...].astype(jnp.float32) for out_ref in out_refs)
        else:
            for shift in range(chips):
                for part in range(parts):
                    each = owned // parts
                    at = pl.ds(partner(chip, shift, chips) * owned + part * each, each)
                    value = sum(in_ref[at].astype(jnp.float32) for in_ref in in_refs)
                    if shift > 0:
                        for step in range(steps):
                            sent_ref = sent_refs[(step * parts + part) * (chips - 1) + shift - 1]
                            value -= sent_ref[...].astype(jnp.float32)
                    total[at] = value
        add_products(half, bits, list_ref, total_ref, values_ref, field_ref, total)


def stage_kernel(stage, bits, pieces, list_ref, total_ref, values_ref, *refs):
    piece_refs, refs = refs[:pieces], refs[pieces + CORES:]
    totals, field = refs[:CORES], refs[-1]
    field_ref = join(piece_refs, field)
    for half, total in enumerate(totals):
        add_products(stage * CORES + half, bits, list_ref, total_ref, values_ref, field_ref, total)


def last_kernel(stage, half, bits, pieces, list_ref, total_ref, values_ref, *refs):
    piece_refs, refs = refs[:pieces], refs[pieces + 1:]
    total, outs, field = refs[0], refs[1:-1], refs[-1]
    field_ref = join(piece_refs, field)
    add_products(stage * CORES + half, bits, list_ref, total_ref, values_ref, field_ref, total)
    for out_ref in outs:
        out_ref[...] = total[pl.ds(0, out_ref.shape[0])].astype(out_ref.dtype)


def chip_rows(shift, chips, part, parts, own_ref, other_ref):
    chip = lax.axis_index("row") // CORES
    owned = other_ref.shape[0] // chips
    each = owned // parts
    at = pl.ds(partner(chip, shift, chips) * owned + part * each, each)
    return own_ref[at] + other_ref[at].astype(jnp.float32)


def combine_kernel(shifts, chips, part, parts, own_ref, other_ref, *send_refs):
    for shift, send_ref in zip(shifts, send_refs):
        send_ref[...] = chip_rows(shift, chips, part, parts, own_ref, other_ref).astype(send_ref.dtype)


def keep_kernel(chips, own_ref, other_ref, left_ref, sol_ref, base_ref):
    base_ref[...] = left_ref[...] - sol_ref[...] - chip_rows(0, chips, 0, 1, own_ref, other_ref)


def per_device(block_values, block_rows, block_cols, block_counts, precond, right_side):
    owned, rhs, size = right_side.shape[1:]
    row_devices = lax.axis_size("row")
    groups = lax.axis_size("col")
    chips = row_devices // CORES
    group = owned * row_devices
    half_rows = chips * owned
    slots = block_values.shape[2]

    stages = gather_stages(groups)
    final = len(stages) - 1
    lists_total = len(stages) * CORES
    widest = max(len(stage) for stage in stages) * owned
    row_bits, col_bits = bits = half_rows.bit_length(), (widest - 1).bit_length()
    assert (slots - 1).bit_length() + row_bits + col_bits <= 31
    assert slots % LANES == 0

    field_type = jax.ShapeDtypeStruct((owned, rhs, size), jnp.float32)
    rounded_type = jax.ShapeDtypeStruct((owned, rhs, size), jnp.bfloat16)
    matrix_type = jax.ShapeDtypeStruct((owned, size, size), jnp.bfloat16)
    total_type = jax.ShapeDtypeStruct((half_rows + 1, rhs, size), jnp.float32)
    index_type = pltpu.SMEM(block_rows.shape, jnp.int32)
    token_type = jax.ShapeDtypeStruct((8, 128), jnp.float32)
    loads = next(count for count in (4, 2, 1) if owned % count == 0)
    parts = 2 if owned % 2 == 0 else 1
    part_type = jax.ShapeDtypeStruct((owned // parts, rhs, size), jnp.bfloat16)

    high, low, sol, left, whole, *rounded = pl.pallas_call(
        start_kernel,
        out_shape=[matrix_type] * 2 + [field_type] * 2 + [rounded_type] + [part_type] * parts,
        in_specs=[in_hbm()] * 2,
        out_specs=[in_vmem()] * (5 + parts),
        scratch_shapes=[
            pltpu.VMEM((owned, size, size), jnp.float32),
            pltpu.SemaphoreType.DMA((loads + 1,)),
        ],
        compiler_params=params(),
        name="start",
    )(stay_in_hbm(precond[0]), stay_in_hbm(right_side[0]))

    *lists, values = pl.pallas_call(
        functools.partial(order_kernel, group, owned, groups, stages, bits),
        out_shape=[
            pltpu.SMEM((lists_total + 1, slots + UNROLL), jnp.int32),
            pltpu.SMEM((lists_total,), jnp.int32),
            pltpu.VMEM(block_values.shape[2:], block_values.dtype),
        ],
        in_specs=[in_smem()] + [in_hbm()] * 3,
        out_specs=[in_smem()] * 2 + [in_vmem()],
        scratch_shapes=[
            index_type, index_type,
            pltpu.SMEM((groups,), jnp.int32), pltpu.SMEM((lists_total + 1,), jnp.int32),
            pltpu.SemaphoreType.DMA((3,)),
        ],
        compiler_params=params(),
        name="order",
    )(block_counts, *[stay_in_hbm(array) for array in (block_rows, block_cols, block_values[0, 0])])

    def cost(share):
        return pl.CostEstimate(
            flops=int(slots * share) * 2 * rhs * size * size,
            bytes_accessed=int(slots * share) * 2 * size * size, transcendentals=0)

    def field_scratch(pieces):
        return pltpu.VMEM((sum(piece.shape[0] for piece in pieces), rhs, size), jnp.bfloat16)

    def product_first(field, outs, ins, sent):
        return pl.pallas_call(
            functools.partial(first_kernel, len(outs), parts, chips, bits),
            out_shape=[total_type] * CORES + [token_type],
            in_specs=[in_smem()] * 2 + [in_vmem()] * (2 + len(outs) + len(ins) + len(sent)),
            out_specs=[in_vmem()] * (CORES + 1),
            compiler_params=params(),
            cost_estimate=cost(1 / groups),
            name="stage0",
        )(*lists, values, field, *outs, *ins, *sent)

    def product_stage(stage, pieces, totals):
        inputs = 3 + len(pieces)
        return pl.pallas_call(
            functools.partial(stage_kernel, stage, bits, len(pieces)),
            out_shape=[total_type] * CORES,
            in_specs=[in_smem()] * 2 + [in_vmem()] * (1 + len(pieces) + CORES),
            out_specs=[in_vmem()] * CORES,
            scratch_shapes=[field_scratch(pieces)],
            input_output_aliases={inputs + half: half for half in range(CORES)},
            compiler_params=params(),
            cost_estimate=cost(len(pieces) / groups),
            name="stage%d" % stage,
        )(*lists, values, *pieces, *totals)

    def product_last(half, pieces, total):
        send = [jax.ShapeDtypeStruct((half_rows, rhs, size), jnp.bfloat16)] if half == 0 else []
        return pl.pallas_call(
            functools.partial(last_kernel, final, half, bits, len(pieces)),
            out_shape=[total_type] + send,
            in_specs=[in_smem()] * 2 + [in_vmem()] * (2 + len(pieces)),
            out_specs=[in_vmem()] * (1 + len(send)),
            scratch_shapes=[field_scratch(pieces)],
            input_output_aliases={3 + len(pieces): 0},
            compiler_params=params(),
            cost_estimate=cost(len(pieces) / groups / CORES),
            name="last%d" % half,
        )(*lists, values, *pieces, total)[-1]

    def hold(piece, token):
        return pl.pallas_call(
            hold_kernel,
            out_shape=part_type,
            in_specs=[in_vmem()] * 2,
            out_specs=in_vmem(),
            input_output_aliases={0: 0},
            compiler_params=params(),
            name="hold",
        )(piece, token)

    shifts = list(reversed(range(1, chips)))

    def combine(part, parts, own, incoming):
        send_type = jax.ShapeDtypeStruct((owned // parts, rhs, size), jnp.bfloat16)
        return pl.pallas_call(
            functools.partial(combine_kernel, shifts, chips, part, parts),
            out_shape=[send_type] * len(shifts),
            in_specs=[in_vmem()] * 2,
            out_specs=[in_vmem()] * len(shifts),
            compiler_params=params(),
            name="combine%d" % part,
        )(own, incoming)

    def apply(part, sol, left, base, pieces, earlier):
        last = part == parts - 1
        return pl.pallas_call(
            functools.partial(apply_kernel, part, len(earlier), len(pieces)),
            out_shape=[field_type, field_type, part_type] + [rounded_type] * last,
            in_specs=[in_vmem()] * (5 + len(pieces) + len(earlier)),
            out_specs=[in_vmem()] * (3 + last),
            input_output_aliases={2: 1, 3: 0},
            compiler_params=params(),
            cost_estimate=pl.CostEstimate(flops=APPLY_FLOPS, bytes_accessed=0, transcendentals=0),
            name="apply%d" % part,
        )(high, low, left, sol, base, *pieces, *earlier)

    outs, ins, sent = [], [], []
    for step in range(ITERS):
        sets = gather(whole, rounded, groups)
        *totals, token = product_first(whole, outs, ins, sent)
        if groups % 2 == 0:
            for index in range(1, groups // 2):
                sets[index] = [hold(piece, token) for piece in sets[index]]
                sets[groups // 2 + index] = [lax.ppermute(piece, "col", neighbours(groups)) for piece in sets[index]]

        def stage_pieces(stage):
            return [piece for index in stages[stage] for piece in sets[index]]

        for stage in range(1, final):
            totals = product_stage(stage, stage_pieces(stage), totals)
        outgoing = product_last(0, stage_pieces(final), totals[0])
        incoming = lax.ppermute(outgoing, "row", neighbours(row_devices))
        own = product_last(1, stage_pieces(final), totals[1])
        outs.append(outgoing)
        ins.append(incoming)
        parts_now = parts if step < ITERS - 1 else 1
        received = []
        for part in range(parts_now):
            sends = combine(part, parts_now, own, incoming)
            sent += reversed(sends)
            received.append([
                lax.ppermute(send, "row", [
                    (chip * CORES + core, partner(chip, shift, chips) * CORES + core)
                    for chip in range(chips) for core in range(CORES)
                ])
                for shift, send in zip(shifts, sends)
            ])
        base = pl.pallas_call(
            functools.partial(keep_kernel, chips),
            out_shape=field_type,
            in_specs=[in_vmem()] * 4,
            out_specs=in_vmem(),
            compiler_params=params(),
            name="keep",
        )(own, incoming, left, sol)
        if step < ITERS - 1:
            rounded = []
            for part in range(parts):
                sol, left, new, *rest = apply(part, sol, left, base, received[part], rounded if part == parts - 1 else [])
                rounded.append(new)
            whole, = rest
    pieces = received[0]
    return pl.pallas_call(
        functools.partial(finish_kernel, len(pieces)),
        out_shape=field_type,
        in_specs=[in_vmem()] * (4 + len(pieces)),
        out_specs=in_hbm(),
        scratch_shapes=[
            pltpu.VMEM((owned, rhs, size), jnp.float32),
            pltpu.SemaphoreType.DMA((2 if owned % 2 == 0 else 1,)),
        ],
        compiler_params=params(),
        name="finish",
    )(high, low, sol, base, *pieces)[None]


def solution(mesh):
    placed = (
        P("row", "col", None, None, None),
        P("row", "col", None),
        P("row", "col", None),
        P("row", "col"),
        P("col", "row", None, None),
        P("col", "row", None, None),
    )
    return jax.shard_map(
        per_device,
        mesh=mesh,
        in_specs=placed,
        out_specs=P("col", "row", None, None),
        check_vma=False,
    )
```

```python
import functools

import jax
import jax.numpy as jnp
from jax import lax
from jax.experimental import pallas as pl
from jax.experimental.pallas import tpu as pltpu
from jax.sharding import PartitionSpec as P

ITERS = 3
UNROLL = 16
LANES = 4
DEPTH = 6
APPLY_FLOPS = 20_000_000_000
CORES = 2
VMEM_LIMIT = 24 * 1024 * 1024

NT = (((1,), (1,)), ((), ()))


def in_vmem():
    return pl.BlockSpec(memory_space=pltpu.VMEM)


def in_hbm():
    return pl.BlockSpec(memory_space=pltpu.HBM)


def in_smem():
    return pl.BlockSpec(memory_space=pltpu.SMEM)


def stay_in_hbm(array):
    return pltpu.with_memory_space_constraint(array, pltpu.HBM)


def params():
    return pltpu.CompilerParams(vmem_limit_bytes=VMEM_LIMIT)


def split(value):
    high = value.astype(jnp.bfloat16)
    low = (value - high.astype(jnp.float32)).astype(jnp.bfloat16)
    return high, low


def times_block(field, high, low):
    field_high, field_low = split(field)
    rhs = field.shape[0]
    both = jnp.concatenate([field_high, field_low], axis=0)
    first = lax.dot_general(both, high, NT, preferred_element_type=jnp.float32)
    second = lax.dot_general(field_high, low, NT, preferred_element_type=jnp.float32)
    return first[:rhs] + (first[rhs:] + second)


def partner(chip, shift, chips):
    if chips & (chips - 1) == 0:
        return chip ^ shift
    return (chip + shift) % chips


def halves(value, size):
    if size & (size - 1) == 0:
        return lax.shift_right_logical(value, size.bit_length() - 1), value & (size - 1)
    return lax.div(value, size), lax.rem(value, size)


def relative(mine, source, groups):
    if groups % 2:
        away = mine - source
        return jnp.where(away < 0, away + groups, away)
    other = (mine ^ source) & 1
    away = (mine ^ other) - source
    away = jnp.where(away < 0, away + groups, away)
    return other * (groups // 2) + lax.shift_right_logical(away, 1)


def gather_stages(groups, parts):
    every = range(parts)
    own = [(0, part) for part in every]
    if groups % 2:
        return [own, [(index, part) for index in range(1, groups) for part in every]]
    pairs = groups // 2
    early = range(parts - 1)
    stages = [
        own + [(index, part) for part in early for index in range(1, pairs + 1)],
        [(index, parts - 1) for index in range(1, pairs + 1)]
        + [(index, part) for part in early for index in range(pairs + 1, groups)],
        [(index, parts - 1) for index in range(pairs + 1, groups)],
    ]
    return [stage for stage in stages if stage]


def ring(groups, step):
    return [(c, (c + step) % groups) for c in range(groups)]


def gather(rounded, groups):
    sets = {(0, part): piece for part, piece in enumerate(rounded)}
    for part, piece in enumerate(rounded):
        if groups % 2:
            for step in range(1, groups):
                sets[step, part] = lax.ppermute(piece, "col", ring(groups, step))
        else:
            for step in range(1, groups // 2):
                sets[step, part] = lax.ppermute(piece, "col", ring(groups, 2 * step))
            sets[groups // 2, part] = lax.ppermute(piece, "col", neighbours(groups))
    return sets


def neighbours(count):
    return [(index, index ^ 1) for index in range(count)]


def hold_kernel(piece_ref, token_ref, out_ref):
    pass


def start_kernel(precond_hbm, rhs_hbm, high_ref, low_ref, sol_ref, left_ref, *refs):
    part_refs, (precond_ref, sems) = refs[:-2], refs[-2:]
    owned = left_ref.shape[0]
    parts = sems.shape[0] - 1
    each = owned // parts
    loads = [pltpu.make_async_copy(rhs_hbm, left_ref, sems.at[parts])]
    for part in range(parts):
        at = pl.ds(part * each, each)
        loads.append(pltpu.make_async_copy(precond_hbm.at[at], precond_ref.at[at], sems.at[part]))
    for load in loads:
        load.start()
    loads[0].wait()
    for part in range(parts):
        loads[1 + part].wait()
        for p in range(part * each, (part + 1) * each):
            high, low = split(precond_ref[p])
            high_ref[p] = high
            low_ref[p] = low
            value = times_block(left_ref[p], high, low)
            sol_ref[p] = value
            part_refs[p * len(part_refs) // owned][p % (owned // len(part_refs))] = value.astype(jnp.bfloat16)


def apply_kernel(part, pieces, high_ref, low_ref, left_ref, sol_ref, base_ref, *refs):
    piece_refs, (new_ref, new_left_ref, rounded_ref) = refs[:pieces], refs[pieces:]
    each = rounded_ref.shape[0]
    for inner in range(each):
        p = part * each + inner
        received = sum(piece_ref[inner].astype(jnp.float32) for piece_ref in piece_refs)
        value = sol_ref[p] + times_block(base_ref[p] - received, high_ref[p], low_ref[p])
        new_ref[p] = value
        new_left_ref[p] = left_ref[p] - received
        rounded_ref[inner] = value.astype(jnp.bfloat16)


def finish_kernel(pieces, high_ref, low_ref, sol_ref, base_ref, *refs):
    piece_refs, (out_hbm, value_ref, sems) = refs[:pieces], refs[pieces:]
    owned = sol_ref.shape[0]
    parts = sems.shape[0]
    each = owned // parts
    stores = []
    for part in range(parts):
        for p in range(part * each, (part + 1) * each):
            received = sum(piece_ref[p].astype(jnp.float32) for piece_ref in piece_refs)
            value_ref[p] = sol_ref[p] + times_block(base_ref[p] - received, high_ref[p], low_ref[p])
        at = pl.ds(part * each, each)
        stores.append(pltpu.make_async_copy(value_ref.at[at], out_hbm.at[at], sems.at[part]))
        stores[-1].start()
    for store in stores:
        store.wait()


def order_kernel(group, owned, groups, parts, stages, bits, count_ref, rows_hbm, cols_hbm, values_hbm,
                 list_out, total_out, values_out, rows_ref, cols_ref, table_ref, total_ref, sems):
    loads = [
        pltpu.make_async_copy(rows_hbm, rows_ref, sems.at[0]),
        pltpu.make_async_copy(cols_hbm, cols_ref, sems.at[1]),
        pltpu.make_async_copy(values_hbm, values_out, sems.at[2]),
    ]
    for load in loads:
        load.start()
    core = lax.axis_index("row") & (CORES - 1)
    mine = lax.axis_index("col")
    row_bits, col_bits = bits
    lists = len(stages) * CORES
    each = owned // parts
    trash = (group // CORES) << col_bits
    for index, stage in enumerate(stages):
        for place, (piece, part) in enumerate(stage):
            table_ref[piece * parts + part] = ((index * CORES) << col_bits) + place * each
    for index in range(lists + 1):
        total_ref[index] = 0
    for load in loads[:2]:
        load.wait()
    used = count_ref[0, 0]

    def place(chunk, carry):
        entries = []
        for lane in range(LANES):
            slot = chunk * LANES + lane
            owner, row_inner = halves(halves(rows_ref[0, 0, slot], group)[1], owned)
            source, rest = halves(cols_ref[0, 0, slot], group)
            half = 1 - ((owner & (CORES - 1)) ^ core)
            part, inner = halves(halves(rest, owned)[1], each)
            first, base = halves(table_ref[relative(mine, source, groups) * parts + part], 1 << col_bits)
            which = jnp.where(slot < used, first + half, lists)
            row = lax.shift_right_logical(owner, 1) * owned + row_inner
            col = base + inner
            entries.append((which, (((slot << row_bits) | row) << col_bits) | col))
        for which, entry in entries:
            at = total_ref[which]
            list_out[which, at] = entry
            total_ref[which] = at + 1
        return carry

    lax.fori_loop(0, lax.div(used + LANES - 1, LANES), place, 0)
    for index in range(lists):
        total_out[index] = total_ref[index]

    def close(index, carry):
        for extra in range(UNROLL):
            list_out[index, total_ref[index] + extra] = trash
        return carry

    lax.fori_loop(0, lists, close, 0)
    loads[2].wait()


def add_products(which, bits, list_ref, total_ref, values_ref, field_ref, total):
    row_bits, col_bits = bits

    def step(chunk, carry):
        terms = []

        def store(row, term):
            total[row] += term

        for lane in range(UNROLL):
            entry = list_ref[which, chunk * UNROLL + lane]
            col = entry & ((1 << col_bits) - 1)
            row = lax.shift_right_logical(entry, col_bits) & ((1 << row_bits) - 1)
            slot = lax.shift_right_logical(entry, col_bits + row_bits)
            term = lax.dot_general(
                field_ref[col], values_ref[slot], NT, preferred_element_type=jnp.float32)
            terms.append((row, term))
            if len(terms) > DEPTH:
                store(*terms.pop(0))
        for row, term in terms:
            store(row, term)
        return carry

    lax.fori_loop(0, lax.div(total_ref[which] + UNROLL - 1, UNROLL), step, 0)


def join(pieces, field):
    if len(pieces) == 1:
        return pieces[0]
    at = 0
    for piece in pieces:
        field[pl.ds(at, piece.shape[0])] = piece[...]
        at += piece.shape[0]
    return field


def first_kernel(pieces, steps, parts, chips, bits, list_ref, total_ref, values_ref, *refs):
    piece_refs, refs = refs[:pieces], refs[pieces:]
    out_refs, refs = refs[:steps], refs[steps:]
    in_refs, refs = refs[:steps], refs[steps:]
    sent_refs, totals, (token_ref, field) = refs[:-CORES - 2], refs[-CORES - 2:-2], refs[-2:]
    field_ref = join(piece_refs, field)
    token_ref[...] = jnp.zeros_like(token_ref)
    chip = lax.axis_index("row") // CORES
    for half, total in enumerate(totals):
        rows = total.shape[0] - 1
        owned = rows // chips
        if steps == 0:
            total[...] = jnp.zeros(total.shape, jnp.float32)
        elif half == 0:
            total[pl.ds(0, rows)] = -sum(out_ref[...].astype(jnp.float32) for out_ref in out_refs)
        else:
            for shift in range(chips):
                for part in range(parts):
                    each = owned // parts
                    at = pl.ds(partner(chip, shift, chips) * owned + part * each, each)
                    value = sum(in_ref[at].astype(jnp.float32) for in_ref in in_refs)
                    if shift > 0:
                        for step in range(steps):
                            sent_ref = sent_refs[(step * parts + part) * (chips - 1) + shift - 1]
                            value -= sent_ref[...].astype(jnp.float32)
                    total[at] = value
        add_products(half, bits, list_ref, total_ref, values_ref, field_ref, total)


def stage_kernel(stage, bits, pieces, list_ref, total_ref, values_ref, *refs):
    piece_refs, refs = refs[:pieces], refs[pieces + CORES:]
    totals, field = refs[:CORES], refs[-1]
    field_ref = join(piece_refs, field)
    for half, total in enumerate(totals):
        add_products(stage * CORES + half, bits, list_ref, total_ref, values_ref, field_ref, total)


def last_kernel(stage, half, bits, pieces, list_ref, total_ref, values_ref, *refs):
    piece_refs, refs = refs[:pieces], refs[pieces + 1:]
    total, outs, field = refs[0], refs[1:-1], refs[-1]
    field_ref = join(piece_refs, field)
    add_products(stage * CORES + half, bits, list_ref, total_ref, values_ref, field_ref, total)
    for out_ref in outs:
        out_ref[...] = total[pl.ds(0, out_ref.shape[0])].astype(out_ref.dtype)


def chip_rows(shift, chips, part, parts, own_ref, other_ref):
    chip = lax.axis_index("row") // CORES
    owned = other_ref.shape[0] // chips
    each = owned // parts
    at = pl.ds(partner(chip, shift, chips) * owned + part * each, each)
    return own_ref[at] + other_ref[at].astype(jnp.float32)


def combine_kernel(shifts, chips, part, parts, own_ref, other_ref, *send_refs):
    for shift, send_ref in zip(shifts, send_refs):
        send_ref[...] = chip_rows(shift, chips, part, parts, own_ref, other_ref).astype(send_ref.dtype)


def keep_kernel(chips, own_ref, other_ref, left_ref, sol_ref, base_ref):
    base_ref[...] = left_ref[...] - sol_ref[...] - chip_rows(0, chips, 0, 1, own_ref, other_ref)


def per_device(block_values, block_rows, block_cols, block_counts, precond, right_side):
    owned, rhs, size = right_side.shape[1:]
    row_devices = lax.axis_size("row")
    groups = lax.axis_size("col")
    chips = row_devices // CORES
    group = owned * row_devices
    half_rows = chips * owned
    slots = block_values.shape[2]

    parts = 2 if owned % 2 == 0 else 1
    stages = gather_stages(groups, parts)
    final = len(stages) - 1
    lists_total = len(stages) * CORES
    widest = max(len(stage) for stage in stages) * owned // parts
    row_bits, col_bits = bits = half_rows.bit_length(), (widest - 1).bit_length()
    assert (slots - 1).bit_length() + row_bits + col_bits <= 31
    assert slots % LANES == 0

    field_type = jax.ShapeDtypeStruct((owned, rhs, size), jnp.float32)
    matrix_type = jax.ShapeDtypeStruct((owned, size, size), jnp.bfloat16)
    total_type = jax.ShapeDtypeStruct((half_rows + 1, rhs, size), jnp.float32)
    index_type = pltpu.SMEM(block_rows.shape, jnp.int32)
    token_type = jax.ShapeDtypeStruct((8, 128), jnp.float32)
    loads = next(count for count in (4, 2, 1) if owned % count == 0)
    part_type = jax.ShapeDtypeStruct((owned // parts, rhs, size), jnp.bfloat16)

    high, low, sol, left, *rounded = pl.pallas_call(
        start_kernel,
        out_shape=[matrix_type] * 2 + [field_type] * 2 + [part_type] * parts,
        in_specs=[in_hbm()] * 2,
        out_specs=[in_vmem()] * (4 + parts),
        scratch_shapes=[
            pltpu.VMEM((owned, size, size), jnp.float32),
            pltpu.SemaphoreType.DMA((loads + 1,)),
        ],
        compiler_params=params(),
        name="start",
    )(stay_in_hbm(precond[0]), stay_in_hbm(right_side[0]))

    *lists, values = pl.pallas_call(
        functools.partial(order_kernel, group, owned, groups, parts, stages, bits),
        out_shape=[
            pltpu.SMEM((lists_total + 1, slots + UNROLL), jnp.int32),
            pltpu.SMEM((lists_total,), jnp.int32),
            pltpu.VMEM(block_values.shape[2:], block_values.dtype),
        ],
        in_specs=[in_smem()] + [in_hbm()] * 3,
        out_specs=[in_smem()] * 2 + [in_vmem()],
        scratch_shapes=[
            index_type, index_type,
            pltpu.SMEM((groups * parts,), jnp.int32), pltpu.SMEM((lists_total + 1,), jnp.int32),
            pltpu.SemaphoreType.DMA((3,)),
        ],
        compiler_params=params(),
        name="order",
    )(block_counts, *[stay_in_hbm(array) for array in (block_rows, block_cols, block_values[0, 0])])

    def cost(share):
        return pl.CostEstimate(
            flops=int(slots * share) * 2 * rhs * size * size,
            bytes_accessed=int(slots * share) * 2 * size * size, transcendentals=0)

    def field_scratch(pieces):
        return pltpu.VMEM((sum(piece.shape[0] for piece in pieces), rhs, size), jnp.bfloat16)

    def product_first(pieces, outs, ins, sent):
        return pl.pallas_call(
            functools.partial(first_kernel, len(pieces), len(outs), parts, chips, bits),
            out_shape=[total_type] * CORES + [token_type],
            in_specs=[in_smem()] * 2 + [in_vmem()] * (1 + len(pieces) + len(outs) + len(ins) + len(sent)),
            out_specs=[in_vmem()] * (CORES + 1),
            scratch_shapes=[field_scratch(pieces)],
            compiler_params=params(),
            cost_estimate=cost(len(pieces) / groups / parts),
            name="stage0",
        )(*lists, values, *pieces, *outs, *ins, *sent)

    def product_stage(stage, pieces, totals):
        inputs = 3 + len(pieces)
        return pl.pallas_call(
            functools.partial(stage_kernel, stage, bits, len(pieces)),
            out_shape=[total_type] * CORES,
            in_specs=[in_smem()] * 2 + [in_vmem()] * (1 + len(pieces) + CORES),
            out_specs=[in_vmem()] * CORES,
            scratch_shapes=[field_scratch(pieces)],
            input_output_aliases={inputs + half: half for half in range(CORES)},
            compiler_params=params(),
            cost_estimate=cost(len(pieces) / groups / parts),
            name="stage%d" % stage,
        )(*lists, values, *pieces, *totals)

    def product_last(half, pieces, total):
        send = [jax.ShapeDtypeStruct((half_rows, rhs, size), jnp.bfloat16)] if half == 0 else []
        return pl.pallas_call(
            functools.partial(last_kernel, final, half, bits, len(pieces)),
            out_shape=[total_type] + send,
            in_specs=[in_smem()] * 2 + [in_vmem()] * (2 + len(pieces)),
            out_specs=[in_vmem()] * (1 + len(send)),
            scratch_shapes=[field_scratch(pieces)],
            input_output_aliases={3 + len(pieces): 0},
            compiler_params=params(),
            cost_estimate=cost(len(pieces) / groups / parts / CORES),
            name="last%d" % half,
        )(*lists, values, *pieces, total)[-1]

    def hold(piece, token):
        return pl.pallas_call(
            hold_kernel,
            out_shape=part_type,
            in_specs=[in_vmem()] * 2,
            out_specs=in_vmem(),
            input_output_aliases={0: 0},
            compiler_params=params(),
            name="hold",
        )(piece, token)

    shifts = list(reversed(range(1, chips)))

    def combine(part, parts, own, incoming):
        send_type = jax.ShapeDtypeStruct((owned // parts, rhs, size), jnp.bfloat16)
        return pl.pallas_call(
            functools.partial(combine_kernel, shifts, chips, part, parts),
            out_shape=[send_type] * len(shifts),
            in_specs=[in_vmem()] * 2,
            out_specs=[in_vmem()] * len(shifts),
            compiler_params=params(),
            name="combine%d" % part,
        )(own, incoming)

    def apply(part, sol, left, base, pieces):
        return pl.pallas_call(
            functools.partial(apply_kernel, part, len(pieces)),
            out_shape=[field_type, field_type, part_type],
            in_specs=[in_vmem()] * (5 + len(pieces)),
            out_specs=[in_vmem()] * 3,
            input_output_aliases={2: 1, 3: 0},
            compiler_params=params(),
            cost_estimate=pl.CostEstimate(flops=APPLY_FLOPS, bytes_accessed=0, transcendentals=0),
            name="apply%d" % part,
        )(high, low, left, sol, base, *pieces)

    outs, ins, sent = [], [], []
    for step in range(ITERS):
        sets = gather(rounded, groups)

        def stage_pieces(stage):
            return [sets[piece] for piece in stages[stage]]

        *totals, token = product_first(stage_pieces(0), outs, ins, sent)
        if groups % 2 == 0:
            for index in range(1, groups // 2):
                for part in range(parts):
                    if part == parts - 1:
                        sets[index, part] = hold(sets[index, part], token)
                    sets[groups // 2 + index, part] = lax.ppermute(sets[index, part], "col", neighbours(groups))

        for stage in range(1, final):
            totals = product_stage(stage, stage_pieces(stage), totals)
        outgoing = product_last(0, stage_pieces(final), totals[0])
        incoming = lax.ppermute(outgoing, "row", neighbours(row_devices))
        own = product_last(1, stage_pieces(final), totals[1])
        outs.append(outgoing)
        ins.append(incoming)
        parts_now = parts if step < ITERS - 1 else 1
        received = []
        for part in range(parts_now):
            sends = combine(part, parts_now, own, incoming)
            sent += reversed(sends)
            received.append([
                lax.ppermute(send, "row", [
                    (chip * CORES + core, partner(chip, shift, chips) * CORES + core)
                    for chip in range(chips) for core in range(CORES)
                ])
                for shift, send in zip(shifts, sends)
            ])
        base = pl.pallas_call(
            functools.partial(keep_kernel, chips),
            out_shape=field_type,
            in_specs=[in_vmem()] * 4,
            out_specs=in_vmem(),
            compiler_params=params(),
            name="keep",
        )(own, incoming, left, sol)
        if step < ITERS - 1:
            rounded = []
            for part in range(parts):
                sol, left, new = apply(part, sol, left, base, received[part])
                rounded.append(new)
    pieces = received[0]
    return pl.pallas_call(
        functools.partial(finish_kernel, len(pieces)),
        out_shape=field_type,
        in_specs=[in_vmem()] * (4 + len(pieces)),
        out_specs=in_hbm(),
        scratch_shapes=[
            pltpu.VMEM((owned, rhs, size), jnp.float32),
            pltpu.SemaphoreType.DMA((2 if owned % 2 == 0 else 1,)),
        ],
        compiler_params=params(),
        name="finish",
    )(high, low, sol, base, *pieces)[None]


def solution(mesh):
    placed = (
        P("row", "col", None, None, None),
        P("row", "col", None),
        P("row", "col", None),
        P("row", "col"),
        P("col", "row", None, None),
        P("col", "row", None, None),
    )
    return jax.shard_map(
        per_device,
        mesh=mesh,
        in_specs=placed,
        out_specs=P("col", "row", None, None),
        check_vma=False,
    )
```

```python
import functools

import jax
import jax.numpy as jnp
from jax import lax
from jax.experimental import pallas as pl
from jax.experimental.pallas import tpu as pltpu
from jax.sharding import PartitionSpec as P

ITERS = 3
UNROLL = 16
LANES = 4
DEPTH = 6
APPLY_FLOPS = 20_000_000_000
CORES = 2
VMEM_LIMIT = 24 * 1024 * 1024

NT = (((1,), (1,)), ((), ()))


def in_vmem():
    return pl.BlockSpec(memory_space=pltpu.VMEM)


def in_hbm():
    return pl.BlockSpec(memory_space=pltpu.HBM)


def in_smem():
    return pl.BlockSpec(memory_space=pltpu.SMEM)


def stay_in_hbm(array):
    return pltpu.with_memory_space_constraint(array, pltpu.HBM)


def params():
    return pltpu.CompilerParams(vmem_limit_bytes=VMEM_LIMIT)


def split(value):
    high = value.astype(jnp.bfloat16)
    low = (value - high.astype(jnp.float32)).astype(jnp.bfloat16)
    return high, low


def times_block(field, high, low):
    field_high, field_low = split(field)
    rhs = field.shape[0]
    both = jnp.concatenate([field_high, field_low], axis=0)
    first = lax.dot_general(both, high, NT, preferred_element_type=jnp.float32)
    second = lax.dot_general(field_high, low, NT, preferred_element_type=jnp.float32)
    return first[:rhs] + (first[rhs:] + second)


def partner(chip, shift, chips):
    if chips & (chips - 1) == 0:
        return chip ^ shift
    return (chip + shift) % chips


def halves(value, size):
    if size & (size - 1) == 0:
        return lax.shift_right_logical(value, size.bit_length() - 1), value & (size - 1)
    return lax.div(value, size), lax.rem(value, size)


def relative(mine, source, groups):
    if groups % 2:
        away = mine - source
        return jnp.where(away < 0, away + groups, away)
    other = (mine ^ source) & 1
    away = (mine ^ other) - source
    away = jnp.where(away < 0, away + groups, away)
    return other * (groups // 2) + lax.shift_right_logical(away, 1)


def gather_stages(groups, parts):
    every = range(parts)
    own = [(0, part) for part in every]
    if groups % 2:
        return [own, [(index, part) for index in range(1, groups) for part in every]]
    pairs = groups // 2
    early = range(parts - 1)
    stages = [
        own + [(index, part) for part in early for index in range(1, pairs + 1)],
        [(index, parts - 1) for index in range(1, pairs + 1)]
        + [(index, part) for part in early for index in range(pairs + 1, groups)],
        [(index, parts - 1) for index in range(pairs + 1, groups)],
    ]
    return [stage for stage in stages if stage]


def ring(groups, step):
    return [(c, (c + step) % groups) for c in range(groups)]


def gather(rounded, groups):
    sets = {(0, part): piece for part, piece in enumerate(rounded)}
    for part, piece in enumerate(rounded):
        if groups % 2:
            for step in range(1, groups):
                sets[step, part] = lax.ppermute(piece, "col", ring(groups, step))
        else:
            for step in range(1, groups // 2):
                sets[step, part] = lax.ppermute(piece, "col", ring(groups, 2 * step))
            sets[groups // 2, part] = lax.ppermute(piece, "col", neighbours(groups))
    return sets


def neighbours(count):
    return [(index, index ^ 1) for index in range(count)]


def hold_kernel(piece_ref, token_ref, out_ref):
    pass


def start_kernel(precond_hbm, rhs_hbm, high_ref, low_ref, sol_ref, left_ref, *refs):
    part_refs, (precond_ref, sems) = refs[:-2], refs[-2:]
    owned = left_ref.shape[0]
    parts = sems.shape[0] - 1
    each = owned // parts
    loads = [pltpu.make_async_copy(rhs_hbm, left_ref, sems.at[parts])]
    for part in range(parts):
        at = pl.ds(part * each, each)
        loads.append(pltpu.make_async_copy(precond_hbm.at[at], precond_ref.at[at], sems.at[part]))
    for load in loads:
        load.start()
    loads[0].wait()
    for part in range(parts):
        loads[1 + part].wait()
        for p in range(part * each, (part + 1) * each):
            high, low = split(precond_ref[p])
            high_ref[p] = high
            low_ref[p] = low
            value = times_block(left_ref[p], high, low)
            sol_ref[p] = value
            part_refs[p * len(part_refs) // owned][p % (owned // len(part_refs))] = value.astype(jnp.bfloat16)


def apply_kernel(part, pieces, high_ref, low_ref, left_ref, sol_ref, base_ref, *refs):
    piece_refs, (new_ref, new_left_ref, rounded_ref) = refs[:pieces], refs[pieces:]
    each = rounded_ref.shape[0]
    for inner in range(each):
        p = part * each + inner
        received = sum(piece_ref[inner].astype(jnp.float32) for piece_ref in piece_refs)
        value = sol_ref[p] + times_block(base_ref[p] - received, high_ref[p], low_ref[p])
        new_ref[p] = value
        new_left_ref[p] = left_ref[p] - received
        rounded_ref[inner] = value.astype(jnp.bfloat16)


def finish_kernel(pieces, high_ref, low_ref, sol_ref, base_ref, *refs):
    piece_refs, (out_hbm, value_ref, sems) = refs[:pieces], refs[pieces:]
    owned = sol_ref.shape[0]
    parts = sems.shape[0]
    each = owned // parts
    stores = []
    for part in range(parts):
        for p in range(part * each, (part + 1) * each):
            received = sum(piece_ref[p].astype(jnp.float32) for piece_ref in piece_refs)
            value_ref[p] = sol_ref[p] + times_block(base_ref[p] - received, high_ref[p], low_ref[p])
        at = pl.ds(part * each, each)
        stores.append(pltpu.make_async_copy(value_ref.at[at], out_hbm.at[at], sems.at[part]))
        stores[-1].start()
    for store in stores:
        store.wait()


def order_kernel(group, owned, groups, parts, stages, bits, count_ref, rows_hbm, cols_hbm, values_hbm,
                 list_out, total_out, values_out, rows_ref, cols_ref, table_ref, total_ref, sems):
    loads = [
        pltpu.make_async_copy(rows_hbm, rows_ref, sems.at[0]),
        pltpu.make_async_copy(cols_hbm, cols_ref, sems.at[1]),
        pltpu.make_async_copy(values_hbm, values_out, sems.at[2]),
    ]
    for load in loads:
        load.start()
    core = lax.axis_index("row") & (CORES - 1)
    mine = lax.axis_index("col")
    row_bits, col_bits = bits
    lists = len(stages) * CORES
    each = owned // parts
    trash = (group // CORES) << col_bits
    for index, stage in enumerate(stages):
        for place, (piece, part) in enumerate(stage):
            table_ref[piece * parts + part] = ((index * CORES) << col_bits) + place * each
    for index in range(lists + 1):
        total_ref[index] = 0
    for load in loads[:2]:
        load.wait()
    used = count_ref[0, 0]

    def place(chunk, carry):
        entries = []
        for lane in range(LANES):
            slot = chunk * LANES + lane
            owner, row_inner = halves(halves(rows_ref[0, 0, slot], group)[1], owned)
            source, rest = halves(cols_ref[0, 0, slot], group)
            half = 1 - ((owner & (CORES - 1)) ^ core)
            part, inner = halves(halves(rest, owned)[1], each)
            first, base = halves(table_ref[relative(mine, source, groups) * parts + part], 1 << col_bits)
            which = jnp.where(slot < used, first + half, lists)
            row = lax.shift_right_logical(owner, 1) * owned + row_inner
            col = base + inner
            entries.append((which, (((slot << row_bits) | row) << col_bits) | col))
        for which, entry in entries:
            at = total_ref[which]
            list_out[which, at] = entry
            total_ref[which] = at + 1
        return carry

    lax.fori_loop(0, lax.div(used + LANES - 1, LANES), place, 0)
    for index in range(lists):
        total_out[index] = total_ref[index]

    def close(index, carry):
        for extra in range(UNROLL):
            list_out[index, total_ref[index] + extra] = trash
        return carry

    lax.fori_loop(0, lists, close, 0)
    loads[2].wait()

    def turn(chunk, carry):
        blocks = [values_out[chunk * LANES + lane] for lane in range(LANES)]
        for lane, block in enumerate(blocks):
            values_out[chunk * LANES + lane] = block.T
        return carry

    lax.fori_loop(0, lax.div(used + LANES - 1, LANES), turn, 0)


def add_products(which, bits, list_ref, total_ref, values_ref, field_ref, total):
    row_bits, col_bits = bits

    def step(chunk, carry):
        terms = []

        def store(row, term):
            total[row] += term

        for lane in range(UNROLL):
            entry = list_ref[which, chunk * UNROLL + lane]
            col = entry & ((1 << col_bits) - 1)
            row = lax.shift_right_logical(entry, col_bits) & ((1 << row_bits) - 1)
            slot = lax.shift_right_logical(entry, col_bits + row_bits)
            term = jnp.dot(field_ref[col], values_ref[slot], preferred_element_type=jnp.float32)
            terms.append((row, term))
            if len(terms) > DEPTH:
                store(*terms.pop(0))
        for row, term in terms:
            store(row, term)
        return carry

    lax.fori_loop(0, lax.div(total_ref[which] + UNROLL - 1, UNROLL), step, 0)


def join(pieces, field):
    if len(pieces) == 1:
        return pieces[0]
    at = 0
    for piece in pieces:
        field[pl.ds(at, piece.shape[0])] = piece[...]
        at += piece.shape[0]
    return field


def first_kernel(pieces, steps, parts, chips, bits, list_ref, total_ref, values_ref, *refs):
    piece_refs, refs = refs[:pieces], refs[pieces:]
    out_refs, refs = refs[:steps], refs[steps:]
    in_refs, refs = refs[:steps], refs[steps:]
    sent_refs, totals, (token_ref, field) = refs[:-CORES - 2], refs[-CORES - 2:-2], refs[-2:]
    field_ref = join(piece_refs, field)
    token_ref[...] = jnp.zeros_like(token_ref)
    chip = lax.axis_index("row") // CORES
    for half, total in enumerate(totals):
        rows = total.shape[0] - 1
        owned = rows // chips
        if steps == 0:
            total[...] = jnp.zeros(total.shape, jnp.float32)
        elif half == 0:
            total[pl.ds(0, rows)] = -sum(out_ref[...].astype(jnp.float32) for out_ref in out_refs)
        else:
            for shift in range(chips):
                for part in range(parts):
                    each = owned // parts
                    at = pl.ds(partner(chip, shift, chips) * owned + part * each, each)
                    value = sum(in_ref[at].astype(jnp.float32) for in_ref in in_refs)
                    if shift > 0:
                        for step in range(steps):
                            sent_ref = sent_refs[(step * parts + part) * (chips - 1) + shift - 1]
                            value -= sent_ref[...].astype(jnp.float32)
                    total[at] = value
        add_products(half, bits, list_ref, total_ref, values_ref, field_ref, total)


def stage_kernel(stage, bits, pieces, list_ref, total_ref, values_ref, *refs):
    piece_refs, refs = refs[:pieces], refs[pieces + CORES:]
    totals, field = refs[:CORES], refs[-1]
    field_ref = join(piece_refs, field)
    for half, total in enumerate(totals):
        add_products(stage * CORES + half, bits, list_ref, total_ref, values_ref, field_ref, total)


def last_kernel(stage, half, bits, pieces, list_ref, total_ref, values_ref, *refs):
    piece_refs, refs = refs[:pieces], refs[pieces + 1:]
    total, outs, field = refs[0], refs[1:-1], refs[-1]
    field_ref = join(piece_refs, field)
    add_products(stage * CORES + half, bits, list_ref, total_ref, values_ref, field_ref, total)
    for out_ref in outs:
        out_ref[...] = total[pl.ds(0, out_ref.shape[0])].astype(out_ref.dtype)


def chip_rows(shift, chips, part, parts, own_ref, other_ref):
    chip = lax.axis_index("row") // CORES
    owned = other_ref.shape[0] // chips
    each = owned // parts
    at = pl.ds(partner(chip, shift, chips) * owned + part * each, each)
    return own_ref[at] + other_ref[at].astype(jnp.float32)


def combine_kernel(shifts, chips, part, parts, own_ref, other_ref, *send_refs):
    for shift, send_ref in zip(shifts, send_refs):
        send_ref[...] = chip_rows(shift, chips, part, parts, own_ref, other_ref).astype(send_ref.dtype)


def keep_kernel(chips, own_ref, other_ref, left_ref, sol_ref, base_ref):
    base_ref[...] = left_ref[...] - sol_ref[...] - chip_rows(0, chips, 0, 1, own_ref, other_ref)


def per_device(block_values, block_rows, block_cols, block_counts, precond, right_side):
    owned, rhs, size = right_side.shape[1:]
    row_devices = lax.axis_size("row")
    groups = lax.axis_size("col")
    chips = row_devices // CORES
    group = owned * row_devices
    half_rows = chips * owned
    slots = block_values.shape[2]

    parts = 2 if owned % 2 == 0 else 1
    stages = gather_stages(groups, parts)
    final = len(stages) - 1
    lists_total = len(stages) * CORES
    widest = max(len(stage) for stage in stages) * owned // parts
    row_bits, col_bits = bits = half_rows.bit_length(), (widest - 1).bit_length()
    assert (slots - 1).bit_length() + row_bits + col_bits <= 31
    assert slots % LANES == 0

    field_type = jax.ShapeDtypeStruct((owned, rhs, size), jnp.float32)
    matrix_type = jax.ShapeDtypeStruct((owned, size, size), jnp.bfloat16)
    total_type = jax.ShapeDtypeStruct((half_rows + 1, rhs, size), jnp.float32)
    index_type = pltpu.SMEM(block_rows.shape, jnp.int32)
    token_type = jax.ShapeDtypeStruct((8, 128), jnp.float32)
    loads = next(count for count in (4, 2, 1) if owned % count == 0)
    part_type = jax.ShapeDtypeStruct((owned // parts, rhs, size), jnp.bfloat16)

    high, low, sol, left, *rounded = pl.pallas_call(
        start_kernel,
        out_shape=[matrix_type] * 2 + [field_type] * 2 + [part_type] * parts,
        in_specs=[in_hbm()] * 2,
        out_specs=[in_vmem()] * (4 + parts),
        scratch_shapes=[
            pltpu.VMEM((owned, size, size), jnp.float32),
            pltpu.SemaphoreType.DMA((loads + 1,)),
        ],
        compiler_params=params(),
        name="start",
    )(stay_in_hbm(precond[0]), stay_in_hbm(right_side[0]))

    *lists, values = pl.pallas_call(
        functools.partial(order_kernel, group, owned, groups, parts, stages, bits),
        out_shape=[
            pltpu.SMEM((lists_total + 1, slots + UNROLL), jnp.int32),
            pltpu.SMEM((lists_total,), jnp.int32),
            pltpu.VMEM(block_values.shape[2:], block_values.dtype),
        ],
        in_specs=[in_smem()] + [in_hbm()] * 3,
        out_specs=[in_smem()] * 2 + [in_vmem()],
        scratch_shapes=[
            index_type, index_type,
            pltpu.SMEM((groups * parts,), jnp.int32), pltpu.SMEM((lists_total + 1,), jnp.int32),
            pltpu.SemaphoreType.DMA((3,)),
        ],
        compiler_params=params(),
        name="order",
    )(block_counts, *[stay_in_hbm(array) for array in (block_rows, block_cols, block_values[0, 0])])

    def cost(share):
        return pl.CostEstimate(
            flops=int(slots * share) * 2 * rhs * size * size,
            bytes_accessed=int(slots * share) * 2 * size * size, transcendentals=0)

    def field_scratch(pieces):
        return pltpu.VMEM((sum(piece.shape[0] for piece in pieces), rhs, size), jnp.bfloat16)

    def product_first(pieces, outs, ins, sent):
        return pl.pallas_call(
            functools.partial(first_kernel, len(pieces), len(outs), parts, chips, bits),
            out_shape=[total_type] * CORES + [token_type],
            in_specs=[in_smem()] * 2 + [in_vmem()] * (1 + len(pieces) + len(outs) + len(ins) + len(sent)),
            out_specs=[in_vmem()] * (CORES + 1),
            scratch_shapes=[field_scratch(pieces)],
            compiler_params=params(),
            cost_estimate=cost(len(pieces) / groups / parts),
            name="stage0",
        )(*lists, values, *pieces, *outs, *ins, *sent)

    def product_stage(stage, pieces, totals):
        inputs = 3 + len(pieces)
        return pl.pallas_call(
            functools.partial(stage_kernel, stage, bits, len(pieces)),
            out_shape=[total_type] * CORES,
            in_specs=[in_smem()] * 2 + [in_vmem()] * (1 + len(pieces) + CORES),
            out_specs=[in_vmem()] * CORES,
            scratch_shapes=[field_scratch(pieces)],
            input_output_aliases={inputs + half: half for half in range(CORES)},
            compiler_params=params(),
            cost_estimate=cost(len(pieces) / groups / parts),
            name="stage%d" % stage,
        )(*lists, values, *pieces, *totals)

    def product_last(half, pieces, total):
        send = [jax.ShapeDtypeStruct((half_rows, rhs, size), jnp.bfloat16)] if half == 0 else []
        return pl.pallas_call(
            functools.partial(last_kernel, final, half, bits, len(pieces)),
            out_shape=[total_type] + send,
            in_specs=[in_smem()] * 2 + [in_vmem()] * (2 + len(pieces)),
            out_specs=[in_vmem()] * (1 + len(send)),
            scratch_shapes=[field_scratch(pieces)],
            input_output_aliases={3 + len(pieces): 0},
            compiler_params=params(),
            cost_estimate=cost(len(pieces) / groups / parts / CORES),
            name="last%d" % half,
        )(*lists, values, *pieces, total)[-1]

    def hold(piece, token):
        return pl.pallas_call(
            hold_kernel,
            out_shape=part_type,
            in_specs=[in_vmem()] * 2,
            out_specs=in_vmem(),
            input_output_aliases={0: 0},
            compiler_params=params(),
            name="hold",
        )(piece, token)

    shifts = list(reversed(range(1, chips)))

    def combine(part, parts, own, incoming):
        send_type = jax.ShapeDtypeStruct((owned // parts, rhs, size), jnp.bfloat16)
        return pl.pallas_call(
            functools.partial(combine_kernel, shifts, chips, part, parts),
            out_shape=[send_type] * len(shifts),
            in_specs=[in_vmem()] * 2,
            out_specs=[in_vmem()] * len(shifts),
            compiler_params=params(),
            name="combine%d" % part,
        )(own, incoming)

    def apply(part, sol, left, base, pieces):
        return pl.pallas_call(
            functools.partial(apply_kernel, part, len(pieces)),
            out_shape=[field_type, field_type, part_type],
            in_specs=[in_vmem()] * (5 + len(pieces)),
            out_specs=[in_vmem()] * 3,
            input_output_aliases={2: 1, 3: 0},
            compiler_params=params(),
            cost_estimate=pl.CostEstimate(flops=APPLY_FLOPS, bytes_accessed=0, transcendentals=0),
            name="apply%d" % part,
        )(high, low, left, sol, base, *pieces)

    outs, ins, sent = [], [], []
    for step in range(ITERS):
        sets = gather(rounded, groups)

        def stage_pieces(stage):
            return [sets[piece] for piece in stages[stage]]

        *totals, token = product_first(stage_pieces(0), outs, ins, sent)
        if groups % 2 == 0:
            for index in range(1, groups // 2):
                for part in range(parts):
                    if part == parts - 1:
                        sets[index, part] = hold(sets[index, part], token)
                    sets[groups // 2 + index, part] = lax.ppermute(sets[index, part], "col", neighbours(groups))

        for stage in range(1, final):
            totals = product_stage(stage, stage_pieces(stage), totals)
        outgoing = product_last(0, stage_pieces(final), totals[0])
        incoming = lax.ppermute(outgoing, "row", neighbours(row_devices))
        own = product_last(1, stage_pieces(final), totals[1])
        outs.append(outgoing)
        ins.append(incoming)
        parts_now = parts if step < ITERS - 1 else 1
        received = []
        for part in range(parts_now):
            sends = combine(part, parts_now, own, incoming)
            sent += reversed(sends)
            received.append([
                lax.ppermute(send, "row", [
                    (chip * CORES + core, partner(chip, shift, chips) * CORES + core)
                    for chip in range(chips) for core in range(CORES)
                ])
                for shift, send in zip(shifts, sends)
            ])
        base = pl.pallas_call(
            functools.partial(keep_kernel, chips),
            out_shape=field_type,
            in_specs=[in_vmem()] * 4,
            out_specs=in_vmem(),
            compiler_params=params(),
            name="keep",
        )(own, incoming, left, sol)
        if step < ITERS - 1:
            rounded = []
            for part in range(parts):
                sol, left, new = apply(part, sol, left, base, received[part])
                rounded.append(new)
    pieces = received[0]
    return pl.pallas_call(
        functools.partial(finish_kernel, len(pieces)),
        out_shape=field_type,
        in_specs=[in_vmem()] * (4 + len(pieces)),
        out_specs=in_hbm(),
        scratch_shapes=[
            pltpu.VMEM((owned, rhs, size), jnp.float32),
            pltpu.SemaphoreType.DMA((2 if owned % 2 == 0 else 1,)),
        ],
        compiler_params=params(),
        name="finish",
    )(high, low, sol, base, *pieces)[None]


def solution(mesh):
    placed = (
        P("row", "col", None, None, None),
        P("row", "col", None),
        P("row", "col", None),
        P("row", "col"),
        P("col", "row", None, None),
        P("col", "row", None, None),
    )
    return jax.shard_map(
        per_device,
        mesh=mesh,
        in_specs=placed,
        out_specs=P("col", "row", None, None),
        check_vma=False,
    )
```

```python
import functools

import jax
import jax.numpy as jnp
from jax import lax
from jax.experimental import pallas as pl
from jax.experimental.pallas import tpu as pltpu
from jax.sharding import PartitionSpec as P

ITERS = 3
UNROLL = 16
LANES = 4
DEPTH = 6
CORES = 2
VMEM_LIMIT = 24 * 1024 * 1024

NT = (((1,), (1,)), ((), ()))


def in_vmem():
    return pl.BlockSpec(memory_space=pltpu.VMEM)


def in_hbm():
    return pl.BlockSpec(memory_space=pltpu.HBM)


def in_smem():
    return pl.BlockSpec(memory_space=pltpu.SMEM)


def stay_in_hbm(array):
    return pltpu.with_memory_space_constraint(array, pltpu.HBM)


def params():
    return pltpu.CompilerParams(vmem_limit_bytes=VMEM_LIMIT)


def split(value):
    high = value.astype(jnp.bfloat16)
    low = (value - high.astype(jnp.float32)).astype(jnp.bfloat16)
    return high, low


def times_block(field, high, low):
    field_high, field_low = split(field)
    rhs = field.shape[0]
    both = jnp.concatenate([field_high, field_low], axis=0)
    first = lax.dot_general(both, high, NT, preferred_element_type=jnp.float32)
    second = lax.dot_general(field_high, low, NT, preferred_element_type=jnp.float32)
    return first[:rhs] + (first[rhs:] + second)


def partner(chip, shift, chips):
    if chips & (chips - 1) == 0:
        return chip ^ shift
    return (chip + shift) % chips


def halves(value, size):
    if size & (size - 1) == 0:
        return lax.shift_right_logical(value, size.bit_length() - 1), value & (size - 1)
    return lax.div(value, size), lax.rem(value, size)


def relative(mine, source, groups):
    if groups % 2:
        away = mine - source
        return jnp.where(away < 0, away + groups, away)
    other = (mine ^ source) & 1
    away = (mine ^ other) - source
    away = jnp.where(away < 0, away + groups, away)
    return other * (groups // 2) + lax.shift_right_logical(away, 1)


def gather_stages(groups, parts):
    every = range(parts)
    own = [(0, part) for part in every]
    if groups % 2:
        return [own, [(index, part) for index in range(1, groups) for part in every]]
    pairs = groups // 2
    early = range(parts - 1)
    far, forwarded = range(1, pairs), range(pairs + 1, groups)
    stages = [
        own + [(index, part) for part in early for index in far],
        [(pairs, part) for part in every] + [(index, parts - 1) for index in far]
        + [(index, part) for part in early for index in forwarded],
        [(index, parts - 1) for index in forwarded],
    ]
    return [stage for stage in stages if stage]


def ring(groups, step):
    return [(c, (c + step) % groups) for c in range(groups)]


def gather(whole, rounded, groups):
    sets = {(0, 0): whole}
    if groups % 2:
        for step in range(1, groups):
            sets[step, 0] = lax.ppermute(whole, "col", ring(groups, step))
        return sets
    for part, piece in enumerate(rounded):
        for step in range(1, groups // 2):
            sets[step, part] = lax.ppermute(piece, "col", ring(groups, 2 * step))
    sets[groups // 2, 0] = lax.ppermute(whole, "col", neighbours(groups))
    return sets


def neighbours(count):
    return [(index, index ^ 1) for index in range(count)]


def hold_kernel(piece_ref, token_ref, out_ref):
    pass


def put_rounded(p, value, whole_ref, part_refs):
    part, inner = divmod(p, part_refs[0].shape[0])
    rounded = value.astype(jnp.bfloat16)
    whole_ref[p] = rounded
    part_refs[part][inner] = rounded


def start_kernel(precond_hbm, rhs_hbm, high_ref, low_ref, sol_ref, left_ref, whole_ref, *refs):
    part_refs, (precond_ref, sems) = refs[:-2], refs[-2:]
    owned = left_ref.shape[0]
    parts = sems.shape[0] - 1
    each = owned // parts
    loads = [pltpu.make_async_copy(rhs_hbm, left_ref, sems.at[parts])]
    for part in range(parts):
        at = pl.ds(part * each, each)
        loads.append(pltpu.make_async_copy(precond_hbm.at[at], precond_ref.at[at], sems.at[part]))
    for load in loads:
        load.start()
    loads[0].wait()
    for part in range(parts):
        loads[1 + part].wait()
        for p in range(part * each, (part + 1) * each):
            high, low = split(precond_ref[p])
            high_ref[p] = high
            low_ref[p] = low
            value = times_block(left_ref[p], high, low)
            sol_ref[p] = value
            put_rounded(p, value, whole_ref, part_refs)


def apply_kernel(pieces, high_ref, low_ref, left_ref, sol_ref, base_ref, *refs):
    piece_refs, (new_ref, new_left_ref, whole_ref, *part_refs) = refs[:pieces], refs[pieces:]
    for p in range(sol_ref.shape[0]):
        received = sum(piece_ref[p].astype(jnp.float32) for piece_ref in piece_refs)
        value = sol_ref[p] + times_block(base_ref[p] - received, high_ref[p], low_ref[p])
        new_ref[p] = value
        new_left_ref[p] = left_ref[p] - received
        put_rounded(p, value, whole_ref, part_refs)


def finish_kernel(pieces, high_ref, low_ref, sol_ref, base_ref, *refs):
    piece_refs, (out_hbm, value_ref, sems) = refs[:pieces], refs[pieces:]
    owned = sol_ref.shape[0]
    parts = sems.shape[0]
    each = owned // parts
    stores = []
    for part in range(parts):
        for p in range(part * each, (part + 1) * each):
            received = sum(piece_ref[p].astype(jnp.float32) for piece_ref in piece_refs)
            value_ref[p] = sol_ref[p] + times_block(base_ref[p] - received, high_ref[p], low_ref[p])
        at = pl.ds(part * each, each)
        stores.append(pltpu.make_async_copy(value_ref.at[at], out_hbm.at[at], sems.at[part]))
        stores[-1].start()
    for store in stores:
        store.wait()


def order_kernel(group, owned, groups, parts, stages, bits, count_ref, rows_hbm, cols_hbm, values_hbm,
                 list_out, total_out, values_out, rows_ref, cols_ref, table_ref, total_ref, sems):
    loads = [
        pltpu.make_async_copy(rows_hbm, rows_ref, sems.at[0]),
        pltpu.make_async_copy(cols_hbm, cols_ref, sems.at[1]),
        pltpu.make_async_copy(values_hbm, values_out, sems.at[2]),
    ]
    for load in loads:
        load.start()
    core = lax.axis_index("row") & (CORES - 1)
    mine = lax.axis_index("col")
    row_bits, col_bits = bits
    lists = len(stages) * CORES
    each = owned // parts
    trash = (group // CORES) << col_bits
    for index, stage in enumerate(stages):
        for place, (piece, part) in enumerate(stage):
            table_ref[piece * parts + part] = ((index * CORES) << col_bits) + place * each
    for index in range(lists + 1):
        total_ref[index] = 0
    for load in loads[:2]:
        load.wait()
    used = count_ref[0, 0]

    def place(chunk, carry):
        entries = []
        for lane in range(LANES):
            slot = chunk * LANES + lane
            owner, row_inner = halves(halves(rows_ref[0, 0, slot], group)[1], owned)
            source, rest = halves(cols_ref[0, 0, slot], group)
            half = 1 - ((owner & (CORES - 1)) ^ core)
            part, inner = halves(halves(rest, owned)[1], each)
            first, base = halves(table_ref[relative(mine, source, groups) * parts + part], 1 << col_bits)
            which = jnp.where(slot < used, first + half, lists)
            row = lax.shift_right_logical(owner, 1) * owned + row_inner
            col = base + inner
            entries.append((which, (((slot << row_bits) | row) << col_bits) | col))
        for which, entry in entries:
            at = total_ref[which]
            list_out[which, at] = entry
            total_ref[which] = at + 1
        return carry

    lax.fori_loop(0, lax.div(used + LANES - 1, LANES), place, 0)
    for index in range(lists):
        total_out[index] = total_ref[index]

    def close(index, carry):
        for extra in range(UNROLL):
            list_out[index, total_ref[index] + extra] = trash
        return carry

    lax.fori_loop(0, lists, close, 0)
    loads[2].wait()

    def turn(chunk, carry):
        blocks = [values_out[chunk * LANES + lane] for lane in range(LANES)]
        for lane, block in enumerate(blocks):
            values_out[chunk * LANES + lane] = block.T
        return carry

    lax.fori_loop(0, lax.div(used + LANES - 1, LANES), turn, 0)


def add_products(which, bits, list_ref, total_ref, values_ref, field_ref, total):
    row_bits, col_bits = bits

    def step(chunk, carry):
        terms = []

        def store(row, term):
            total[row] += term

        for lane in range(UNROLL):
            entry = list_ref[which, chunk * UNROLL + lane]
            col = entry & ((1 << col_bits) - 1)
            row = lax.shift_right_logical(entry, col_bits) & ((1 << row_bits) - 1)
            slot = lax.shift_right_logical(entry, col_bits + row_bits)
            term = jnp.dot(field_ref[col], values_ref[slot], preferred_element_type=jnp.float32)
            terms.append((row, term))
            if len(terms) > DEPTH:
                store(*terms.pop(0))
        for row, term in terms:
            store(row, term)
        return carry

    lax.fori_loop(0, lax.div(total_ref[which] + UNROLL - 1, UNROLL), step, 0)


def join(pieces, field):
    if len(pieces) == 1:
        return pieces[0]
    at = 0
    for piece in pieces:
        field[pl.ds(at, piece.shape[0])] = piece[...]
        at += piece.shape[0]
    return field


def first_kernel(pieces, steps, chips, bits, list_ref, total_ref, values_ref, *refs):
    piece_refs, refs = refs[:pieces], refs[pieces:]
    out_refs, refs = refs[:steps], refs[steps:]
    in_refs, refs = refs[:steps], refs[steps:]
    sent_refs, totals, (token_ref, field) = refs[:-CORES - 2], refs[-CORES - 2:-2], refs[-2:]
    field_ref = join(piece_refs, field)
    token_ref[...] = jnp.zeros_like(token_ref)
    chip = lax.axis_index("row") // CORES
    for half, total in enumerate(totals):
        rows = total.shape[0] - 1
        owned = rows // chips
        if steps == 0:
            total[...] = jnp.zeros(total.shape, jnp.float32)
        elif half == 0:
            total[pl.ds(0, rows)] = -sum(out_ref[...].astype(jnp.float32) for out_ref in out_refs)
        else:
            for shift in range(chips):
                at = pl.ds(partner(chip, shift, chips) * owned, owned)
                value = sum(in_ref[at].astype(jnp.float32) for in_ref in in_refs)
                if shift > 0:
                    for step in range(steps):
                        value -= sent_refs[step * (chips - 1) + shift - 1][...].astype(jnp.float32)
                total[at] = value
        add_products(half, bits, list_ref, total_ref, values_ref, field_ref, total)


def stage_kernel(stage, bits, pieces, list_ref, total_ref, values_ref, *refs):
    piece_refs, refs = refs[:pieces], refs[pieces + CORES:]
    totals, field = refs[:CORES], refs[-1]
    field_ref = join(piece_refs, field)
    for half, total in enumerate(totals):
        add_products(stage * CORES + half, bits, list_ref, total_ref, values_ref, field_ref, total)


def last_kernel(stage, half, bits, pieces, list_ref, total_ref, values_ref, *refs):
    piece_refs, refs = refs[:pieces], refs[pieces + 1:]
    total, outs, field = refs[0], refs[1:-1], refs[-1]
    field_ref = join(piece_refs, field)
    add_products(stage * CORES + half, bits, list_ref, total_ref, values_ref, field_ref, total)
    for out_ref in outs:
        out_ref[...] = total[pl.ds(0, out_ref.shape[0])].astype(out_ref.dtype)


def chip_rows(shift, chips, own_ref, other_ref):
    chip = lax.axis_index("row") // CORES
    owned = other_ref.shape[0] // chips
    at = pl.ds(partner(chip, shift, chips) * owned, owned)
    return own_ref[at] + other_ref[at].astype(jnp.float32)


def combine_kernel(shifts, chips, own_ref, other_ref, *send_refs):
    for shift, send_ref in zip(shifts, send_refs):
        send_ref[...] = chip_rows(shift, chips, own_ref, other_ref).astype(send_ref.dtype)


def keep_kernel(chips, own_ref, other_ref, left_ref, sol_ref, base_ref):
    base_ref[...] = left_ref[...] - sol_ref[...] - chip_rows(0, chips, own_ref, other_ref)


def per_device(block_values, block_rows, block_cols, block_counts, precond, right_side):
    owned, rhs, size = right_side.shape[1:]
    row_devices = lax.axis_size("row")
    groups = lax.axis_size("col")
    chips = row_devices // CORES
    group = owned * row_devices
    half_rows = chips * owned
    slots = block_values.shape[2]

    parts = 2 if owned % 2 == 0 else 1
    stages = gather_stages(groups, parts)
    final = len(stages) - 1
    lists_total = len(stages) * CORES
    widest = max(len(stage) for stage in stages) * owned // parts
    row_bits, col_bits = bits = half_rows.bit_length(), (widest - 1).bit_length()
    assert (slots - 1).bit_length() + row_bits + col_bits <= 31
    assert slots % LANES == 0

    field_type = jax.ShapeDtypeStruct((owned, rhs, size), jnp.float32)
    matrix_type = jax.ShapeDtypeStruct((owned, size, size), jnp.bfloat16)
    total_type = jax.ShapeDtypeStruct((half_rows + 1, rhs, size), jnp.float32)
    index_type = pltpu.SMEM(block_rows.shape, jnp.int32)
    token_type = jax.ShapeDtypeStruct((8, 128), jnp.float32)
    loads = next(count for count in (4, 2, 1) if owned % count == 0)
    rounded_type = jax.ShapeDtypeStruct((owned, rhs, size), jnp.bfloat16)
    part_type = jax.ShapeDtypeStruct((owned // parts, rhs, size), jnp.bfloat16)

    high, low, sol, left, whole, *rounded = pl.pallas_call(
        start_kernel,
        out_shape=[matrix_type] * 2 + [field_type] * 2 + [rounded_type] + [part_type] * parts,
        in_specs=[in_hbm()] * 2,
        out_specs=[in_vmem()] * (5 + parts),
        scratch_shapes=[
            pltpu.VMEM((owned, size, size), jnp.float32),
            pltpu.SemaphoreType.DMA((loads + 1,)),
        ],
        compiler_params=params(),
        name="start",
    )(stay_in_hbm(precond[0]), stay_in_hbm(right_side[0]))

    *lists, values = pl.pallas_call(
        functools.partial(order_kernel, group, owned, groups, parts, stages, bits),
        out_shape=[
            pltpu.SMEM((lists_total + 1, slots + UNROLL), jnp.int32),
            pltpu.SMEM((lists_total,), jnp.int32),
            pltpu.VMEM(block_values.shape[2:], block_values.dtype),
        ],
        in_specs=[in_smem()] + [in_hbm()] * 3,
        out_specs=[in_smem()] * 2 + [in_vmem()],
        scratch_shapes=[
            index_type, index_type,
            pltpu.SMEM((groups * parts,), jnp.int32), pltpu.SMEM((lists_total + 1,), jnp.int32),
            pltpu.SemaphoreType.DMA((3,)),
        ],
        compiler_params=params(),
        name="order",
    )(block_counts, *[stay_in_hbm(array) for array in (block_rows, block_cols, block_values[0, 0])])

    def cost(share):
        return pl.CostEstimate(
            flops=int(slots * share) * 2 * rhs * size * size,
            bytes_accessed=int(slots * share) * 2 * size * size, transcendentals=0)

    def field_scratch(pieces):
        return pltpu.VMEM((sum(piece.shape[0] for piece in pieces), rhs, size), jnp.bfloat16)

    def product_first(pieces, outs, ins, sent):
        return pl.pallas_call(
            functools.partial(first_kernel, len(pieces), len(outs), chips, bits),
            out_shape=[total_type] * CORES + [token_type],
            in_specs=[in_smem()] * 2 + [in_vmem()] * (1 + len(pieces) + len(outs) + len(ins) + len(sent)),
            out_specs=[in_vmem()] * (CORES + 1),
            compiler_params=params(),
            scratch_shapes=[field_scratch(pieces)],
            cost_estimate=cost(len(stages[0]) / groups / parts),
            name="stage0",
        )(*lists, values, *pieces, *outs, *ins, *sent)

    def product_stage(stage, pieces, totals):
        inputs = 3 + len(pieces)
        return pl.pallas_call(
            functools.partial(stage_kernel, stage, bits, len(pieces)),
            out_shape=[total_type] * CORES,
            in_specs=[in_smem()] * 2 + [in_vmem()] * (1 + len(pieces) + CORES),
            out_specs=[in_vmem()] * CORES,
            scratch_shapes=[field_scratch(pieces)],
            input_output_aliases={inputs + half: half for half in range(CORES)},
            compiler_params=params(),
            cost_estimate=cost(len(stages[stage]) / groups / parts),
            name="stage%d" % stage,
        )(*lists, values, *pieces, *totals)

    def product_last(half, pieces, total):
        send = [jax.ShapeDtypeStruct((half_rows, rhs, size), jnp.bfloat16)] if half == 0 else []
        return pl.pallas_call(
            functools.partial(last_kernel, final, half, bits, len(pieces)),
            out_shape=[total_type] + send,
            in_specs=[in_smem()] * 2 + [in_vmem()] * (2 + len(pieces)),
            out_specs=[in_vmem()] * (1 + len(send)),
            scratch_shapes=[field_scratch(pieces)],
            input_output_aliases={3 + len(pieces): 0},
            compiler_params=params(),
            cost_estimate=cost(len(stages[final]) / groups / parts / CORES),
            name="last%d" % half,
        )(*lists, values, *pieces, total)[-1]

    def hold(piece, token):
        return pl.pallas_call(
            hold_kernel,
            out_shape=part_type,
            in_specs=[in_vmem()] * 2,
            out_specs=in_vmem(),
            input_output_aliases={0: 0},
            compiler_params=params(),
            name="hold",
        )(piece, token)

    shifts = list(reversed(range(1, chips)))

    def combine(own, incoming):
        return pl.pallas_call(
            functools.partial(combine_kernel, shifts, chips),
            out_shape=[rounded_type] * len(shifts),
            in_specs=[in_vmem()] * 2,
            out_specs=[in_vmem()] * len(shifts),
            compiler_params=params(),
            name="combine",
        )(own, incoming)

    outs, ins, sent = [], [], []
    for step in range(ITERS):
        sets = gather(whole, rounded, groups)

        def stage_pieces(stage):
            return [sets[piece] for piece in stages[stage] if piece in sets]

        def forward(part, token=None):
            for index in range(1, groups // 2):
                if token is not None:
                    sets[index, part] = hold(sets[index, part], token)
                sets[groups // 2 + index, part] = lax.ppermute(sets[index, part], "col", neighbours(groups))

        if groups % 2 == 0:
            for part in range(parts - 1):
                forward(part)
        *totals, token = product_first(stage_pieces(0), outs, ins, sent)
        if groups % 2 == 0:
            forward(parts - 1, token)

        for stage in range(1, final):
            totals = product_stage(stage, stage_pieces(stage), totals)
        outgoing = product_last(0, stage_pieces(final), totals[0])
        incoming = lax.ppermute(outgoing, "row", neighbours(row_devices))
        own = product_last(1, stage_pieces(final), totals[1])
        outs.append(outgoing)
        ins.append(incoming)
        sends = combine(own, incoming)
        sent += reversed(sends)
        pieces = [
            lax.ppermute(send, "row", [
                (chip * CORES + core, partner(chip, shift, chips) * CORES + core)
                for chip in range(chips) for core in range(CORES)
            ])
            for shift, send in zip(shifts, sends)
        ]
        base = pl.pallas_call(
            functools.partial(keep_kernel, chips),
            out_shape=field_type,
            in_specs=[in_vmem()] * 4,
            out_specs=in_vmem(),
            compiler_params=params(),
            name="keep",
        )(own, incoming, left, sol)
        if step < ITERS - 1:
            sol, left, whole, *rounded = pl.pallas_call(
                functools.partial(apply_kernel, len(pieces)),
                out_shape=[field_type, field_type, rounded_type] + [part_type] * parts,
                in_specs=[in_vmem()] * (5 + len(pieces)),
                out_specs=[in_vmem()] * (3 + parts),
                compiler_params=params(),
                name="apply",
            )(high, low, left, sol, base, *pieces)
    return pl.pallas_call(
        functools.partial(finish_kernel, len(pieces)),
        out_shape=field_type,
        in_specs=[in_vmem()] * (4 + len(pieces)),
        out_specs=in_hbm(),
        scratch_shapes=[
            pltpu.VMEM((owned, rhs, size), jnp.float32),
            pltpu.SemaphoreType.DMA((2 if owned % 2 == 0 else 1,)),
        ],
        compiler_params=params(),
        name="finish",
    )(high, low, sol, base, *pieces)[None]


def solution(mesh):
    placed = (
        P("row", "col", None, None, None),
        P("row", "col", None),
        P("row", "col", None),
        P("row", "col"),
        P("col", "row", None, None),
        P("col", "row", None, None),
    )
    return jax.shard_map(
        per_device,
        mesh=mesh,
        in_specs=placed,
        out_specs=P("col", "row", None, None),
        check_vma=False,
    )
```

```python
import functools

import jax
import jax.numpy as jnp
from jax import lax
from jax.experimental import pallas as pl
from jax.experimental.pallas import tpu as pltpu
from jax.sharding import PartitionSpec as P

ITERS = 3
UNROLL = 16
LANES = 4
DEPTH = 6
LAST_FLOPS = 20_000_000_000
CORES = 2
VMEM_LIMIT = 24 * 1024 * 1024

NT = (((1,), (1,)), ((), ()))


def in_vmem():
    return pl.BlockSpec(memory_space=pltpu.VMEM)


def in_hbm():
    return pl.BlockSpec(memory_space=pltpu.HBM)


def in_smem():
    return pl.BlockSpec(memory_space=pltpu.SMEM)


def stay_in_hbm(array):
    return pltpu.with_memory_space_constraint(array, pltpu.HBM)


def params():
    return pltpu.CompilerParams(vmem_limit_bytes=VMEM_LIMIT)


def split(value):
    high = value.astype(jnp.bfloat16)
    low = (value - high.astype(jnp.float32)).astype(jnp.bfloat16)
    return high, low


def times_block(field, high, low):
    field_high, field_low = split(field)
    rhs = field.shape[0]
    both = jnp.concatenate([field_high, field_low], axis=0)
    first = lax.dot_general(both, high, NT, preferred_element_type=jnp.float32)
    second = lax.dot_general(field_high, low, NT, preferred_element_type=jnp.float32)
    return first[:rhs] + (first[rhs:] + second)


def partner(chip, shift, chips):
    if chips & (chips - 1) == 0:
        return chip ^ shift
    return (chip + shift) % chips


def halves(value, size):
    if size & (size - 1) == 0:
        return lax.shift_right_logical(value, size.bit_length() - 1), value & (size - 1)
    return lax.div(value, size), lax.rem(value, size)


def relative(mine, source, groups):
    if groups % 2:
        away = mine - source
        return jnp.where(away < 0, away + groups, away)
    other = (mine ^ source) & 1
    away = (mine ^ other) - source
    away = jnp.where(away < 0, away + groups, away)
    return other * (groups // 2) + lax.shift_right_logical(away, 1)


def gather_stages(groups, parts):
    every = range(parts)
    own = [(0, part) for part in every]
    if groups % 2:
        return [own, [(index, part) for index in range(1, groups) for part in every]]
    pairs = groups // 2
    early = range(parts - 1)
    far, forwarded = range(1, pairs), range(pairs + 1, groups)
    stages = [
        own + [(index, part) for part in early for index in far],
        [(pairs, part) for part in every] + [(index, parts - 1) for index in far]
        + [(index, part) for part in early for index in forwarded],
        [(index, parts - 1) for index in forwarded],
    ]
    return [stage for stage in stages if stage]


def ring(groups, step):
    return [(c, (c + step) % groups) for c in range(groups)]


def gather(whole, rounded, groups):
    sets = {(0, 0): whole}
    if groups % 2:
        for step in range(1, groups):
            sets[step, 0] = lax.ppermute(whole, "col", ring(groups, step))
        return sets
    for part, piece in enumerate(rounded):
        for step in range(1, groups // 2):
            sets[step, part] = lax.ppermute(piece, "col", ring(groups, 2 * step))
    sets[groups // 2, 0] = lax.ppermute(whole, "col", neighbours(groups))
    return sets


def neighbours(count):
    return [(index, index ^ 1) for index in range(count)]


def hold_kernel(piece_ref, token_ref, out_ref):
    pass


def put_rounded(p, value, whole_ref, part_refs):
    part, inner = divmod(p, part_refs[0].shape[0])
    rounded = value.astype(jnp.bfloat16)
    whole_ref[p] = rounded
    part_refs[part][inner] = rounded


def start_kernel(precond_hbm, rhs_hbm, high_ref, low_ref, sol_ref, left_ref, whole_ref, *refs):
    part_refs, (precond_ref, sems) = refs[:-2], refs[-2:]
    owned = left_ref.shape[0]
    parts = sems.shape[0] - 1
    each = owned // parts
    loads = [pltpu.make_async_copy(rhs_hbm, left_ref, sems.at[parts])]
    for part in range(parts):
        at = pl.ds(part * each, each)
        loads.append(pltpu.make_async_copy(precond_hbm.at[at], precond_ref.at[at], sems.at[part]))
    for load in loads:
        load.start()
    loads[0].wait()
    for part in range(parts):
        loads[1 + part].wait()
        for p in range(part * each, (part + 1) * each):
            high, low = split(precond_ref[p])
            high_ref[p] = high
            low_ref[p] = low
            value = times_block(left_ref[p], high, low)
            sol_ref[p] = value
            put_rounded(p, value, whole_ref, part_refs)


def apply_kernel(pieces, high_ref, low_ref, left_ref, sol_ref, base_ref, *refs):
    piece_refs, (new_ref, new_left_ref, whole_ref, *part_refs) = refs[:pieces], refs[pieces:]
    for p in range(sol_ref.shape[0]):
        received = sum(piece_ref[p].astype(jnp.float32) for piece_ref in piece_refs)
        value = sol_ref[p] + times_block(base_ref[p] - received, high_ref[p], low_ref[p])
        new_ref[p] = value
        new_left_ref[p] = left_ref[p] - received
        put_rounded(p, value, whole_ref, part_refs)


def finish_kernel(pieces, high_ref, low_ref, sol_ref, base_ref, *refs):
    piece_refs, (out_hbm, value_ref, sems) = refs[:pieces], refs[pieces:]
    owned = sol_ref.shape[0]
    parts = sems.shape[0]
    each = owned // parts
    stores = []
    for part in range(parts):
        for p in range(part * each, (part + 1) * each):
            received = sum(piece_ref[p].astype(jnp.float32) for piece_ref in piece_refs)
            value_ref[p] = sol_ref[p] + times_block(base_ref[p] - received, high_ref[p], low_ref[p])
        at = pl.ds(part * each, each)
        stores.append(pltpu.make_async_copy(value_ref.at[at], out_hbm.at[at], sems.at[part]))
        stores[-1].start()
    for store in stores:
        store.wait()


def order_kernel(group, owned, groups, parts, stages, bits, count_ref, rows_hbm, cols_hbm, values_hbm,
                 list_out, total_out, values_out, token_ref, rows_ref, cols_ref, table_ref, total_ref, sems):
    token_ref[...] = jnp.zeros_like(token_ref)
    loads = [
        pltpu.make_async_copy(rows_hbm, rows_ref, sems.at[0]),
        pltpu.make_async_copy(cols_hbm, cols_ref, sems.at[1]),
        pltpu.make_async_copy(values_hbm, values_out, sems.at[2]),
    ]
    for load in loads:
        load.start()
    core = lax.axis_index("row") & (CORES - 1)
    mine = lax.axis_index("col")
    row_bits, col_bits = bits
    lists = len(stages) * CORES
    each = owned // parts
    trash = (group // CORES) << col_bits
    for index, stage in enumerate(stages):
        for place, (piece, part) in enumerate(stage):
            table_ref[piece * parts + part] = ((index * CORES) << col_bits) + place * each
    for index in range(lists + 1):
        total_ref[index] = 0
    for load in loads[:2]:
        load.wait()
    used = count_ref[0, 0]

    def place(chunk, carry):
        entries = []
        for lane in range(LANES):
            slot = chunk * LANES + lane
            owner, row_inner = halves(halves(rows_ref[0, 0, slot], group)[1], owned)
            source, rest = halves(cols_ref[0, 0, slot], group)
            half = 1 - ((owner & (CORES - 1)) ^ core)
            part, inner = halves(halves(rest, owned)[1], each)
            first, base = halves(table_ref[relative(mine, source, groups) * parts + part], 1 << col_bits)
            which = jnp.where(slot < used, first + half, lists)
            row = lax.shift_right_logical(owner, 1) * owned + row_inner
            col = base + inner
            entries.append((which, (((slot << row_bits) | row) << col_bits) | col))
        for which, entry in entries:
            at = total_ref[which]
            list_out[which, at] = entry
            total_ref[which] = at + 1
        return carry

    lax.fori_loop(0, lax.div(used + LANES - 1, LANES), place, 0)
    for index in range(lists):
        total_out[index] = total_ref[index]

    def close(index, carry):
        for extra in range(UNROLL):
            list_out[index, total_ref[index] + extra] = trash
        return carry

    lax.fori_loop(0, lists, close, 0)
    loads[2].wait()


def turn_kernel(total_ref, values_ref, turned_ref, token_ref):
    token_ref[...] = jnp.zeros_like(token_ref)
    used = sum(total_ref[index] for index in range(total_ref.shape[0]))

    def turn(chunk, carry):
        blocks = [values_ref[chunk * LANES + lane] for lane in range(LANES)]
        for lane, block in enumerate(blocks):
            turned_ref[chunk * LANES + lane] = block.T
        return carry

    lax.fori_loop(0, lax.div(used + LANES - 1, LANES), turn, 0)


def add_products(which, bits, list_ref, total_ref, values_ref, field_ref, total):
    row_bits, col_bits = bits

    def step(chunk, carry):
        terms = []

        def store(row, term):
            total[row] += term

        for lane in range(UNROLL):
            entry = list_ref[which, chunk * UNROLL + lane]
            col = entry & ((1 << col_bits) - 1)
            row = lax.shift_right_logical(entry, col_bits) & ((1 << row_bits) - 1)
            slot = lax.shift_right_logical(entry, col_bits + row_bits)
            term = jnp.dot(field_ref[col], values_ref[slot], preferred_element_type=jnp.float32)
            terms.append((row, term))
            if len(terms) > DEPTH:
                store(*terms.pop(0))
        for row, term in terms:
            store(row, term)
        return carry

    lax.fori_loop(0, lax.div(total_ref[which] + UNROLL - 1, UNROLL), step, 0)


def join(pieces, field):
    if len(pieces) == 1:
        return pieces[0]
    at = 0
    for piece in pieces:
        field[pl.ds(at, piece.shape[0])] = piece[...]
        at += piece.shape[0]
    return field


def swap_order(chips):
    return list(reversed(range(chips)))


def swapped_early(chips):
    return chips // 2


def swapped_rows(index, chips, owned, first_ref, rest_ref):
    early = swapped_early(chips)
    if index < early:
        return first_ref[pl.ds(index * owned, owned)]
    return rest_ref[pl.ds((index - early) * owned, owned)]


def first_kernel(pieces, steps, chips, bits, list_ref, total_ref, values_ref, *refs):
    piece_refs, refs = refs[:pieces], refs[pieces:]
    out_refs, refs = refs[:2 * steps], refs[2 * steps:]
    in_refs, refs = refs[:2 * steps], refs[2 * steps:]
    sent_refs, totals, (token_ref, field) = refs[:-CORES - 2], refs[-CORES - 2:-2], refs[-2:]
    field_ref = join(piece_refs, field)
    token_ref[...] = jnp.zeros_like(token_ref)
    chip = lax.axis_index("row") // CORES
    for half, total in enumerate(totals):
        rows = total.shape[0] - 1
        owned = rows // chips
        if steps == 0:
            total[...] = jnp.zeros(total.shape, jnp.float32)
        else:
            for index, shift in enumerate(swap_order(chips)):
                swapped = in_refs if half else out_refs
                value = sum(
                    swapped_rows(index, chips, owned, *swapped[2 * step:2 * step + 2]).astype(jnp.float32)
                    for step in range(steps))
                if half == 0:
                    value = -value
                elif shift > 0:
                    for step in range(steps):
                        value -= sent_refs[step * (chips - 1) + index][...].astype(jnp.float32)
                total[pl.ds(partner(chip, shift, chips) * owned, owned)] = value
        add_products(half, bits, list_ref, total_ref, values_ref, field_ref, total)


def stage_kernel(stage, bits, pieces, list_ref, total_ref, values_ref, *refs):
    piece_refs, refs = refs[:pieces], refs[pieces + CORES:]
    totals, field = refs[:CORES], refs[-1]
    field_ref = join(piece_refs, field)
    for half, total in enumerate(totals):
        add_products(stage * CORES + half, bits, list_ref, total_ref, values_ref, field_ref, total)


def last_kernel(stage, half, bits, pieces, chips, list_ref, total_ref, values_ref, *refs):
    piece_refs, refs = refs[:pieces], refs[pieces + 1:]
    if half == 0:
        total, out_ref, field = refs
        other = total
    else:
        other, total, out_ref, field = refs
    field_ref = join(piece_refs, field)
    add_products(stage * CORES + half, bits, list_ref, total_ref, values_ref, field_ref, total)
    chip = lax.axis_index("row") // CORES
    owned = (other.shape[0] - 1) // chips
    shifts, early = swap_order(chips), swapped_early(chips)
    for index, shift in enumerate(shifts[early:] if half else shifts[:early]):
        rows = other[pl.ds(partner(chip, shift, chips) * owned, owned)]
        out_ref[pl.ds(index * owned, owned)] = rows.astype(out_ref.dtype)


def chip_rows(index, chips, owned, own_ref, *other_refs):
    chip = lax.axis_index("row") // CORES
    at = pl.ds(partner(chip, swap_order(chips)[index], chips) * owned, owned)
    return own_ref[at] + swapped_rows(index, chips, owned, *other_refs).astype(jnp.float32)


def combine_first_kernel(chips, own_ref, first_ref, *send_refs):
    for index, send_ref in enumerate(send_refs):
        rows = chip_rows(index, chips, send_ref.shape[0], own_ref, first_ref, None)
        send_ref[...] = rows.astype(send_ref.dtype)


def combine_rest_kernel(chips, own_ref, rest_ref, left_ref, sol_ref, base_ref, *send_refs):
    owned = base_ref.shape[0]
    for index, send_ref in enumerate(send_refs):
        rows = chip_rows(swapped_early(chips) + index, chips, owned, own_ref, None, rest_ref)
        send_ref[...] = rows.astype(send_ref.dtype)
    keep = chip_rows(chips - 1, chips, owned, own_ref, None, rest_ref)
    base_ref[...] = left_ref[...] - sol_ref[...] - keep


def per_device(block_values, block_rows, block_cols, block_counts, precond, right_side):
    owned, rhs, size = right_side.shape[1:]
    row_devices = lax.axis_size("row")
    groups = lax.axis_size("col")
    chips = row_devices // CORES
    group = owned * row_devices
    half_rows = chips * owned
    slots = block_values.shape[2]

    parts = 2 if owned % 2 == 0 else 1
    stages = gather_stages(groups, parts)
    final = len(stages) - 1
    lists_total = len(stages) * CORES
    widest = max(len(stage) for stage in stages) * owned // parts
    row_bits, col_bits = bits = half_rows.bit_length(), (widest - 1).bit_length()
    assert (slots - 1).bit_length() + row_bits + col_bits <= 31
    assert slots % LANES == 0

    field_type = jax.ShapeDtypeStruct((owned, rhs, size), jnp.float32)
    matrix_type = jax.ShapeDtypeStruct((owned, size, size), jnp.bfloat16)
    total_type = jax.ShapeDtypeStruct((half_rows + 1, rhs, size), jnp.float32)
    index_type = pltpu.SMEM(block_rows.shape, jnp.int32)
    token_type = jax.ShapeDtypeStruct((8, 128), jnp.float32)
    loads = next(count for count in (4, 2, 1) if owned % count == 0)
    rounded_type = jax.ShapeDtypeStruct((owned, rhs, size), jnp.bfloat16)
    part_type = jax.ShapeDtypeStruct((owned // parts, rhs, size), jnp.bfloat16)

    high, low, sol, left, whole, *rounded = pl.pallas_call(
        start_kernel,
        out_shape=[matrix_type] * 2 + [field_type] * 2 + [rounded_type] + [part_type] * parts,
        in_specs=[in_hbm()] * 2,
        out_specs=[in_vmem()] * (5 + parts),
        scratch_shapes=[
            pltpu.VMEM((owned, size, size), jnp.float32),
            pltpu.SemaphoreType.DMA((loads + 1,)),
        ],
        compiler_params=params(),
        name="start",
    )(stay_in_hbm(precond[0]), stay_in_hbm(right_side[0]))

    *lists, values, order_token = pl.pallas_call(
        functools.partial(order_kernel, group, owned, groups, parts, stages, bits),
        out_shape=[
            pltpu.SMEM((lists_total + 1, slots + UNROLL), jnp.int32),
            pltpu.SMEM((lists_total,), jnp.int32),
            pltpu.VMEM(block_values.shape[2:], block_values.dtype),
            token_type,
        ],
        in_specs=[in_smem()] + [in_hbm()] * 3,
        out_specs=[in_smem()] * 2 + [in_vmem()] * 2,
        scratch_shapes=[
            index_type, index_type,
            pltpu.SMEM((groups * parts,), jnp.int32), pltpu.SMEM((lists_total + 1,), jnp.int32),
            pltpu.SemaphoreType.DMA((3,)),
        ],
        compiler_params=params(),
        name="order",
    )(block_counts, *[stay_in_hbm(array) for array in (block_rows, block_cols, block_values[0, 0])])

    values, turn_token = pl.pallas_call(
        turn_kernel,
        out_shape=[pltpu.VMEM(values.shape, values.dtype), token_type],
        in_specs=[in_smem(), in_vmem()],
        out_specs=[in_vmem()] * 2,
        input_output_aliases={1: 0},
        compiler_params=params(),
        name="turn",
    )(lists[1], values)

    def cost(share):
        return pl.CostEstimate(
            flops=int(slots * share) * 2 * rhs * size * size,
            bytes_accessed=int(slots * share) * 2 * size * size, transcendentals=0)

    def field_scratch(pieces):
        return pltpu.VMEM((sum(piece.shape[0] for piece in pieces), rhs, size), jnp.bfloat16)

    def product_first(pieces, outs, ins, sent):
        return pl.pallas_call(
            functools.partial(first_kernel, len(pieces), len(outs) // 2, chips, bits),
            out_shape=[total_type] * CORES + [token_type],
            in_specs=[in_smem()] * 2 + [in_vmem()] * (1 + len(pieces) + len(outs) + len(ins) + len(sent)),
            out_specs=[in_vmem()] * (CORES + 1),
            compiler_params=params(),
            scratch_shapes=[field_scratch(pieces)],
            cost_estimate=cost(len(stages[0]) / groups / parts),
            name="stage0",
        )(*lists, values, *pieces, *outs, *ins, *sent)

    def product_stage(stage, pieces, totals):
        inputs = 3 + len(pieces)
        return pl.pallas_call(
            functools.partial(stage_kernel, stage, bits, len(pieces)),
            out_shape=[total_type] * CORES,
            in_specs=[in_smem()] * 2 + [in_vmem()] * (1 + len(pieces) + CORES),
            out_specs=[in_vmem()] * CORES,
            scratch_shapes=[field_scratch(pieces)],
            input_output_aliases={inputs + half: half for half in range(CORES)},
            compiler_params=params(),
            cost_estimate=cost(len(stages[stage]) / groups / parts),
            name="stage%d" % stage,
        )(*lists, values, *pieces, *totals)

    def product_last(half, pieces, total, *other):
        send_chips = chips - swapped_early(chips) if half else swapped_early(chips)
        return pl.pallas_call(
            functools.partial(last_kernel, final, half, bits, len(pieces), chips),
            out_shape=[total_type, jax.ShapeDtypeStruct((send_chips * owned, rhs, size), jnp.bfloat16)],
            in_specs=[in_smem()] * 2 + [in_vmem()] * (2 + len(pieces) + len(other)),
            out_specs=[in_vmem()] * 2,
            scratch_shapes=[field_scratch(pieces)],
            input_output_aliases={3 + len(pieces): 0},
            compiler_params=params(),
            cost_estimate=pl.CostEstimate(
                flops=LAST_FLOPS if half else 0, bytes_accessed=0, transcendentals=0),
            name="last%d" % half,
        )(*lists, values, *pieces, total, *other)

    def hold(piece, token):
        return pl.pallas_call(
            hold_kernel,
            out_shape=part_type,
            in_specs=[in_vmem()] * 2,
            out_specs=in_vmem(),
            input_output_aliases={0: 0},
            compiler_params=params(),
            name="hold",
        )(piece, token)

    early = swapped_early(chips)

    def combine_first(own, first):
        return pl.pallas_call(
            functools.partial(combine_first_kernel, chips),
            out_shape=[rounded_type] * early,
            in_specs=[in_vmem()] * 2,
            out_specs=[in_vmem()] * early,
            compiler_params=params(),
            name="combine0",
        )(own, first)

    def combine_rest(own, rest, left, sol):
        return pl.pallas_call(
            functools.partial(combine_rest_kernel, chips),
            out_shape=[field_type] + [rounded_type] * (chips - 1 - early),
            in_specs=[in_vmem()] * 4,
            out_specs=[in_vmem()] * (chips - early),
            compiler_params=params(),
            name="combine1",
        )(own, rest, left, sol)

    outs, ins, sent = [], [], []
    for step in range(ITERS):
        sets = gather(whole, rounded, groups)

        def stage_pieces(stage):
            return [sets[piece] for piece in stages[stage] if piece in sets]

        def forward(part, token=None):
            for index in range(1, groups // 2):
                if token is not None:
                    sets[index, part] = hold(sets[index, part], token)
                sets[groups // 2 + index, part] = lax.ppermute(sets[index, part], "col", neighbours(groups))

        if groups % 2 == 0:
            for part in range(parts - 1):
                forward(part, order_token if step == 0 else None)
        *totals, token = product_first(stage_pieces(0), outs, ins, sent)
        if groups % 2 == 0:
            forward(parts - 1, turn_token if step == 0 else token)

        for stage in range(1, final):
            totals = product_stage(stage, stage_pieces(stage), totals)
        other, out_first = product_last(0, stage_pieces(final), totals[0])
        own, out_rest = product_last(1, stage_pieces(final), totals[1], other)
        outgoing = [out_first, out_rest]
        incoming = [lax.ppermute(rows, "row", neighbours(row_devices)) for rows in outgoing]
        outs += outgoing
        ins += incoming
        first = combine_first(own, incoming[0])
        base, *rest = combine_rest(own, incoming[1], left, sol)
        sends = list(first) + rest
        sent += sends
        pieces = [
            lax.ppermute(send, "row", [
                (chip * CORES + core, partner(chip, shift, chips) * CORES + core)
                for chip in range(chips) for core in range(CORES)
            ])
            for shift, send in zip(swap_order(chips), sends)
        ]
        if step < ITERS - 1:
            sol, left, whole, *rounded = pl.pallas_call(
                functools.partial(apply_kernel, len(pieces)),
                out_shape=[field_type, field_type, rounded_type] + [part_type] * parts,
                in_specs=[in_vmem()] * (5 + len(pieces)),
                out_specs=[in_vmem()] * (3 + parts),
                compiler_params=params(),
                name="apply",
            )(high, low, left, sol, base, *pieces)
    return pl.pallas_call(
        functools.partial(finish_kernel, len(pieces)),
        out_shape=field_type,
        in_specs=[in_vmem()] * (4 + len(pieces)),
        out_specs=in_hbm(),
        scratch_shapes=[
            pltpu.VMEM((owned, rhs, size), jnp.float32),
            pltpu.SemaphoreType.DMA((2 if owned % 2 == 0 else 1,)),
        ],
        compiler_params=params(),
        name="finish",
    )(high, low, sol, base, *pieces)[None]


def solution(mesh):
    placed = (
        P("row", "col", None, None, None),
        P("row", "col", None),
        P("row", "col", None),
        P("row", "col"),
        P("col", "row", None, None),
        P("col", "row", None, None),
    )
    return jax.shard_map(
        per_device,
        mesh=mesh,
        in_specs=placed,
        out_specs=P("col", "row", None, None),
        check_vma=False,
    )
```

```python
import functools

import jax
import jax.numpy as jnp
from jax import lax
from jax.experimental import pallas as pl
from jax.experimental.pallas import tpu as pltpu
from jax.sharding import PartitionSpec as P

ITERS = 3
UNROLL = 16
LANES = 4
DEPTH = 6
HIDE_FLOPS = 20_000_000_000
CORES = 2
VMEM_LIMIT = 24 * 1024 * 1024

NT = (((1,), (1,)), ((), ()))
NN = (((1,), (0,)), ((), ()))


def in_vmem():
    return pl.BlockSpec(memory_space=pltpu.VMEM)


def in_hbm():
    return pl.BlockSpec(memory_space=pltpu.HBM)


def in_smem():
    return pl.BlockSpec(memory_space=pltpu.SMEM)


def stay_in_hbm(array):
    return pltpu.with_memory_space_constraint(array, pltpu.HBM)


def params():
    return pltpu.CompilerParams(vmem_limit_bytes=VMEM_LIMIT)


def split(value):
    high = value.astype(jnp.bfloat16)
    low = (value - high.astype(jnp.float32)).astype(jnp.bfloat16)
    return high, low


def times_block(field, high, low):
    field_high, field_low = split(field)
    rhs = field.shape[0]
    both = jnp.concatenate([field_high, field_low], axis=0)
    first = lax.dot_general(both, high, NT, preferred_element_type=jnp.float32)
    second = lax.dot_general(field_high, low, NT, preferred_element_type=jnp.float32)
    return first[:rhs] + (first[rhs:] + second)


def partner(chip, shift, chips):
    if chips & (chips - 1) == 0:
        return chip ^ shift
    return (chip + shift) % chips


def halves(value, size):
    if size & (size - 1) == 0:
        return lax.shift_right_logical(value, size.bit_length() - 1), value & (size - 1)
    return lax.div(value, size), lax.rem(value, size)


def relative(mine, source, groups):
    if groups % 2:
        away = mine - source
        return jnp.where(away < 0, away + groups, away)
    other = (mine ^ source) & 1
    away = (mine ^ other) - source
    away = jnp.where(away < 0, away + groups, away)
    return other * (groups // 2) + lax.shift_right_logical(away, 1)


def gather_stages(groups, parts):
    every = range(parts)
    own = [(0, part) for part in every]
    if groups % 2:
        return [own, [(index, part) for index in range(1, groups) for part in every]]
    pairs = groups // 2
    early = range(parts - 1)
    far, forwarded = range(1, pairs), range(pairs + 1, groups)
    stages = [
        own + [(index, part) for part in early for index in far],
        [(pairs, part) for part in every] + [(index, parts - 1) for index in far]
        + [(index, part) for part in early for index in forwarded],
        [(index, parts - 1) for index in forwarded],
    ]
    return [stage for stage in stages if stage]


def ring(groups, step):
    return [(c, (c + step) % groups) for c in range(groups)]


def gather(whole, rounded, groups):
    sets = {(0, 0): whole}
    if groups % 2:
        for step in range(1, groups):
            sets[step, 0] = lax.ppermute(whole, "col", ring(groups, step))
        return sets
    for part, piece in enumerate(rounded):
        for step in range(1, groups // 2):
            sets[step, part] = lax.ppermute(piece, "col", ring(groups, 2 * step))
    sets[groups // 2, 0] = lax.ppermute(whole, "col", neighbours(groups))
    return sets


def neighbours(count):
    return [(index, index ^ 1) for index in range(count)]


def hold_kernel(piece_ref, token_ref, out_ref):
    pass


def put_rounded(p, value, whole_ref, part_refs):
    part, inner = divmod(p, part_refs[0].shape[0])
    rounded = value.astype(jnp.bfloat16)
    whole_ref[p] = rounded
    part_refs[part][inner] = rounded


def start_kernel(precond_hbm, rhs_hbm, high_ref, low_ref, sol_ref, left_ref, whole_ref, *refs):
    part_refs, (precond_ref, sems) = refs[:-2], refs[-2:]
    owned = left_ref.shape[0]
    parts = sems.shape[0] - 1
    each = owned // parts
    loads = [pltpu.make_async_copy(rhs_hbm, left_ref, sems.at[parts])]
    for part in range(parts):
        at = pl.ds(part * each, each)
        loads.append(pltpu.make_async_copy(precond_hbm.at[at], precond_ref.at[at], sems.at[part]))
    for load in loads:
        load.start()
    loads[0].wait()
    for part in range(parts):
        loads[1 + part].wait()
        for p in range(part * each, (part + 1) * each):
            high, low = split(precond_ref[p])
            high_ref[p] = high
            low_ref[p] = low
            value = times_block(left_ref[p], high, low)
            sol_ref[p] = value
            put_rounded(p, value, whole_ref, part_refs)


def apply_kernel(part, parts, pieces, high_ref, low_ref, left_ref, sol_ref, base_ref, *refs):
    piece_refs, refs = refs[:pieces], refs[pieces:]
    earlier_refs, refs = refs[:-3 - (part == parts - 1)], refs[-3 - (part == parts - 1):]
    new_ref, new_left_ref, rounded_ref, *whole_refs = refs
    each = rounded_ref.shape[0]
    for whole_ref in whole_refs:
        for index, earlier_ref in enumerate(earlier_refs):
            whole_ref[pl.ds(index * each, each)] = earlier_ref[...]
    for inner in range(each):
        p = part * each + inner
        received = sum(piece_ref[p].astype(jnp.float32) for piece_ref in piece_refs)
        value = sol_ref[p] + times_block(base_ref[p] - received, high_ref[p], low_ref[p])
        new_ref[p] = value
        new_left_ref[p] = left_ref[p] - received
        for out_ref, at in [(rounded_ref, inner)] + [(whole_ref, p) for whole_ref in whole_refs]:
            out_ref[at] = value.astype(jnp.bfloat16)


def finish_kernel(pieces, high_ref, low_ref, sol_ref, base_ref, *refs):
    piece_refs, (out_hbm, value_ref, sems) = refs[:pieces], refs[pieces:]
    owned = sol_ref.shape[0]
    parts = sems.shape[0]
    each = owned // parts
    stores = []
    for part in range(parts):
        for p in range(part * each, (part + 1) * each):
            received = sum(piece_ref[p].astype(jnp.float32) for piece_ref in piece_refs)
            value_ref[p] = sol_ref[p] + times_block(base_ref[p] - received, high_ref[p], low_ref[p])
        at = pl.ds(part * each, each)
        stores.append(pltpu.make_async_copy(value_ref.at[at], out_hbm.at[at], sems.at[part]))
        stores[-1].start()
    for store in stores:
        store.wait()


def order_kernel(group, owned, groups, parts, stages, bits, count_ref, rows_hbm, cols_hbm, values_hbm,
                 list_out, total_out, values_out, token_ref, rows_ref, cols_ref, table_ref, total_ref, sems):
    token_ref[...] = jnp.zeros_like(token_ref)
    loads = [
        pltpu.make_async_copy(rows_hbm, rows_ref, sems.at[0]),
        pltpu.make_async_copy(cols_hbm, cols_ref, sems.at[1]),
        pltpu.make_async_copy(values_hbm, values_out, sems.at[2]),
    ]
    for load in loads:
        load.start()
    core = lax.axis_index("row") & (CORES - 1)
    mine = lax.axis_index("col")
    row_bits, col_bits = bits
    lists = len(stages) * CORES
    each = owned // parts
    trash = (group // CORES) << col_bits
    for index, stage in enumerate(stages):
        for place, (piece, part) in enumerate(stage):
            table_ref[piece * parts + part] = ((index * CORES) << col_bits) + place * each
    for index in range(lists + 1):
        total_ref[index] = 0
    for load in loads[:2]:
        load.wait()
    used = count_ref[0, 0]

    def place(chunk, carry):
        entries = []
        for lane in range(LANES):
            slot = chunk * LANES + lane
            owner, row_inner = halves(halves(rows_ref[0, 0, slot], group)[1], owned)
            source, rest = halves(cols_ref[0, 0, slot], group)
            half = 1 - ((owner & (CORES - 1)) ^ core)
            part, inner = halves(halves(rest, owned)[1], each)
            first, base = halves(table_ref[relative(mine, source, groups) * parts + part], 1 << col_bits)
            which = jnp.where(slot < used, first + half, lists)
            row = lax.shift_right_logical(owner, 1) * owned + row_inner
            col = base + inner
            entries.append((which, (((slot << row_bits) | row) << col_bits) | col))
        for which, entry in entries:
            at = total_ref[which]
            list_out[which, at] = entry
            total_ref[which] = at + 1
        return carry

    lax.fori_loop(0, lax.div(used + LANES - 1, LANES), place, 0)
    for index in range(lists):
        total_out[index] = total_ref[index]

    def close(index, carry):
        for extra in range(UNROLL):
            list_out[index, total_ref[index] + extra] = trash
        return carry

    lax.fori_loop(0, lists, close, 0)
    loads[2].wait()


def turn_kernel(total_ref, values_ref, base_ref, turned_ref, same_ref):
    used = sum(total_ref[index] for index in range(total_ref.shape[0]))

    def turn(chunk, carry):
        for lane in range(LANES):
            turned_ref[chunk * LANES + lane] = values_ref[chunk * LANES + lane].T
        return carry

    lax.fori_loop(0, lax.div(used + LANES - 1, LANES), turn, 0)


def add_products(which, bits, dims, list_ref, total_ref, values_ref, field_ref, total):
    row_bits, col_bits = bits

    def step(chunk, carry):
        terms = []

        def store(row, term):
            total[row] += term

        for lane in range(UNROLL):
            entry = list_ref[which, chunk * UNROLL + lane]
            col = entry & ((1 << col_bits) - 1)
            row = lax.shift_right_logical(entry, col_bits) & ((1 << row_bits) - 1)
            slot = lax.shift_right_logical(entry, col_bits + row_bits)
            term = lax.dot_general(field_ref[col], values_ref[slot], dims, preferred_element_type=jnp.float32)
            terms.append((row, term))
            if len(terms) > DEPTH:
                store(*terms.pop(0))
        for row, term in terms:
            store(row, term)
        return carry

    lax.fori_loop(0, lax.div(total_ref[which] + UNROLL - 1, UNROLL), step, 0)


def join(pieces, field):
    if len(pieces) == 1:
        return pieces[0]
    at = 0
    for piece in pieces:
        field[pl.ds(at, piece.shape[0])] = piece[...]
        at += piece.shape[0]
    return field


def swap_order(chips):
    return list(reversed(range(chips)))


def swapped_early(chips):
    return chips - 1


def swapped_rows(index, chips, owned, first_ref, rest_ref):
    early = swapped_early(chips)
    if index < early:
        return first_ref[pl.ds(index * owned, owned)]
    return rest_ref[pl.ds((index - early) * owned, owned)]


def first_kernel(pieces, steps, chips, bits, dims, list_ref, total_ref, values_ref, *refs):
    piece_refs, refs = refs[:pieces], refs[pieces:]
    out_refs, refs = refs[:2 * steps], refs[2 * steps:]
    in_refs, refs = refs[:2 * steps], refs[2 * steps:]
    sent_refs, totals, (token_ref, field) = refs[:-CORES - 2], refs[-CORES - 2:-2], refs[-2:]
    field_ref = join(piece_refs, field)
    token_ref[...] = jnp.zeros_like(token_ref)
    chip = lax.axis_index("row") // CORES
    for half, total in enumerate(totals):
        rows = total.shape[0] - 1
        owned = rows // chips
        if steps == 0:
            total[...] = jnp.zeros(total.shape, jnp.float32)
        else:
            for index, shift in enumerate(swap_order(chips)):
                swapped = in_refs if half else out_refs
                value = sum(
                    swapped_rows(index, chips, owned, *swapped[2 * step:2 * step + 2]).astype(jnp.float32)
                    for step in range(steps))
                if half == 0:
                    value = -value
                elif shift > 0:
                    for step in range(steps):
                        value -= sent_refs[step * (chips - 1) + index][...].astype(jnp.float32)
                total[pl.ds(partner(chip, shift, chips) * owned, owned)] = value
        add_products(half, bits, dims, list_ref, total_ref, values_ref, field_ref, total)


def stage_kernel(stage, bits, dims, pieces, list_ref, total_ref, values_ref, *refs):
    piece_refs, refs = refs[:pieces], refs[pieces + CORES:]
    totals, field = refs[:CORES], refs[-1]
    field_ref = join(piece_refs, field)
    for half, total in enumerate(totals):
        add_products(stage * CORES + half, bits, dims, list_ref, total_ref, values_ref, field_ref, total)


def last_kernel(stage, half, bits, dims, pieces, chips, list_ref, total_ref, values_ref, *refs):
    piece_refs, refs = refs[:pieces], refs[pieces + 1:]
    if half == 0:
        total, out_ref, field = refs
        other = total
    else:
        other, total, out_ref, field = refs
    field_ref = join(piece_refs, field)
    add_products(stage * CORES + half, bits, dims, list_ref, total_ref, values_ref, field_ref, total)
    chip = lax.axis_index("row") // CORES
    owned = (other.shape[0] - 1) // chips
    shifts, early = swap_order(chips), swapped_early(chips)
    for index, shift in enumerate(shifts[early:] if half else shifts[:early]):
        rows = other[pl.ds(partner(chip, shift, chips) * owned, owned)]
        out_ref[pl.ds(index * owned, owned)] = rows.astype(out_ref.dtype)


def chip_rows(index, chips, owned, own_ref, *other_refs):
    chip = lax.axis_index("row") // CORES
    at = pl.ds(partner(chip, swap_order(chips)[index], chips) * owned, owned)
    return own_ref[at] + swapped_rows(index, chips, owned, *other_refs).astype(jnp.float32)


def combine_first_kernel(chips, own_ref, first_ref, *send_refs):
    for index, send_ref in enumerate(send_refs):
        rows = chip_rows(index, chips, send_ref.shape[0], own_ref, first_ref, None)
        send_ref[...] = rows.astype(send_ref.dtype)


def combine_rest_kernel(chips, own_ref, rest_ref, left_ref, sol_ref, before_ref, base_ref, *send_refs):
    owned = base_ref.shape[0]
    for index, send_ref in enumerate(send_refs):
        rows = chip_rows(swapped_early(chips) + index, chips, owned, own_ref, None, rest_ref)
        send_ref[...] = rows.astype(send_ref.dtype)
    keep = chip_rows(chips - 1, chips, owned, own_ref, None, rest_ref)
    base_ref[...] = left_ref[...] - sol_ref[...] - keep


def per_device(block_values, block_rows, block_cols, block_counts, precond, right_side):
    owned, rhs, size = right_side.shape[1:]
    row_devices = lax.axis_size("row")
    groups = lax.axis_size("col")
    chips = row_devices // CORES
    group = owned * row_devices
    half_rows = chips * owned
    slots = block_values.shape[2]

    parts = 2 if owned % 2 == 0 else 1
    stages = gather_stages(groups, parts)
    final = len(stages) - 1
    lists_total = len(stages) * CORES
    widest = max(len(stage) for stage in stages) * owned // parts
    row_bits, col_bits = bits = half_rows.bit_length(), (widest - 1).bit_length()
    assert (slots - 1).bit_length() + row_bits + col_bits <= 31
    assert slots % LANES == 0

    field_type = jax.ShapeDtypeStruct((owned, rhs, size), jnp.float32)
    matrix_type = jax.ShapeDtypeStruct((owned, size, size), jnp.bfloat16)
    total_type = jax.ShapeDtypeStruct((half_rows + 1, rhs, size), jnp.float32)
    index_type = pltpu.SMEM(block_rows.shape, jnp.int32)
    token_type = jax.ShapeDtypeStruct((8, 128), jnp.float32)
    loads = next(count for count in (4, 2, 1) if owned % count == 0)
    rounded_type = jax.ShapeDtypeStruct((owned, rhs, size), jnp.bfloat16)
    part_type = jax.ShapeDtypeStruct((owned // parts, rhs, size), jnp.bfloat16)

    high, low, sol, left, whole, *rounded = pl.pallas_call(
        start_kernel,
        out_shape=[matrix_type] * 2 + [field_type] * 2 + [rounded_type] + [part_type] * parts,
        in_specs=[in_hbm()] * 2,
        out_specs=[in_vmem()] * (5 + parts),
        scratch_shapes=[
            pltpu.VMEM((owned, size, size), jnp.float32),
            pltpu.SemaphoreType.DMA((loads + 1,)),
        ],
        compiler_params=params(),
        name="start",
    )(stay_in_hbm(precond[0]), stay_in_hbm(right_side[0]))

    *lists, values, order_token = pl.pallas_call(
        functools.partial(order_kernel, group, owned, groups, parts, stages, bits),
        out_shape=[
            pltpu.SMEM((lists_total + 1, slots + UNROLL), jnp.int32),
            pltpu.SMEM((lists_total,), jnp.int32),
            pltpu.VMEM(block_values.shape[2:], block_values.dtype),
            token_type,
        ],
        in_specs=[in_smem()] + [in_hbm()] * 3,
        out_specs=[in_smem()] * 2 + [in_vmem()] * 2,
        scratch_shapes=[
            index_type, index_type,
            pltpu.SMEM((groups * parts,), jnp.int32), pltpu.SMEM((lists_total + 1,), jnp.int32),
            pltpu.SemaphoreType.DMA((3,)),
        ],
        compiler_params=params(),
        name="order",
    )(block_counts, *[stay_in_hbm(array) for array in (block_rows, block_cols, block_values[0, 0])])

    def turn(values, base):
        return pl.pallas_call(
            turn_kernel,
            out_shape=[pltpu.VMEM(values.shape, values.dtype), field_type],
            in_specs=[in_smem()] + [in_vmem()] * 2,
            out_specs=[in_vmem()] * 2,
            input_output_aliases={2: 1},
            compiler_params=params(),
            cost_estimate=pl.CostEstimate(flops=HIDE_FLOPS, bytes_accessed=0, transcendentals=0),
            name="turn",
        )(lists[1], values, base)

    def cost(share):
        return pl.CostEstimate(
            flops=int(slots * share) * 2 * rhs * size * size,
            bytes_accessed=int(slots * share) * 2 * size * size, transcendentals=0)

    def field_scratch(pieces):
        return pltpu.VMEM((sum(piece.shape[0] for piece in pieces), rhs, size), jnp.bfloat16)

    def product_first(values, dims, pieces, outs, ins, sent):
        return pl.pallas_call(
            functools.partial(first_kernel, len(pieces), len(outs) // 2, chips, bits, dims),
            out_shape=[total_type] * CORES + [token_type],
            in_specs=[in_smem()] * 2 + [in_vmem()] * (1 + len(pieces) + len(outs) + len(ins) + len(sent)),
            out_specs=[in_vmem()] * (CORES + 1),
            compiler_params=params(),
            scratch_shapes=[field_scratch(pieces)],
            cost_estimate=cost(len(stages[0]) / groups / parts),
            name="stage0",
        )(*lists, values, *pieces, *outs, *ins, *sent)

    def product_stage(values, dims, stage, pieces, totals):
        inputs = 3 + len(pieces)
        return pl.pallas_call(
            functools.partial(stage_kernel, stage, bits, dims, len(pieces)),
            out_shape=[total_type] * CORES,
            in_specs=[in_smem()] * 2 + [in_vmem()] * (1 + len(pieces) + CORES),
            out_specs=[in_vmem()] * CORES,
            scratch_shapes=[field_scratch(pieces)],
            input_output_aliases={inputs + half: half for half in range(CORES)},
            compiler_params=params(),
            cost_estimate=cost(len(stages[stage]) / groups / parts),
            name="stage%d" % stage,
        )(*lists, values, *pieces, *totals)

    def product_last(values, dims, half, pieces, total, *other):
        send_chips = chips - swapped_early(chips) if half else swapped_early(chips)
        return pl.pallas_call(
            functools.partial(last_kernel, final, half, bits, dims, len(pieces), chips),
            out_shape=[total_type, jax.ShapeDtypeStruct((send_chips * owned, rhs, size), jnp.bfloat16)],
            in_specs=[in_smem()] * 2 + [in_vmem()] * (2 + len(pieces) + len(other)),
            out_specs=[in_vmem()] * 2,
            scratch_shapes=[field_scratch(pieces)],
            input_output_aliases={3 + len(pieces): 0},
            compiler_params=params(),
            cost_estimate=pl.CostEstimate(
                flops=HIDE_FLOPS if half else 0, bytes_accessed=0, transcendentals=0),
            name="last%d" % half,
        )(*lists, values, *pieces, total, *other)

    def hold(piece, token):
        return pl.pallas_call(
            hold_kernel,
            out_shape=part_type,
            in_specs=[in_vmem()] * 2,
            out_specs=in_vmem(),
            input_output_aliases={0: 0},
            compiler_params=params(),
            name="hold",
        )(piece, token)

    early = swapped_early(chips)

    def combine_first(own, first):
        return pl.pallas_call(
            functools.partial(combine_first_kernel, chips),
            out_shape=[rounded_type] * early,
            in_specs=[in_vmem()] * 2,
            out_specs=[in_vmem()] * early,
            compiler_params=params(),
            name="combine0",
        )(own, first)

    def combine_rest(own, rest, left, sol, before):
        return pl.pallas_call(
            functools.partial(combine_rest_kernel, chips),
            out_shape=[field_type] + [rounded_type] * (chips - 1 - early),
            in_specs=[in_vmem()] * 5,
            out_specs=[in_vmem()] * (chips - early),
            compiler_params=params(),
            name="combine1",
        )(own, rest, left, sol, before)

    def apply(part, sol, left, base, pieces, earlier):
        last = part == parts - 1
        return pl.pallas_call(
            functools.partial(apply_kernel, part, parts, len(pieces)),
            out_shape=[field_type, field_type, part_type] + [rounded_type] * last,
            in_specs=[in_vmem()] * (5 + len(pieces) + len(earlier)),
            out_specs=[in_vmem()] * (3 + last),
            input_output_aliases={2: 1, 3: 0},
            compiler_params=params(),
            cost_estimate=pl.CostEstimate(flops=HIDE_FLOPS, bytes_accessed=0, transcendentals=0),
            name="apply%d" % part,
        )(high, low, left, sol, base, *pieces, *earlier)

    blocks = values, NT
    outs, ins, sent = [], [], []
    for step in range(ITERS):
        sets = gather(whole, rounded, groups)

        def stage_pieces(stage):
            return [sets[piece] for piece in stages[stage] if piece in sets]

        def forward(part, token=None):
            for index in range(1, groups // 2):
                if token is not None:
                    sets[index, part] = hold(sets[index, part], token)
                sets[groups // 2 + index, part] = lax.ppermute(sets[index, part], "col", neighbours(groups))

        if groups % 2 == 0:
            for part in range(parts - 1):
                forward(part, order_token if step == 0 else None)
        *totals, token = product_first(*blocks, stage_pieces(0), outs, ins, sent)
        if groups % 2 == 0:
            forward(parts - 1, order_token if step == 0 else token)

        for stage in range(1, final):
            totals = product_stage(*blocks, stage, stage_pieces(stage), totals)
        other, out_first = product_last(*blocks, 0, stage_pieces(final), totals[0])
        own, out_rest = product_last(*blocks, 1, stage_pieces(final), totals[1], other)
        outgoing = [out_first, out_rest]
        incoming = [lax.ppermute(rows, "row", neighbours(row_devices)) for rows in outgoing]
        outs += outgoing
        ins += incoming
        first = combine_first(own, incoming[0])
        base, *rest = combine_rest(own, incoming[1], left, sol, first[-1])
        sends = list(first) + rest
        sent += sends
        pieces = [
            lax.ppermute(send, "row", [
                (chip * CORES + core, partner(chip, shift, chips) * CORES + core)
                for chip in range(chips) for core in range(CORES)
            ])
            for shift, send in zip(swap_order(chips), sends)
        ]
        if step == 0:
            turned, base = turn(values, base)
            blocks = turned, NN
        if step < ITERS - 1:
            rounded = []
            for part in range(parts):
                sol, left, new, *done = apply(part, sol, left, base, pieces, rounded if part == parts - 1 else [])
                rounded.append(new)
            whole, = done
    return pl.pallas_call(
        functools.partial(finish_kernel, len(pieces)),
        out_shape=field_type,
        in_specs=[in_vmem()] * (4 + len(pieces)),
        out_specs=in_hbm(),
        scratch_shapes=[
            pltpu.VMEM((owned, rhs, size), jnp.float32),
            pltpu.SemaphoreType.DMA((2 if owned % 2 == 0 else 1,)),
        ],
        compiler_params=params(),
        name="finish",
    )(high, low, sol, base, *pieces)[None]


def solution(mesh):
    placed = (
        P("row", "col", None, None, None),
        P("row", "col", None),
        P("row", "col", None),
        P("row", "col"),
        P("col", "row", None, None),
        P("col", "row", None, None),
    )
    return jax.shard_map(
        per_device,
        mesh=mesh,
        in_specs=placed,
        out_specs=P("col", "row", None, None),
        check_vma=False,
    )
```

```python
import functools

import jax
import jax.numpy as jnp
from jax import lax
from jax.experimental import pallas as pl
from jax.experimental.pallas import tpu as pltpu
from jax.sharding import PartitionSpec as P

ITERS = 3
UNROLL = 16
LANES = 4
DEPTH = 6
HIDE_FLOPS = 20_000_000_000
CORES = 2
VMEM_LIMIT = 24 * 1024 * 1024

NT = (((1,), (1,)), ((), ()))
NN = (((1,), (0,)), ((), ()))


def in_vmem():
    return pl.BlockSpec(memory_space=pltpu.VMEM)


def in_hbm():
    return pl.BlockSpec(memory_space=pltpu.HBM)


def in_smem():
    return pl.BlockSpec(memory_space=pltpu.SMEM)


def stay_in_hbm(array):
    return pltpu.with_memory_space_constraint(array, pltpu.HBM)


def params():
    return pltpu.CompilerParams(vmem_limit_bytes=VMEM_LIMIT)


def split(value):
    high = value.astype(jnp.bfloat16)
    low = (value - high.astype(jnp.float32)).astype(jnp.bfloat16)
    return high, low


def times_block(field, high, low):
    field_high, field_low = split(field)
    rhs = field.shape[0]
    both = jnp.concatenate([field_high, field_low], axis=0)
    first = lax.dot_general(both, high, NT, preferred_element_type=jnp.float32)
    second = lax.dot_general(field_high, low, NT, preferred_element_type=jnp.float32)
    return first[:rhs] + (first[rhs:] + second)


def partner(chip, shift, chips):
    if chips & (chips - 1) == 0:
        return chip ^ shift
    return (chip + shift) % chips


def halves(value, size):
    if size & (size - 1) == 0:
        return lax.shift_right_logical(value, size.bit_length() - 1), value & (size - 1)
    return lax.div(value, size), lax.rem(value, size)


def relative(mine, source, groups):
    if groups % 2:
        away = mine - source
        return jnp.where(away < 0, away + groups, away)
    other = (mine ^ source) & 1
    away = (mine ^ other) - source
    away = jnp.where(away < 0, away + groups, away)
    return other * (groups // 2) + lax.shift_right_logical(away, 1)


def gather_stages(groups, parts):
    every = range(parts)
    own = [(0, part) for part in every]
    if groups % 2:
        return [own, [(index, part) for index in range(1, groups) for part in every]]
    pairs = groups // 2
    early = range(parts - 1)
    far, forwarded = range(1, pairs), range(pairs + 1, groups)
    stages = [
        own + [(index, part) for part in early for index in far],
        [(pairs, part) for part in every] + [(index, parts - 1) for index in far]
        + [(index, part) for part in early for index in forwarded],
        [(index, parts - 1) for index in forwarded],
    ]
    return [stage for stage in stages if stage]


def ring(groups, step):
    return [(c, (c + step) % groups) for c in range(groups)]


def gather(whole, rounded, groups):
    sets = {(0, 0): whole}
    if groups % 2:
        for step in range(1, groups):
            sets[step, 0] = lax.ppermute(whole, "col", ring(groups, step))
        return sets
    for part, piece in enumerate(rounded):
        for step in range(1, groups // 2):
            sets[step, part] = lax.ppermute(piece, "col", ring(groups, 2 * step))
    sets[groups // 2, 0] = lax.ppermute(whole, "col", neighbours(groups))
    return sets


def neighbours(count):
    return [(index, index ^ 1) for index in range(count)]


def hold_kernel(piece_ref, token_ref, out_ref):
    pass


def part_sizes(owned):
    if owned % 8 == 0:
        return [owned - 3 * owned // 8, 3 * owned // 8]
    return [owned]


def part_starts(sizes):
    return [sum(sizes[:part]) for part in range(len(sizes))]


def put_rounded(p, value, whole_ref, part_refs):
    first = part_refs[0].shape[0]
    part, inner = (0, p) if p < first else (1, p - first)
    rounded = value.astype(jnp.bfloat16)
    whole_ref[p] = rounded
    part_refs[part][inner] = rounded


def start_kernel(precond_hbm, rhs_hbm, high_ref, low_ref, sol_ref, left_ref, whole_ref, *refs):
    part_refs, (precond_ref, sems) = refs[:-2], refs[-2:]
    owned = left_ref.shape[0]
    parts = sems.shape[0] - 1
    each = owned // parts
    loads = [pltpu.make_async_copy(rhs_hbm, left_ref, sems.at[parts])]
    for part in range(parts):
        at = pl.ds(part * each, each)
        loads.append(pltpu.make_async_copy(precond_hbm.at[at], precond_ref.at[at], sems.at[part]))
    for load in loads:
        load.start()
    loads[0].wait()
    for part in range(parts):
        loads[1 + part].wait()
        for p in range(part * each, (part + 1) * each):
            high, low = split(precond_ref[p])
            high_ref[p] = high
            low_ref[p] = low
            value = times_block(left_ref[p], high, low)
            sol_ref[p] = value
            put_rounded(p, value, whole_ref, part_refs)


def apply_kernel(start, pieces, earlier, high_ref, low_ref, left_ref, sol_ref, base_ref, *refs):
    piece_refs, refs = refs[:pieces], refs[pieces:]
    earlier_refs, (new_ref, new_left_ref, rounded_ref, *whole_refs) = refs[:earlier], refs[earlier:]
    for whole_ref in whole_refs:
        at = 0
        for earlier_ref in earlier_refs:
            whole_ref[pl.ds(at, earlier_ref.shape[0])] = earlier_ref[...]
            at += earlier_ref.shape[0]
    for inner in range(rounded_ref.shape[0]):
        p = start + inner
        received = sum(piece_ref[p].astype(jnp.float32) for piece_ref in piece_refs)
        value = sol_ref[p] + times_block(base_ref[p] - received, high_ref[p], low_ref[p])
        new_ref[p] = value
        new_left_ref[p] = left_ref[p] - received
        for out_ref, at in [(rounded_ref, inner)] + [(whole_ref, p) for whole_ref in whole_refs]:
            out_ref[at] = value.astype(jnp.bfloat16)


def finish_kernel(pieces, high_ref, low_ref, sol_ref, base_ref, *refs):
    piece_refs, (out_hbm, value_ref, sems) = refs[:pieces], refs[pieces:]
    owned = sol_ref.shape[0]
    parts = sems.shape[0]
    each = owned // parts
    stores = []
    for part in range(parts):
        for p in range(part * each, (part + 1) * each):
            received = sum(piece_ref[p].astype(jnp.float32) for piece_ref in piece_refs)
            value_ref[p] = sol_ref[p] + times_block(base_ref[p] - received, high_ref[p], low_ref[p])
        at = pl.ds(part * each, each)
        stores.append(pltpu.make_async_copy(value_ref.at[at], out_hbm.at[at], sems.at[part]))
        stores[-1].start()
    for store in stores:
        store.wait()


def order_kernel(group, owned, groups, parts, stages, bits, count_ref, rows_hbm, cols_hbm, values_hbm,
                 list_out, total_out, values_out, token_ref, rows_ref, cols_ref, table_ref, total_ref, sems):
    token_ref[...] = jnp.zeros_like(token_ref)
    loads = [
        pltpu.make_async_copy(rows_hbm, rows_ref, sems.at[0]),
        pltpu.make_async_copy(cols_hbm, cols_ref, sems.at[1]),
        pltpu.make_async_copy(values_hbm, values_out, sems.at[2]),
    ]
    for load in loads:
        load.start()
    core = lax.axis_index("row") & (CORES - 1)
    mine = lax.axis_index("col")
    row_bits, col_bits = bits
    lists = len(stages) * CORES
    sizes = part_sizes(owned)
    trash = (group // CORES) << col_bits
    for index, stage in enumerate(stages):
        base = 0
        for piece, part in stage:
            table_ref[piece * parts + part] = ((index * CORES) << col_bits) + base
            base += sizes[part]
    for index in range(lists + 1):
        total_ref[index] = 0
    for load in loads[:2]:
        load.wait()
    used = count_ref[0, 0]

    def place(chunk, carry):
        entries = []
        for lane in range(LANES):
            slot = chunk * LANES + lane
            owner, row_inner = halves(halves(rows_ref[0, 0, slot], group)[1], owned)
            source, rest = halves(cols_ref[0, 0, slot], group)
            half = 1 - ((owner & (CORES - 1)) ^ core)
            inner = halves(rest, owned)[1]
            part = jnp.where(inner >= sizes[0], parts - 1, 0)
            inner = jnp.where(inner >= sizes[0], inner - sizes[0], inner)
            first, base = halves(table_ref[relative(mine, source, groups) * parts + part], 1 << col_bits)
            which = jnp.where(slot < used, first + half, lists)
            row = lax.shift_right_logical(owner, 1) * owned + row_inner
            col = base + inner
            entries.append((which, (((slot << row_bits) | row) << col_bits) | col))
        for which, entry in entries:
            at = total_ref[which]
            list_out[which, at] = entry
            total_ref[which] = at + 1
        return carry

    lax.fori_loop(0, lax.div(used + LANES - 1, LANES), place, 0)
    for index in range(lists):
        total_out[index] = total_ref[index]

    def close(index, carry):
        for extra in range(UNROLL):
            list_out[index, total_ref[index] + extra] = trash
        return carry

    lax.fori_loop(0, lists, close, 0)
    loads[2].wait()


def turn_kernel(total_ref, values_ref, base_ref, turned_ref, same_ref):
    used = sum(total_ref[index] for index in range(total_ref.shape[0]))

    def turn(chunk, carry):
        for lane in range(LANES):
            turned_ref[chunk * LANES + lane] = values_ref[chunk * LANES + lane].T
        return carry

    lax.fori_loop(0, lax.div(used + LANES - 1, LANES), turn, 0)


def add_products(which, bits, dims, list_ref, total_ref, values_ref, field_ref, total):
    row_bits, col_bits = bits

    def step(chunk, carry):
        terms = []

        def store(row, term):
            total[row] += term

        for lane in range(UNROLL):
            entry = list_ref[which, chunk * UNROLL + lane]
            col = entry & ((1 << col_bits) - 1)
            row = lax.shift_right_logical(entry, col_bits) & ((1 << row_bits) - 1)
            slot = lax.shift_right_logical(entry, col_bits + row_bits)
            term = lax.dot_general(field_ref[col], values_ref[slot], dims, preferred_element_type=jnp.float32)
            terms.append((row, term))
            if len(terms) > DEPTH:
                store(*terms.pop(0))
        for row, term in terms:
            store(row, term)
        return carry

    lax.fori_loop(0, lax.div(total_ref[which] + UNROLL - 1, UNROLL), step, 0)


def join(pieces, field):
    if len(pieces) == 1:
        return pieces[0]
    at = 0
    for piece in pieces:
        field[pl.ds(at, piece.shape[0])] = piece[...]
        at += piece.shape[0]
    return field


def swap_order(chips):
    return list(reversed(range(chips)))


def swapped_early(chips):
    return chips - 1


def swapped_rows(index, chips, owned, first_ref, rest_ref):
    early = swapped_early(chips)
    if index < early:
        return first_ref[pl.ds(index * owned, owned)]
    return rest_ref[pl.ds((index - early) * owned, owned)]


def first_kernel(pieces, steps, chips, bits, dims, list_ref, total_ref, values_ref, *refs):
    piece_refs, refs = refs[:pieces], refs[pieces:]
    out_refs, refs = refs[:2 * steps], refs[2 * steps:]
    in_refs, refs = refs[:2 * steps], refs[2 * steps:]
    sent_refs, totals, (token_ref, field) = refs[:-CORES - 2], refs[-CORES - 2:-2], refs[-2:]
    field_ref = join(piece_refs, field)
    token_ref[...] = jnp.zeros_like(token_ref)
    chip = lax.axis_index("row") // CORES
    for half, total in enumerate(totals):
        rows = total.shape[0] - 1
        owned = rows // chips
        if steps == 0:
            total[...] = jnp.zeros(total.shape, jnp.float32)
        else:
            for index, shift in enumerate(swap_order(chips)):
                swapped = in_refs if half else out_refs
                value = sum(
                    swapped_rows(index, chips, owned, *swapped[2 * step:2 * step + 2]).astype(jnp.float32)
                    for step in range(steps))
                if half == 0:
                    value = -value
                elif shift > 0:
                    for step in range(steps):
                        value -= sent_refs[step * (chips - 1) + index][...].astype(jnp.float32)
                total[pl.ds(partner(chip, shift, chips) * owned, owned)] = value
        add_products(half, bits, dims, list_ref, total_ref, values_ref, field_ref, total)


def stage_kernel(stage, bits, dims, pieces, list_ref, total_ref, values_ref, *refs):
    piece_refs, refs = refs[:pieces], refs[pieces + CORES:]
    totals, field = refs[:CORES], refs[-1]
    field_ref = join(piece_refs, field)
    for half, total in enumerate(totals):
        add_products(stage * CORES + half, bits, dims, list_ref, total_ref, values_ref, field_ref, total)


def last_kernel(stage, half, bits, dims, pieces, chips, list_ref, total_ref, values_ref, *refs):
    piece_refs, refs = refs[:pieces], refs[pieces + 1:]
    if half == 0:
        total, out_ref, field = refs
        other = total
    else:
        other, total, out_ref, field = refs
    field_ref = join(piece_refs, field)
    add_products(stage * CORES + half, bits, dims, list_ref, total_ref, values_ref, field_ref, total)
    chip = lax.axis_index("row") // CORES
    owned = (other.shape[0] - 1) // chips
    shifts, early = swap_order(chips), swapped_early(chips)
    for index, shift in enumerate(shifts[early:] if half else shifts[:early]):
        rows = other[pl.ds(partner(chip, shift, chips) * owned, owned)]
        out_ref[pl.ds(index * owned, owned)] = rows.astype(out_ref.dtype)


def chip_rows(index, chips, owned, own_ref, *other_refs):
    chip = lax.axis_index("row") // CORES
    at = pl.ds(partner(chip, swap_order(chips)[index], chips) * owned, owned)
    return own_ref[at] + swapped_rows(index, chips, owned, *other_refs).astype(jnp.float32)


def combine_first_kernel(chips, own_ref, first_ref, *send_refs):
    for index, send_ref in enumerate(send_refs):
        rows = chip_rows(index, chips, send_ref.shape[0], own_ref, first_ref, None)
        send_ref[...] = rows.astype(send_ref.dtype)


def combine_rest_kernel(chips, own_ref, rest_ref, left_ref, sol_ref, before_ref, base_ref, *send_refs):
    owned = base_ref.shape[0]
    for index, send_ref in enumerate(send_refs):
        rows = chip_rows(swapped_early(chips) + index, chips, owned, own_ref, None, rest_ref)
        send_ref[...] = rows.astype(send_ref.dtype)
    keep = chip_rows(chips - 1, chips, owned, own_ref, None, rest_ref)
    base_ref[...] = left_ref[...] - sol_ref[...] - keep


def per_device(block_values, block_rows, block_cols, block_counts, precond, right_side):
    owned, rhs, size = right_side.shape[1:]
    row_devices = lax.axis_size("row")
    groups = lax.axis_size("col")
    chips = row_devices // CORES
    group = owned * row_devices
    half_rows = chips * owned
    slots = block_values.shape[2]

    sizes = part_sizes(owned)
    parts = len(sizes)
    stages = gather_stages(groups, parts)
    final = len(stages) - 1
    lists_total = len(stages) * CORES
    widest = max(sum(sizes[part] for _, part in stage) for stage in stages)
    row_bits, col_bits = bits = half_rows.bit_length(), (widest - 1).bit_length()
    assert (slots - 1).bit_length() + row_bits + col_bits <= 31
    assert slots % LANES == 0

    field_type = jax.ShapeDtypeStruct((owned, rhs, size), jnp.float32)
    matrix_type = jax.ShapeDtypeStruct((owned, size, size), jnp.bfloat16)
    total_type = jax.ShapeDtypeStruct((half_rows + 1, rhs, size), jnp.float32)
    index_type = pltpu.SMEM(block_rows.shape, jnp.int32)
    token_type = jax.ShapeDtypeStruct((8, 128), jnp.float32)
    loads = next(count for count in (4, 2, 1) if owned % count == 0)
    rounded_type = jax.ShapeDtypeStruct((owned, rhs, size), jnp.bfloat16)
    part_types = [jax.ShapeDtypeStruct((part, rhs, size), jnp.bfloat16) for part in sizes]

    high, low, sol, left, whole, *rounded = pl.pallas_call(
        start_kernel,
        out_shape=[matrix_type] * 2 + [field_type] * 2 + [rounded_type] + part_types,
        in_specs=[in_hbm()] * 2,
        out_specs=[in_vmem()] * (5 + parts),
        scratch_shapes=[
            pltpu.VMEM((owned, size, size), jnp.float32),
            pltpu.SemaphoreType.DMA((loads + 1,)),
        ],
        compiler_params=params(),
        name="start",
    )(stay_in_hbm(precond[0]), stay_in_hbm(right_side[0]))

    *lists, values, order_token = pl.pallas_call(
        functools.partial(order_kernel, group, owned, groups, parts, stages, bits),
        out_shape=[
            pltpu.SMEM((lists_total + 1, slots + UNROLL), jnp.int32),
            pltpu.SMEM((lists_total,), jnp.int32),
            pltpu.VMEM(block_values.shape[2:], block_values.dtype),
            token_type,
        ],
        in_specs=[in_smem()] + [in_hbm()] * 3,
        out_specs=[in_smem()] * 2 + [in_vmem()] * 2,
        scratch_shapes=[
            index_type, index_type,
            pltpu.SMEM((groups * parts,), jnp.int32), pltpu.SMEM((lists_total + 1,), jnp.int32),
            pltpu.SemaphoreType.DMA((3,)),
        ],
        compiler_params=params(),
        name="order",
    )(block_counts, *[stay_in_hbm(array) for array in (block_rows, block_cols, block_values[0, 0])])

    def turn(values, base):
        return pl.pallas_call(
            turn_kernel,
            out_shape=[pltpu.VMEM(values.shape, values.dtype), field_type],
            in_specs=[in_smem()] + [in_vmem()] * 2,
            out_specs=[in_vmem()] * 2,
            input_output_aliases={2: 1},
            compiler_params=params(),
            cost_estimate=pl.CostEstimate(flops=HIDE_FLOPS, bytes_accessed=0, transcendentals=0),
            name="turn",
        )(lists[1], values, base)

    def cost(share):
        return pl.CostEstimate(
            flops=int(slots * share) * 2 * rhs * size * size,
            bytes_accessed=int(slots * share) * 2 * size * size, transcendentals=0)

    def field_scratch(pieces):
        return pltpu.VMEM((sum(piece.shape[0] for piece in pieces), rhs, size), jnp.bfloat16)

    def product_first(values, dims, pieces, outs, ins, sent):
        return pl.pallas_call(
            functools.partial(first_kernel, len(pieces), len(outs) // 2, chips, bits, dims),
            out_shape=[total_type] * CORES + [token_type],
            in_specs=[in_smem()] * 2 + [in_vmem()] * (1 + len(pieces) + len(outs) + len(ins) + len(sent)),
            out_specs=[in_vmem()] * (CORES + 1),
            compiler_params=params(),
            scratch_shapes=[field_scratch(pieces)],
            cost_estimate=cost(len(stages[0]) / groups / parts),
            name="stage0",
        )(*lists, values, *pieces, *outs, *ins, *sent)

    def product_stage(values, dims, stage, pieces, totals):
        inputs = 3 + len(pieces)
        return pl.pallas_call(
            functools.partial(stage_kernel, stage, bits, dims, len(pieces)),
            out_shape=[total_type] * CORES,
            in_specs=[in_smem()] * 2 + [in_vmem()] * (1 + len(pieces) + CORES),
            out_specs=[in_vmem()] * CORES,
            scratch_shapes=[field_scratch(pieces)],
            input_output_aliases={inputs + half: half for half in range(CORES)},
            compiler_params=params(),
            cost_estimate=cost(len(stages[stage]) / groups / parts),
            name="stage%d" % stage,
        )(*lists, values, *pieces, *totals)

    def product_last(values, dims, half, pieces, total, *other):
        send_chips = chips - swapped_early(chips) if half else swapped_early(chips)
        return pl.pallas_call(
            functools.partial(last_kernel, final, half, bits, dims, len(pieces), chips),
            out_shape=[total_type, jax.ShapeDtypeStruct((send_chips * owned, rhs, size), jnp.bfloat16)],
            in_specs=[in_smem()] * 2 + [in_vmem()] * (2 + len(pieces) + len(other)),
            out_specs=[in_vmem()] * 2,
            scratch_shapes=[field_scratch(pieces)],
            input_output_aliases={3 + len(pieces): 0},
            compiler_params=params(),
            cost_estimate=pl.CostEstimate(
                flops=HIDE_FLOPS if half else 0, bytes_accessed=0, transcendentals=0),
            name="last%d" % half,
        )(*lists, values, *pieces, total, *other)

    def hold(piece, token):
        return pl.pallas_call(
            hold_kernel,
            out_shape=jax.ShapeDtypeStruct(piece.shape, piece.dtype),
            in_specs=[in_vmem()] * 2,
            out_specs=in_vmem(),
            input_output_aliases={0: 0},
            compiler_params=params(),
            name="hold",
        )(piece, token)

    early = swapped_early(chips)

    def combine_first(own, first):
        return pl.pallas_call(
            functools.partial(combine_first_kernel, chips),
            out_shape=[rounded_type] * early,
            in_specs=[in_vmem()] * 2,
            out_specs=[in_vmem()] * early,
            compiler_params=params(),
            name="combine0",
        )(own, first)

    def combine_rest(own, rest, left, sol, before):
        return pl.pallas_call(
            functools.partial(combine_rest_kernel, chips),
            out_shape=[field_type] + [rounded_type] * (chips - 1 - early),
            in_specs=[in_vmem()] * 5,
            out_specs=[in_vmem()] * (chips - early),
            compiler_params=params(),
            name="combine1",
        )(own, rest, left, sol, before)

    def apply(part, sol, left, base, pieces, earlier):
        last = part == parts - 1
        return pl.pallas_call(
            functools.partial(apply_kernel, part_starts(sizes)[part], len(pieces), len(earlier)),
            out_shape=[field_type, field_type, part_types[part]] + [rounded_type] * last,
            in_specs=[in_vmem()] * (5 + len(pieces) + len(earlier)),
            out_specs=[in_vmem()] * (3 + last),
            input_output_aliases={2: 1, 3: 0},
            compiler_params=params(),
            cost_estimate=pl.CostEstimate(flops=HIDE_FLOPS, bytes_accessed=0, transcendentals=0),
            name="apply%d" % part,
        )(high, low, left, sol, base, *pieces, *earlier)

    blocks = values, NT
    outs, ins, sent = [], [], []
    for step in range(ITERS):
        sets = gather(whole, rounded, groups)

        def stage_pieces(stage):
            return [sets[piece] for piece in stages[stage] if piece in sets]

        def forward(part, token=None):
            for index in range(1, groups // 2):
                if token is not None:
                    sets[index, part] = hold(sets[index, part], token)
                sets[groups // 2 + index, part] = lax.ppermute(sets[index, part], "col", neighbours(groups))

        if groups % 2 == 0:
            for part in range(parts - 1):
                forward(part, order_token if step == 0 else None)
        *totals, token = product_first(*blocks, stage_pieces(0), outs, ins, sent)
        if groups % 2 == 0:
            forward(parts - 1, order_token if step == 0 else token)

        for stage in range(1, final):
            totals = product_stage(*blocks, stage, stage_pieces(stage), totals)
        other, out_first = product_last(*blocks, 0, stage_pieces(final), totals[0])
        own, out_rest = product_last(*blocks, 1, stage_pieces(final), totals[1], other)
        outgoing = [out_first, out_rest]
        incoming = [lax.ppermute(rows, "row", neighbours(row_devices)) for rows in outgoing]
        outs += outgoing
        ins += incoming
        first = combine_first(own, incoming[0])
        base, *rest = combine_rest(own, incoming[1], left, sol, first[-1])
        sends = list(first) + rest
        sent += sends
        pieces = [
            lax.ppermute(send, "row", [
                (chip * CORES + core, partner(chip, shift, chips) * CORES + core)
                for chip in range(chips) for core in range(CORES)
            ])
            for shift, send in zip(swap_order(chips), sends)
        ]
        if step == 0:
            turned, base = turn(values, base)
            blocks = turned, NN
        if step < ITERS - 1:
            rounded = []
            for part in range(parts):
                sol, left, new, *done = apply(part, sol, left, base, pieces, rounded if part == parts - 1 else [])
                rounded.append(new)
            whole, = done
    return pl.pallas_call(
        functools.partial(finish_kernel, len(pieces)),
        out_shape=field_type,
        in_specs=[in_vmem()] * (4 + len(pieces)),
        out_specs=in_hbm(),
        scratch_shapes=[
            pltpu.VMEM((owned, rhs, size), jnp.float32),
            pltpu.SemaphoreType.DMA((2 if owned % 2 == 0 else 1,)),
        ],
        compiler_params=params(),
        name="finish",
    )(high, low, sol, base, *pieces)[None]


def solution(mesh):
    placed = (
        P("row", "col", None, None, None),
        P("row", "col", None),
        P("row", "col", None),
        P("row", "col"),
        P("col", "row", None, None),
        P("col", "row", None, None),
    )
    return jax.shard_map(
        per_device,
        mesh=mesh,
        in_specs=placed,
        out_specs=P("col", "row", None, None),
        check_vma=False,
    )
```

```python
import functools

import jax
import jax.numpy as jnp
from jax import lax
from jax.experimental import pallas as pl
from jax.experimental.pallas import tpu as pltpu
from jax.sharding import PartitionSpec as P

ITERS = 3
UNROLL = 16
LANES = 4
DEPTH = 6
HIDE_FLOPS = 20_000_000_000
CORES = 2
VMEM_LIMIT = 24 * 1024 * 1024

NT = (((1,), (1,)), ((), ()))
NN = (((1,), (0,)), ((), ()))


def in_vmem():
    return pl.BlockSpec(memory_space=pltpu.VMEM)


def in_hbm():
    return pl.BlockSpec(memory_space=pltpu.HBM)


def in_smem():
    return pl.BlockSpec(memory_space=pltpu.SMEM)


def stay_in_hbm(array):
    return pltpu.with_memory_space_constraint(array, pltpu.HBM)


def params():
    return pltpu.CompilerParams(vmem_limit_bytes=VMEM_LIMIT)


def split(value):
    high = value.astype(jnp.bfloat16)
    low = (value - high.astype(jnp.float32)).astype(jnp.bfloat16)
    return high, low


def times_block(field, high, low):
    field_high, field_low = split(field)
    rhs = field.shape[0]
    both = jnp.concatenate([field_high, field_low], axis=0)
    first = lax.dot_general(both, high, NT, preferred_element_type=jnp.float32)
    second = lax.dot_general(field_high, low, NT, preferred_element_type=jnp.float32)
    return first[:rhs] + (first[rhs:] + second)


def partner(chip, shift, chips):
    if chips & (chips - 1) == 0:
        return chip ^ shift
    return (chip + shift) % chips


def halves(value, size):
    if size & (size - 1) == 0:
        return lax.shift_right_logical(value, size.bit_length() - 1), value & (size - 1)
    return lax.div(value, size), lax.rem(value, size)


def relative(mine, source, groups):
    if groups % 2:
        away = mine - source
        return jnp.where(away < 0, away + groups, away)
    other = (mine ^ source) & 1
    away = (mine ^ other) - source
    away = jnp.where(away < 0, away + groups, away)
    return other * (groups // 2) + lax.shift_right_logical(away, 1)


def gather_stages(groups, parts):
    every = range(parts)
    own = [(0, part) for part in every]
    if groups % 2:
        return [own, [(index, part) for index in range(1, groups) for part in every]]
    pairs = groups // 2
    early = range(parts - 1)
    far, forwarded = range(1, pairs), range(pairs + 1, groups)
    stages = [
        own + [(index, part) for part in early for index in far],
        [(pairs, part) for part in every] + [(index, parts - 1) for index in far]
        + [(index, part) for part in early for index in forwarded],
        [(index, parts - 1) for index in forwarded],
    ]
    return [stage for stage in stages if stage]


def ring(groups, step):
    return [(c, (c + step) % groups) for c in range(groups)]


def gather(whole, rounded, groups):
    sets = {(0, 0): whole}
    if groups % 2:
        for step in range(1, groups):
            sets[step, 0] = lax.ppermute(whole, "col", ring(groups, step))
        return sets
    for part, piece in enumerate(rounded):
        for step in range(1, groups // 2):
            sets[step, part] = lax.ppermute(piece, "col", ring(groups, 2 * step))
    sets[groups // 2, 0] = lax.ppermute(whole, "col", neighbours(groups))
    return sets


def neighbours(count):
    return [(index, index ^ 1) for index in range(count)]


def hold_kernel(piece_ref, token_ref, out_ref):
    pass


def put_rounded(p, value, whole_ref, part_refs):
    part, inner = divmod(p, part_refs[0].shape[0])
    rounded = value.astype(jnp.bfloat16)
    whole_ref[p] = rounded
    part_refs[part][inner] = rounded


def start_kernel(precond_hbm, rhs_hbm, high_ref, low_ref, sol_ref, left_ref, whole_ref, *refs):
    part_refs, (precond_ref, sems) = refs[:-2], refs[-2:]
    owned = left_ref.shape[0]
    parts = sems.shape[0] - 1
    each = owned // parts
    loads = [pltpu.make_async_copy(rhs_hbm, left_ref, sems.at[parts])]
    for part in range(parts):
        at = pl.ds(part * each, each)
        loads.append(pltpu.make_async_copy(precond_hbm.at[at], precond_ref.at[at], sems.at[part]))
    for load in loads:
        load.start()
    loads[0].wait()
    for part in range(parts):
        loads[1 + part].wait()
        for p in range(part * each, (part + 1) * each):
            high, low = split(precond_ref[p])
            high_ref[p] = high
            low_ref[p] = low
            value = times_block(left_ref[p], high, low)
            sol_ref[p] = value
            put_rounded(p, value, whole_ref, part_refs)


def apply_kernel(part, parts, pieces, high_ref, low_ref, left_ref, sol_ref, base_ref, *refs):
    piece_refs, refs = refs[:pieces], refs[pieces:]
    earlier_refs, refs = refs[:-3 - (part == parts - 1)], refs[-3 - (part == parts - 1):]
    new_ref, new_left_ref, rounded_ref, *whole_refs = refs
    each = rounded_ref.shape[0]
    for whole_ref in whole_refs:
        for index, earlier_ref in enumerate(earlier_refs):
            whole_ref[pl.ds(index * each, each)] = earlier_ref[...]
    for inner in range(each):
        p = part * each + inner
        received = sum(piece_ref[p].astype(jnp.float32) for piece_ref in piece_refs)
        value = sol_ref[p] + times_block(base_ref[p] - received, high_ref[p], low_ref[p])
        new_ref[p] = value
        new_left_ref[p] = left_ref[p] - received
        for out_ref, at in [(rounded_ref, inner)] + [(whole_ref, p) for whole_ref in whole_refs]:
            out_ref[at] = value.astype(jnp.bfloat16)


def finish_kernel(pieces, high_ref, low_ref, sol_ref, base_ref, *refs):
    piece_refs, (out_hbm, value_ref, sems) = refs[:pieces], refs[pieces:]
    owned = sol_ref.shape[0]
    parts = sems.shape[0]
    each = owned // parts
    stores = []
    for part in range(parts):
        for p in range(part * each, (part + 1) * each):
            received = sum(piece_ref[p].astype(jnp.float32) for piece_ref in piece_refs)
            value_ref[p] = sol_ref[p] + times_block(base_ref[p] - received, high_ref[p], low_ref[p])
        at = pl.ds(part * each, each)
        stores.append(pltpu.make_async_copy(value_ref.at[at], out_hbm.at[at], sems.at[part]))
        stores[-1].start()
    for store in stores:
        store.wait()


def order_kernel(group, owned, groups, parts, stages, bits, count_ref, rows_hbm, cols_hbm, values_hbm,
                 list_out, total_out, values_out, token_ref, rows_ref, cols_ref, first_ref, base_ref, total_ref,
                 sems):
    token_ref[...] = jnp.zeros_like(token_ref)
    loads = [
        pltpu.make_async_copy(rows_hbm, rows_ref, sems.at[0]),
        pltpu.make_async_copy(cols_hbm, cols_ref, sems.at[1]),
        pltpu.make_async_copy(values_hbm, values_out, sems.at[2]),
    ]
    for load in loads:
        load.start()
    other = 1 - (lax.axis_index("row") & (CORES - 1))
    mine = lax.axis_index("col")
    row_bits, col_bits = bits
    lists = len(stages) * CORES
    each = owned // parts
    trash = (group // CORES) << col_bits
    places = {
        piece: (index * CORES, place * each) for index, stage in enumerate(stages) for place, piece in enumerate(stage)
    }
    own_rows = lax.axis_index("row") * owned
    for source in range(groups):
        piece = relative(mine, source, groups)
        for part in range(parts):
            first, base = places[0, part]
            for index in range(1, groups):
                first = jnp.where(piece == index, places[index, part][0], first)
                base = jnp.where(piece == index, places[index, part][1], base)
            at = halves(source * group + own_rows + part * each, each)[0]
            first_ref[at] = first
            base_ref[at] = base
    for index in range(lists + 1):
        total_ref[index] = 0
    for load in loads[:2]:
        load.wait()
    used = count_ref[0, 0]

    def place(chunk, carry):
        entries = []
        for lane in range(LANES):
            slot = chunk * LANES + lane
            owner, row_inner = halves(halves(rows_ref[0, 0, slot], group)[1], owned)
            at, inner = halves(cols_ref[0, 0, slot], each)
            half = (owner & (CORES - 1)) ^ other
            which = jnp.where(slot < used, first_ref[at] + half, lists)
            row = lax.shift_right_logical(owner, 1) * owned + row_inner
            col = base_ref[at] + inner
            entries.append((which, (((slot << row_bits) | row) << col_bits) | col))
        for which, entry in entries:
            at = total_ref[which]
            list_out[which, at] = entry
            total_ref[which] = at + 1
        return carry

    lax.fori_loop(0, lax.div(used + LANES - 1, LANES), place, 0)
    for index in range(lists):
        total_out[index] = total_ref[index]

    def close(index, carry):
        for extra in range(UNROLL):
            list_out[index, total_ref[index] + extra] = trash
        return carry

    lax.fori_loop(0, lists, close, 0)
    loads[2].wait()


def turn_kernel(total_ref, values_ref, base_ref, turned_ref, same_ref):
    used = sum(total_ref[index] for index in range(total_ref.shape[0]))

    def turn(chunk, carry):
        for lane in range(LANES):
            turned_ref[chunk * LANES + lane] = values_ref[chunk * LANES + lane].T
        return carry

    lax.fori_loop(0, lax.div(used + LANES - 1, LANES), turn, 0)


def add_products(which, bits, dims, list_ref, total_ref, values_ref, field_ref, total):
    row_bits, col_bits = bits

    def step(chunk, carry):
        terms = []

        def store(row, term):
            total[row] += term

        for lane in range(UNROLL):
            entry = list_ref[which, chunk * UNROLL + lane]
            col = entry & ((1 << col_bits) - 1)
            row = lax.shift_right_logical(entry, col_bits) & ((1 << row_bits) - 1)
            slot = lax.shift_right_logical(entry, col_bits + row_bits)
            term = lax.dot_general(field_ref[col], values_ref[slot], dims, preferred_element_type=jnp.float32)
            terms.append((row, term))
            if len(terms) > DEPTH:
                store(*terms.pop(0))
        for row, term in terms:
            store(row, term)
        return carry

    lax.fori_loop(0, lax.div(total_ref[which] + UNROLL - 1, UNROLL), step, 0)


def join(pieces, field):
    if len(pieces) == 1:
        return pieces[0]
    at = 0
    for piece in pieces:
        field[pl.ds(at, piece.shape[0])] = piece[...]
        at += piece.shape[0]
    return field


def swap_order(chips):
    return list(reversed(range(chips)))


def swapped_early(chips):
    return chips - 1


def swapped_rows(index, chips, owned, first_ref, rest_ref):
    early = swapped_early(chips)
    if index < early:
        return first_ref[pl.ds(index * owned, owned)]
    return rest_ref[pl.ds((index - early) * owned, owned)]


def first_kernel(pieces, steps, chips, bits, dims, list_ref, total_ref, values_ref, *refs):
    piece_refs, refs = refs[:pieces], refs[pieces:]
    out_refs, refs = refs[:2 * steps], refs[2 * steps:]
    in_refs, refs = refs[:2 * steps], refs[2 * steps:]
    sent_refs, totals, (token_ref, field) = refs[:-CORES - 2], refs[-CORES - 2:-2], refs[-2:]
    field_ref = join(piece_refs, field)
    token_ref[...] = jnp.zeros_like(token_ref)
    chip = lax.axis_index("row") // CORES
    for half, total in enumerate(totals):
        rows = total.shape[0] - 1
        owned = rows // chips
        if steps == 0:
            total[...] = jnp.zeros(total.shape, jnp.float32)
        else:
            for index, shift in enumerate(swap_order(chips)):
                swapped = in_refs if half else out_refs
                value = sum(
                    swapped_rows(index, chips, owned, *swapped[2 * step:2 * step + 2]).astype(jnp.float32)
                    for step in range(steps))
                if half == 0:
                    value = -value
                elif shift > 0:
                    for step in range(steps):
                        value -= sent_refs[step * (chips - 1) + index][...].astype(jnp.float32)
                total[pl.ds(partner(chip, shift, chips) * owned, owned)] = value
        add_products(half, bits, dims, list_ref, total_ref, values_ref, field_ref, total)


def stage_kernel(stage, bits, dims, pieces, list_ref, total_ref, values_ref, *refs):
    piece_refs, refs = refs[:pieces], refs[pieces + CORES:]
    totals, field = refs[:CORES], refs[-1]
    field_ref = join(piece_refs, field)
    for half, total in enumerate(totals):
        add_products(stage * CORES + half, bits, dims, list_ref, total_ref, values_ref, field_ref, total)


def last_kernel(stage, half, bits, dims, pieces, chips, list_ref, total_ref, values_ref, *refs):
    piece_refs, refs = refs[:pieces], refs[pieces + 1:]
    if half == 0:
        total, out_ref, field = refs
        other = total
    else:
        other, total, out_ref, field = refs
    field_ref = join(piece_refs, field)
    add_products(stage * CORES + half, bits, dims, list_ref, total_ref, values_ref, field_ref, total)
    chip = lax.axis_index("row") // CORES
    owned = (other.shape[0] - 1) // chips
    shifts, early = swap_order(chips), swapped_early(chips)
    for index, shift in enumerate(shifts[early:] if half else shifts[:early]):
        rows = other[pl.ds(partner(chip, shift, chips) * owned, owned)]
        out_ref[pl.ds(index * owned, owned)] = rows.astype(out_ref.dtype)


def chip_rows(index, chips, owned, own_ref, *other_refs):
    chip = lax.axis_index("row") // CORES
    at = pl.ds(partner(chip, swap_order(chips)[index], chips) * owned, owned)
    return own_ref[at] + swapped_rows(index, chips, owned, *other_refs).astype(jnp.float32)


def combine_first_kernel(chips, own_ref, first_ref, *send_refs):
    for index, send_ref in enumerate(send_refs):
        rows = chip_rows(index, chips, send_ref.shape[0], own_ref, first_ref, None)
        send_ref[...] = rows.astype(send_ref.dtype)


def combine_rest_kernel(chips, own_ref, rest_ref, left_ref, sol_ref, before_ref, base_ref, *send_refs):
    owned = base_ref.shape[0]
    for index, send_ref in enumerate(send_refs):
        rows = chip_rows(swapped_early(chips) + index, chips, owned, own_ref, None, rest_ref)
        send_ref[...] = rows.astype(send_ref.dtype)
    keep = chip_rows(chips - 1, chips, owned, own_ref, None, rest_ref)
    base_ref[...] = left_ref[...] - sol_ref[...] - keep


def per_device(block_values, block_rows, block_cols, block_counts, precond, right_side):
    owned, rhs, size = right_side.shape[1:]
    row_devices = lax.axis_size("row")
    groups = lax.axis_size("col")
    chips = row_devices // CORES
    group = owned * row_devices
    half_rows = chips * owned
    slots = block_values.shape[2]

    parts = 2 if owned % 2 == 0 else 1
    stages = gather_stages(groups, parts)
    final = len(stages) - 1
    lists_total = len(stages) * CORES
    widest = max(len(stage) for stage in stages) * owned // parts
    row_bits, col_bits = bits = half_rows.bit_length(), (widest - 1).bit_length()
    assert (slots - 1).bit_length() + row_bits + col_bits <= 31
    assert slots % LANES == 0

    field_type = jax.ShapeDtypeStruct((owned, rhs, size), jnp.float32)
    matrix_type = jax.ShapeDtypeStruct((owned, size, size), jnp.bfloat16)
    total_type = jax.ShapeDtypeStruct((half_rows + 1, rhs, size), jnp.float32)
    index_type = pltpu.SMEM(block_rows.shape, jnp.int32)
    token_type = jax.ShapeDtypeStruct((8, 128), jnp.float32)
    loads = next(count for count in (4, 2, 1) if owned % count == 0)
    rounded_type = jax.ShapeDtypeStruct((owned, rhs, size), jnp.bfloat16)
    part_type = jax.ShapeDtypeStruct((owned // parts, rhs, size), jnp.bfloat16)

    high, low, sol, left, whole, *rounded = pl.pallas_call(
        start_kernel,
        out_shape=[matrix_type] * 2 + [field_type] * 2 + [rounded_type] + [part_type] * parts,
        in_specs=[in_hbm()] * 2,
        out_specs=[in_vmem()] * (5 + parts),
        scratch_shapes=[
            pltpu.VMEM((owned, size, size), jnp.float32),
            pltpu.SemaphoreType.DMA((loads + 1,)),
        ],
        compiler_params=params(),
        name="start",
    )(stay_in_hbm(precond[0]), stay_in_hbm(right_side[0]))

    *lists, values, order_token = pl.pallas_call(
        functools.partial(order_kernel, group, owned, groups, parts, stages, bits),
        out_shape=[
            pltpu.SMEM((lists_total + 1, slots + UNROLL), jnp.int32),
            pltpu.SMEM((lists_total,), jnp.int32),
            pltpu.VMEM(block_values.shape[2:], block_values.dtype),
            token_type,
        ],
        in_specs=[in_smem()] + [in_hbm()] * 3,
        out_specs=[in_smem()] * 2 + [in_vmem()] * 2,
        scratch_shapes=[
            index_type, index_type,
            pltpu.SMEM((groups * row_devices * parts,), jnp.int32),
            pltpu.SMEM((groups * row_devices * parts,), jnp.int32),
            pltpu.SMEM((lists_total + 1,), jnp.int32),
            pltpu.SemaphoreType.DMA((3,)),
        ],
        compiler_params=params(),
        name="order",
    )(block_counts, *[stay_in_hbm(array) for array in (block_rows, block_cols, block_values[0, 0])])

    def turn(values, base):
        return pl.pallas_call(
            turn_kernel,
            out_shape=[pltpu.VMEM(values.shape, values.dtype), field_type],
            in_specs=[in_smem()] + [in_vmem()] * 2,
            out_specs=[in_vmem()] * 2,
            input_output_aliases={2: 1},
            compiler_params=params(),
            cost_estimate=pl.CostEstimate(flops=HIDE_FLOPS, bytes_accessed=0, transcendentals=0),
            name="turn",
        )(lists[1], values, base)

    def cost(share):
        return pl.CostEstimate(
            flops=int(slots * share) * 2 * rhs * size * size,
            bytes_accessed=int(slots * share) * 2 * size * size, transcendentals=0)

    def field_scratch(pieces):
        return pltpu.VMEM((sum(piece.shape[0] for piece in pieces), rhs, size), jnp.bfloat16)

    def product_first(values, dims, pieces, outs, ins, sent):
        return pl.pallas_call(
            functools.partial(first_kernel, len(pieces), len(outs) // 2, chips, bits, dims),
            out_shape=[total_type] * CORES + [token_type],
            in_specs=[in_smem()] * 2 + [in_vmem()] * (1 + len(pieces) + len(outs) + len(ins) + len(sent)),
            out_specs=[in_vmem()] * (CORES + 1),
            compiler_params=params(),
            scratch_shapes=[field_scratch(pieces)],
            cost_estimate=cost(len(stages[0]) / groups / parts),
            name="stage0",
        )(*lists, values, *pieces, *outs, *ins, *sent)

    def product_stage(values, dims, stage, pieces, totals):
        inputs = 3 + len(pieces)
        return pl.pallas_call(
            functools.partial(stage_kernel, stage, bits, dims, len(pieces)),
            out_shape=[total_type] * CORES,
            in_specs=[in_smem()] * 2 + [in_vmem()] * (1 + len(pieces) + CORES),
            out_specs=[in_vmem()] * CORES,
            scratch_shapes=[field_scratch(pieces)],
            input_output_aliases={inputs + half: half for half in range(CORES)},
            compiler_params=params(),
            cost_estimate=cost(len(stages[stage]) / groups / parts),
            name="stage%d" % stage,
        )(*lists, values, *pieces, *totals)

    def product_last(values, dims, half, pieces, total, *other):
        send_chips = chips - swapped_early(chips) if half else swapped_early(chips)
        return pl.pallas_call(
            functools.partial(last_kernel, final, half, bits, dims, len(pieces), chips),
            out_shape=[total_type, jax.ShapeDtypeStruct((send_chips * owned, rhs, size), jnp.bfloat16)],
            in_specs=[in_smem()] * 2 + [in_vmem()] * (2 + len(pieces) + len(other)),
            out_specs=[in_vmem()] * 2,
            scratch_shapes=[field_scratch(pieces)],
            input_output_aliases={3 + len(pieces): 0},
            compiler_params=params(),
            cost_estimate=pl.CostEstimate(
                flops=HIDE_FLOPS if half else 0, bytes_accessed=0, transcendentals=0),
            name="last%d" % half,
        )(*lists, values, *pieces, total, *other)

    def hold(piece, token):
        return pl.pallas_call(
            hold_kernel,
            out_shape=part_type,
            in_specs=[in_vmem()] * 2,
            out_specs=in_vmem(),
            input_output_aliases={0: 0},
            compiler_params=params(),
            name="hold",
        )(piece, token)

    early = swapped_early(chips)

    def combine_first(own, first):
        return pl.pallas_call(
            functools.partial(combine_first_kernel, chips),
            out_shape=[rounded_type] * early,
            in_specs=[in_vmem()] * 2,
            out_specs=[in_vmem()] * early,
            compiler_params=params(),
            name="combine0",
        )(own, first)

    def combine_rest(own, rest, left, sol, before):
        return pl.pallas_call(
            functools.partial(combine_rest_kernel, chips),
            out_shape=[field_type] + [rounded_type] * (chips - 1 - early),
            in_specs=[in_vmem()] * 5,
            out_specs=[in_vmem()] * (chips - early),
            compiler_params=params(),
            name="combine1",
        )(own, rest, left, sol, before)

    def apply(part, sol, left, base, pieces, earlier):
        last = part == parts - 1
        return pl.pallas_call(
            functools.partial(apply_kernel, part, parts, len(pieces)),
            out_shape=[field_type, field_type, part_type] + [rounded_type] * last,
            in_specs=[in_vmem()] * (5 + len(pieces) + len(earlier)),
            out_specs=[in_vmem()] * (3 + last),
            input_output_aliases={2: 1, 3: 0},
            compiler_params=params(),
            cost_estimate=pl.CostEstimate(flops=HIDE_FLOPS, bytes_accessed=0, transcendentals=0),
            name="apply%d" % part,
        )(high, low, left, sol, base, *pieces, *earlier)

    blocks = values, NT
    outs, ins, sent = [], [], []
    for step in range(ITERS):
        sets = gather(whole, rounded, groups)

        def stage_pieces(stage):
            return [sets[piece] for piece in stages[stage] if piece in sets]

        def forward(part, token=None):
            for index in range(1, groups // 2):
                if token is not None:
                    sets[index, part] = hold(sets[index, part], token)
                sets[groups // 2 + index, part] = lax.ppermute(sets[index, part], "col", neighbours(groups))

        if groups % 2 == 0:
            for part in range(parts - 1):
                forward(part, order_token if step == 0 else None)
        *totals, token = product_first(*blocks, stage_pieces(0), outs, ins, sent)
        if groups % 2 == 0:
            forward(parts - 1, order_token if step == 0 else token)

        for stage in range(1, final):
            totals = product_stage(*blocks, stage, stage_pieces(stage), totals)
        other, out_first = product_last(*blocks, 0, stage_pieces(final), totals[0])
        own, out_rest = product_last(*blocks, 1, stage_pieces(final), totals[1], other)
        outgoing = [out_first, out_rest]
        incoming = [lax.ppermute(rows, "row", neighbours(row_devices)) for rows in outgoing]
        outs += outgoing
        ins += incoming
        first = combine_first(own, incoming[0])
        base, *rest = combine_rest(own, incoming[1], left, sol, first[-1])
        sends = list(first) + rest
        sent += sends
        pieces = [
            lax.ppermute(send, "row", [
                (chip * CORES + core, partner(chip, shift, chips) * CORES + core)
                for chip in range(chips) for core in range(CORES)
            ])
            for shift, send in zip(swap_order(chips), sends)
        ]
        if step == 0:
            turned, base = turn(values, base)
            blocks = turned, NN
        if step < ITERS - 1:
            rounded = []
            for part in range(parts):
                sol, left, new, *done = apply(part, sol, left, base, pieces, rounded if part == parts - 1 else [])
                rounded.append(new)
            whole, = done
    return pl.pallas_call(
        functools.partial(finish_kernel, len(pieces)),
        out_shape=field_type,
        in_specs=[in_vmem()] * (4 + len(pieces)),
        out_specs=in_hbm(),
        scratch_shapes=[
            pltpu.VMEM((owned, rhs, size), jnp.float32),
            pltpu.SemaphoreType.DMA((2 if owned % 2 == 0 else 1,)),
        ],
        compiler_params=params(),
        name="finish",
    )(high, low, sol, base, *pieces)[None]


def solution(mesh):
    placed = (
        P("row", "col", None, None, None),
        P("row", "col", None),
        P("row", "col", None),
        P("row", "col"),
        P("col", "row", None, None),
        P("col", "row", None, None),
    )
    return jax.shard_map(
        per_device,
        mesh=mesh,
        in_specs=placed,
        out_specs=P("col", "row", None, None),
        check_vma=False,
    )
```

```python
import functools

import jax
import jax.numpy as jnp
from jax import lax
from jax.experimental import pallas as pl
from jax.experimental.pallas import tpu as pltpu
from jax.sharding import PartitionSpec as P

ITERS = 3
UNROLL = 16
LANES = 4
DEPTH = 6
HIDE_FLOPS = 20_000_000_000
CORES = 2
VMEM_LIMIT = 24 * 1024 * 1024

NT = (((1,), (1,)), ((), ()))
NN = (((1,), (0,)), ((), ()))


def in_vmem():
    return pl.BlockSpec(memory_space=pltpu.VMEM)


def in_hbm():
    return pl.BlockSpec(memory_space=pltpu.HBM)


def in_smem():
    return pl.BlockSpec(memory_space=pltpu.SMEM)


def stay_in_hbm(array):
    return pltpu.with_memory_space_constraint(array, pltpu.HBM)


def params():
    return pltpu.CompilerParams(vmem_limit_bytes=VMEM_LIMIT)


def split(value):
    high = value.astype(jnp.bfloat16)
    low = (value - high.astype(jnp.float32)).astype(jnp.bfloat16)
    return high, low


def times_block(field, high, low):
    field_high, field_low = split(field)
    rhs = field.shape[0]
    both = jnp.concatenate([field_high, field_low], axis=0)
    first = lax.dot_general(both, high, NT, preferred_element_type=jnp.float32)
    second = lax.dot_general(field_high, low, NT, preferred_element_type=jnp.float32)
    return first[:rhs] + (first[rhs:] + second)


def partner(chip, shift, chips):
    if chips & (chips - 1) == 0:
        return chip ^ shift
    return (chip + shift) % chips


def halves(value, size):
    if size & (size - 1) == 0:
        return lax.shift_right_logical(value, size.bit_length() - 1), value & (size - 1)
    return lax.div(value, size), lax.rem(value, size)


def relative(mine, source, groups):
    if groups % 2:
        away = mine - source
        return jnp.where(away < 0, away + groups, away)
    other = (mine ^ source) & 1
    away = (mine ^ other) - source
    away = jnp.where(away < 0, away + groups, away)
    return other * (groups // 2) + lax.shift_right_logical(away, 1)


def gather_stages(groups, parts):
    every = range(parts)
    own = [(0, part) for part in every]
    if groups % 2:
        return [own, [(index, part) for index in range(1, groups) for part in every]]
    pairs = groups // 2
    early = range(parts - 1)
    far, forwarded = range(1, pairs), range(pairs + 1, groups)
    stages = [
        own + [(index, part) for part in early for index in far],
        [(pairs, part) for part in every] + [(index, parts - 1) for index in far]
        + [(index, part) for part in early for index in forwarded],
        [(index, parts - 1) for index in forwarded],
    ]
    return [stage for stage in stages if stage]


def ring(groups, step):
    return [(c, (c + step) % groups) for c in range(groups)]


def gather(whole, rounded, groups):
    sets = {(0, 0): whole}
    if groups % 2:
        for step in range(1, groups):
            sets[step, 0] = lax.ppermute(whole, "col", ring(groups, step))
        return sets
    for part, piece in enumerate(rounded):
        for step in range(1, groups // 2):
            sets[step, part] = lax.ppermute(piece, "col", ring(groups, 2 * step))
    sets[groups // 2, 0] = lax.ppermute(whole, "col", neighbours(groups))
    for step in range(1, groups // 2):
        across = [(c, ((c + 2 * step) % groups) ^ 1) for c in range(groups)]
        sets[groups // 2 + step, len(rounded) - 1] = lax.ppermute(rounded[-1], "col", across)
    return sets


def neighbours(count):
    return [(index, index ^ 1) for index in range(count)]


def hold_kernel(piece_ref, token_ref, out_ref):
    pass


def put_rounded(p, value, whole_ref, part_refs):
    part, inner = divmod(p, part_refs[0].shape[0])
    rounded = value.astype(jnp.bfloat16)
    whole_ref[p] = rounded
    part_refs[part][inner] = rounded


def start_kernel(precond_hbm, rhs_hbm, high_ref, low_ref, sol_ref, left_ref, whole_ref, *refs):
    part_refs, (precond_ref, sems) = refs[:-2], refs[-2:]
    owned = left_ref.shape[0]
    parts = sems.shape[0] - 1
    each = owned // parts
    loads = [pltpu.make_async_copy(rhs_hbm, left_ref, sems.at[parts])]
    for part in range(parts):
        at = pl.ds(part * each, each)
        loads.append(pltpu.make_async_copy(precond_hbm.at[at], precond_ref.at[at], sems.at[part]))
    for load in loads:
        load.start()
    loads[0].wait()
    for part in range(parts):
        loads[1 + part].wait()
        for p in range(part * each, (part + 1) * each):
            high, low = split(precond_ref[p])
            high_ref[p] = high
            low_ref[p] = low
            value = times_block(left_ref[p], high, low)
            sol_ref[p] = value
            put_rounded(p, value, whole_ref, part_refs)


def apply_kernel(part, parts, pieces, high_ref, low_ref, left_ref, sol_ref, base_ref, *refs):
    piece_refs, refs = refs[:pieces], refs[pieces:]
    earlier_refs, refs = refs[:-3 - (part == parts - 1)], refs[-3 - (part == parts - 1):]
    new_ref, new_left_ref, rounded_ref, *whole_refs = refs
    each = rounded_ref.shape[0]
    for whole_ref in whole_refs:
        for index, earlier_ref in enumerate(earlier_refs):
            whole_ref[pl.ds(index * each, each)] = earlier_ref[...]
    for inner in range(each):
        p = part * each + inner
        received = sum(piece_ref[p].astype(jnp.float32) for piece_ref in piece_refs)
        value = sol_ref[p] + times_block(base_ref[p] - received, high_ref[p], low_ref[p])
        new_ref[p] = value
        new_left_ref[p] = left_ref[p] - received
        for out_ref, at in [(rounded_ref, inner)] + [(whole_ref, p) for whole_ref in whole_refs]:
            out_ref[at] = value.astype(jnp.bfloat16)


def finish_kernel(pieces, high_ref, low_ref, sol_ref, base_ref, *refs):
    piece_refs, (out_hbm, value_ref, sems) = refs[:pieces], refs[pieces:]
    owned = sol_ref.shape[0]
    parts = sems.shape[0]
    each = owned // parts
    stores = []
    for part in range(parts):
        for p in range(part * each, (part + 1) * each):
            received = sum(piece_ref[p].astype(jnp.float32) for piece_ref in piece_refs)
            value_ref[p] = sol_ref[p] + times_block(base_ref[p] - received, high_ref[p], low_ref[p])
        at = pl.ds(part * each, each)
        stores.append(pltpu.make_async_copy(value_ref.at[at], out_hbm.at[at], sems.at[part]))
        stores[-1].start()
    for store in stores:
        store.wait()


def order_kernel(group, owned, groups, parts, stages, bits, count_ref, rows_hbm, cols_hbm, values_hbm,
                 list_out, total_out, values_out, token_ref, rows_ref, cols_ref, first_ref, base_ref, total_ref,
                 sems):
    token_ref[...] = jnp.zeros_like(token_ref)
    loads = [
        pltpu.make_async_copy(rows_hbm, rows_ref, sems.at[0]),
        pltpu.make_async_copy(cols_hbm, cols_ref, sems.at[1]),
        pltpu.make_async_copy(values_hbm, values_out, sems.at[2]),
    ]
    for load in loads:
        load.start()
    other = 1 - (lax.axis_index("row") & (CORES - 1))
    mine = lax.axis_index("col")
    row_bits, col_bits = bits
    lists = len(stages) * CORES
    each = owned // parts
    trash = (group // CORES) << col_bits
    places = {
        piece: (index * CORES, place * each) for index, stage in enumerate(stages) for place, piece in enumerate(stage)
    }
    own_rows = lax.axis_index("row") * owned
    for source in range(groups):
        piece = relative(mine, source, groups)
        for part in range(parts):
            first, base = places[0, part]
            for index in range(1, groups):
                first = jnp.where(piece == index, places[index, part][0], first)
                base = jnp.where(piece == index, places[index, part][1], base)
            at = halves(source * group + own_rows + part * each, each)[0]
            first_ref[at] = first
            base_ref[at] = base
    for index in range(lists + 1):
        total_ref[index] = 0
    for load in loads[:2]:
        load.wait()
    used = count_ref[0, 0]

    def place(chunk, carry):
        entries = []
        for lane in range(LANES):
            slot = chunk * LANES + lane
            owner, row_inner = halves(halves(rows_ref[0, 0, slot], group)[1], owned)
            at, inner = halves(cols_ref[0, 0, slot], each)
            half = (owner & (CORES - 1)) ^ other
            which = jnp.where(slot < used, first_ref[at] + half, lists)
            row = lax.shift_right_logical(owner, 1) * owned + row_inner
            col = base_ref[at] + inner
            entries.append((which, (((slot << row_bits) | row) << col_bits) | col))
        for which, entry in entries:
            at = total_ref[which]
            list_out[which, at] = entry
            total_ref[which] = at + 1
        return carry

    lax.fori_loop(0, lax.div(used + LANES - 1, LANES), place, 0)
    for index in range(lists):
        total_out[index] = total_ref[index]

    def close(index, carry):
        for extra in range(UNROLL):
            list_out[index, total_ref[index] + extra] = trash
        return carry

    lax.fori_loop(0, lists, close, 0)
    loads[2].wait()


def turn_kernel(total_ref, values_ref, base_ref, turned_ref, same_ref):
    used = sum(total_ref[index] for index in range(total_ref.shape[0]))

    def turn(chunk, carry):
        for lane in range(LANES):
            turned_ref[chunk * LANES + lane] = values_ref[chunk * LANES + lane].T
        return carry

    lax.fori_loop(0, lax.div(used + LANES - 1, LANES), turn, 0)


def add_products(which, bits, dims, list_ref, total_ref, values_ref, field_ref, total):
    row_bits, col_bits = bits

    def step(chunk, carry):
        terms = []

        def store(row, term):
            total[row] += term

        for lane in range(UNROLL):
            entry = list_ref[which, chunk * UNROLL + lane]
            col = entry & ((1 << col_bits) - 1)
            row = lax.shift_right_logical(entry, col_bits) & ((1 << row_bits) - 1)
            slot = lax.shift_right_logical(entry, col_bits + row_bits)
            term = lax.dot_general(field_ref[col], values_ref[slot], dims, preferred_element_type=jnp.float32)
            terms.append((row, term))
            if len(terms) > DEPTH:
                store(*terms.pop(0))
        for row, term in terms:
            store(row, term)
        return carry

    lax.fori_loop(0, lax.div(total_ref[which] + UNROLL - 1, UNROLL), step, 0)


def join(pieces, field):
    if len(pieces) == 1:
        return pieces[0]
    at = 0
    for piece in pieces:
        field[pl.ds(at, piece.shape[0])] = piece[...]
        at += piece.shape[0]
    return field


def swap_order(chips):
    return list(reversed(range(chips)))


def swapped_early(chips):
    return chips - 1


def swapped_rows(index, chips, owned, first_ref, rest_ref):
    early = swapped_early(chips)
    if index < early:
        return first_ref[pl.ds(index * owned, owned)]
    return rest_ref[pl.ds((index - early) * owned, owned)]


def first_kernel(pieces, steps, chips, bits, dims, list_ref, total_ref, values_ref, *refs):
    piece_refs, refs = refs[:pieces], refs[pieces:]
    out_refs, refs = refs[:2 * steps], refs[2 * steps:]
    in_refs, refs = refs[:2 * steps], refs[2 * steps:]
    sent_refs, totals, (token_ref, field) = refs[:-CORES - 2], refs[-CORES - 2:-2], refs[-2:]
    field_ref = join(piece_refs, field)
    token_ref[...] = jnp.zeros_like(token_ref)
    chip = lax.axis_index("row") // CORES
    for half, total in enumerate(totals):
        rows = total.shape[0] - 1
        owned = rows // chips
        if steps == 0:
            total[...] = jnp.zeros(total.shape, jnp.float32)
        else:
            for index, shift in enumerate(swap_order(chips)):
                swapped = in_refs if half else out_refs
                value = sum(
                    swapped_rows(index, chips, owned, *swapped[2 * step:2 * step + 2]).astype(jnp.float32)
                    for step in range(steps))
                if half == 0:
                    value = -value
                elif shift > 0:
                    for step in range(steps):
                        value -= sent_refs[step * (chips - 1) + index][...].astype(jnp.float32)
                total[pl.ds(partner(chip, shift, chips) * owned, owned)] = value
        add_products(half, bits, dims, list_ref, total_ref, values_ref, field_ref, total)


def stage_kernel(stage, bits, dims, pieces, list_ref, total_ref, values_ref, *refs):
    piece_refs, refs = refs[:pieces], refs[pieces + CORES:]
    totals, field = refs[:CORES], refs[-1]
    field_ref = join(piece_refs, field)
    for half, total in enumerate(totals):
        add_products(stage * CORES + half, bits, dims, list_ref, total_ref, values_ref, field_ref, total)


def last_kernel(stage, half, bits, dims, pieces, chips, list_ref, total_ref, values_ref, *refs):
    piece_refs, refs = refs[:pieces], refs[pieces + 1:]
    if half == 0:
        total, out_ref, field = refs
        other = total
    else:
        other, total, out_ref, field = refs
    field_ref = join(piece_refs, field)
    add_products(stage * CORES + half, bits, dims, list_ref, total_ref, values_ref, field_ref, total)
    chip = lax.axis_index("row") // CORES
    owned = (other.shape[0] - 1) // chips
    shifts, early = swap_order(chips), swapped_early(chips)
    for index, shift in enumerate(shifts[early:] if half else shifts[:early]):
        rows = other[pl.ds(partner(chip, shift, chips) * owned, owned)]
        out_ref[pl.ds(index * owned, owned)] = rows.astype(out_ref.dtype)


def chip_rows(index, chips, owned, own_ref, *other_refs):
    chip = lax.axis_index("row") // CORES
    at = pl.ds(partner(chip, swap_order(chips)[index], chips) * owned, owned)
    return own_ref[at] + swapped_rows(index, chips, owned, *other_refs).astype(jnp.float32)


def combine_first_kernel(chips, own_ref, first_ref, *send_refs):
    for index, send_ref in enumerate(send_refs):
        rows = chip_rows(index, chips, send_ref.shape[0], own_ref, first_ref, None)
        send_ref[...] = rows.astype(send_ref.dtype)


def combine_rest_kernel(chips, own_ref, rest_ref, left_ref, sol_ref, before_ref, base_ref, *send_refs):
    owned = base_ref.shape[0]
    for index, send_ref in enumerate(send_refs):
        rows = chip_rows(swapped_early(chips) + index, chips, owned, own_ref, None, rest_ref)
        send_ref[...] = rows.astype(send_ref.dtype)
    keep = chip_rows(chips - 1, chips, owned, own_ref, None, rest_ref)
    base_ref[...] = left_ref[...] - sol_ref[...] - keep


def per_device(block_values, block_rows, block_cols, block_counts, precond, right_side):
    owned, rhs, size = right_side.shape[1:]
    row_devices = lax.axis_size("row")
    groups = lax.axis_size("col")
    chips = row_devices // CORES
    group = owned * row_devices
    half_rows = chips * owned
    slots = block_values.shape[2]

    parts = 2 if owned % 2 == 0 else 1
    stages = gather_stages(groups, parts)
    final = len(stages) - 1
    lists_total = len(stages) * CORES
    widest = max(len(stage) for stage in stages) * owned // parts
    row_bits, col_bits = bits = half_rows.bit_length(), (widest - 1).bit_length()
    assert (slots - 1).bit_length() + row_bits + col_bits <= 31
    assert slots % LANES == 0

    field_type = jax.ShapeDtypeStruct((owned, rhs, size), jnp.float32)
    matrix_type = jax.ShapeDtypeStruct((owned, size, size), jnp.bfloat16)
    total_type = jax.ShapeDtypeStruct((half_rows + 1, rhs, size), jnp.float32)
    index_type = pltpu.SMEM(block_rows.shape, jnp.int32)
    token_type = jax.ShapeDtypeStruct((8, 128), jnp.float32)
    loads = next(count for count in (4, 2, 1) if owned % count == 0)
    rounded_type = jax.ShapeDtypeStruct((owned, rhs, size), jnp.bfloat16)
    part_type = jax.ShapeDtypeStruct((owned // parts, rhs, size), jnp.bfloat16)

    high, low, sol, left, whole, *rounded = pl.pallas_call(
        start_kernel,
        out_shape=[matrix_type] * 2 + [field_type] * 2 + [rounded_type] + [part_type] * parts,
        in_specs=[in_hbm()] * 2,
        out_specs=[in_vmem()] * (5 + parts),
        scratch_shapes=[
            pltpu.VMEM((owned, size, size), jnp.float32),
            pltpu.SemaphoreType.DMA((loads + 1,)),
        ],
        compiler_params=params(),
        name="start",
    )(stay_in_hbm(precond[0]), stay_in_hbm(right_side[0]))

    *lists, values, order_token = pl.pallas_call(
        functools.partial(order_kernel, group, owned, groups, parts, stages, bits),
        out_shape=[
            pltpu.SMEM((lists_total + 1, slots + UNROLL), jnp.int32),
            pltpu.SMEM((lists_total,), jnp.int32),
            pltpu.VMEM(block_values.shape[2:], block_values.dtype),
            token_type,
        ],
        in_specs=[in_smem()] + [in_hbm()] * 3,
        out_specs=[in_smem()] * 2 + [in_vmem()] * 2,
        scratch_shapes=[
            index_type, index_type,
            pltpu.SMEM((groups * row_devices * parts,), jnp.int32),
            pltpu.SMEM((groups * row_devices * parts,), jnp.int32),
            pltpu.SMEM((lists_total + 1,), jnp.int32),
            pltpu.SemaphoreType.DMA((3,)),
        ],
        compiler_params=params(),
        name="order",
    )(block_counts, *[stay_in_hbm(array) for array in (block_rows, block_cols, block_values[0, 0])])

    def turn(values, base):
        return pl.pallas_call(
            turn_kernel,
            out_shape=[pltpu.VMEM(values.shape, values.dtype), field_type],
            in_specs=[in_smem()] + [in_vmem()] * 2,
            out_specs=[in_vmem()] * 2,
            input_output_aliases={2: 1},
            compiler_params=params(),
            cost_estimate=pl.CostEstimate(flops=HIDE_FLOPS, bytes_accessed=0, transcendentals=0),
            name="turn",
        )(lists[1], values, base)

    def cost(share):
        return pl.CostEstimate(
            flops=int(slots * share) * 2 * rhs * size * size,
            bytes_accessed=int(slots * share) * 2 * size * size, transcendentals=0)

    def field_scratch(pieces):
        return pltpu.VMEM((sum(piece.shape[0] for piece in pieces), rhs, size), jnp.bfloat16)

    def product_first(values, dims, pieces, outs, ins, sent):
        return pl.pallas_call(
            functools.partial(first_kernel, len(pieces), len(outs) // 2, chips, bits, dims),
            out_shape=[total_type] * CORES + [token_type],
            in_specs=[in_smem()] * 2 + [in_vmem()] * (1 + len(pieces) + len(outs) + len(ins) + len(sent)),
            out_specs=[in_vmem()] * (CORES + 1),
            compiler_params=params(),
            scratch_shapes=[field_scratch(pieces)],
            cost_estimate=cost(len(stages[0]) / groups / parts),
            name="stage0",
        )(*lists, values, *pieces, *outs, *ins, *sent)

    def product_stage(values, dims, stage, pieces, totals):
        inputs = 3 + len(pieces)
        return pl.pallas_call(
            functools.partial(stage_kernel, stage, bits, dims, len(pieces)),
            out_shape=[total_type] * CORES,
            in_specs=[in_smem()] * 2 + [in_vmem()] * (1 + len(pieces) + CORES),
            out_specs=[in_vmem()] * CORES,
            scratch_shapes=[field_scratch(pieces)],
            input_output_aliases={inputs + half: half for half in range(CORES)},
            compiler_params=params(),
            cost_estimate=cost(len(stages[stage]) / groups / parts),
            name="stage%d" % stage,
        )(*lists, values, *pieces, *totals)

    def product_last(values, dims, half, pieces, total, *other):
        send_chips = chips - swapped_early(chips) if half else swapped_early(chips)
        return pl.pallas_call(
            functools.partial(last_kernel, final, half, bits, dims, len(pieces), chips),
            out_shape=[total_type, jax.ShapeDtypeStruct((send_chips * owned, rhs, size), jnp.bfloat16)],
            in_specs=[in_smem()] * 2 + [in_vmem()] * (2 + len(pieces) + len(other)),
            out_specs=[in_vmem()] * 2,
            scratch_shapes=[field_scratch(pieces)],
            input_output_aliases={3 + len(pieces): 0},
            compiler_params=params(),
            cost_estimate=pl.CostEstimate(
                flops=HIDE_FLOPS if half else 0, bytes_accessed=0, transcendentals=0),
            name="last%d" % half,
        )(*lists, values, *pieces, total, *other)

    def hold(piece, token):
        return pl.pallas_call(
            hold_kernel,
            out_shape=part_type,
            in_specs=[in_vmem()] * 2,
            out_specs=in_vmem(),
            input_output_aliases={0: 0},
            compiler_params=params(),
            name="hold",
        )(piece, token)

    early = swapped_early(chips)

    def combine_first(own, first):
        return pl.pallas_call(
            functools.partial(combine_first_kernel, chips),
            out_shape=[rounded_type] * early,
            in_specs=[in_vmem()] * 2,
            out_specs=[in_vmem()] * early,
            compiler_params=params(),
            name="combine0",
        )(own, first)

    def combine_rest(own, rest, left, sol, before):
        return pl.pallas_call(
            functools.partial(combine_rest_kernel, chips),
            out_shape=[field_type] + [rounded_type] * (chips - 1 - early),
            in_specs=[in_vmem()] * 5,
            out_specs=[in_vmem()] * (chips - early),
            compiler_params=params(),
            name="combine1",
        )(own, rest, left, sol, before)

    def apply(part, sol, left, base, pieces, earlier):
        last = part == parts - 1
        return pl.pallas_call(
            functools.partial(apply_kernel, part, parts, len(pieces)),
            out_shape=[field_type, field_type, part_type] + [rounded_type] * last,
            in_specs=[in_vmem()] * (5 + len(pieces) + len(earlier)),
            out_specs=[in_vmem()] * (3 + last),
            input_output_aliases={2: 1, 3: 0},
            compiler_params=params(),
            cost_estimate=pl.CostEstimate(flops=HIDE_FLOPS, bytes_accessed=0, transcendentals=0),
            name="apply%d" % part,
        )(high, low, left, sol, base, *pieces, *earlier)

    blocks = values, NT
    outs, ins, sent = [], [], []
    for step in range(ITERS):
        sets = gather(whole, rounded, groups)

        def stage_pieces(stage):
            return [sets[piece] for piece in stages[stage] if piece in sets]

        def forward(part, token=None):
            for index in range(1, groups // 2):
                if token is not None:
                    sets[index, part] = hold(sets[index, part], token)
                sets[groups // 2 + index, part] = lax.ppermute(sets[index, part], "col", neighbours(groups))

        if groups % 2 == 0:
            for part in range(parts - 1):
                forward(part, order_token if step == 0 else None)
        *totals, _ = product_first(*blocks, stage_pieces(0), outs, ins, sent)

        for stage in range(1, final):
            totals = product_stage(*blocks, stage, stage_pieces(stage), totals)
        other, out_first = product_last(*blocks, 0, stage_pieces(final), totals[0])
        own, out_rest = product_last(*blocks, 1, stage_pieces(final), totals[1], other)
        outgoing = [out_first, out_rest]
        incoming = [lax.ppermute(rows, "row", neighbours(row_devices)) for rows in outgoing]
        outs += outgoing
        ins += incoming
        first = combine_first(own, incoming[0])
        base, *rest = combine_rest(own, incoming[1], left, sol, first[-1])
        sends = list(first) + rest
        sent += sends
        pieces = [
            lax.ppermute(send, "row", [
                (chip * CORES + core, partner(chip, shift, chips) * CORES + core)
                for chip in range(chips) for core in range(CORES)
            ])
            for shift, send in zip(swap_order(chips), sends)
        ]
        if step == 0:
            turned, base = turn(values, base)
            blocks = turned, NN
        if step < ITERS - 1:
            rounded = []
            for part in range(parts):
                sol, left, new, *done = apply(part, sol, left, base, pieces, rounded if part == parts - 1 else [])
                rounded.append(new)
            whole, = done
    return pl.pallas_call(
        functools.partial(finish_kernel, len(pieces)),
        out_shape=field_type,
        in_specs=[in_vmem()] * (4 + len(pieces)),
        out_specs=in_hbm(),
        scratch_shapes=[
            pltpu.VMEM((owned, rhs, size), jnp.float32),
            pltpu.SemaphoreType.DMA((2 if owned % 2 == 0 else 1,)),
        ],
        compiler_params=params(),
        name="finish",
    )(high, low, sol, base, *pieces)[None]


def solution(mesh):
    placed = (
        P("row", "col", None, None, None),
        P("row", "col", None),
        P("row", "col", None),
        P("row", "col"),
        P("col", "row", None, None),
        P("col", "row", None, None),
    )
    return jax.shard_map(
        per_device,
        mesh=mesh,
        in_specs=placed,
        out_specs=P("col", "row", None, None),
        check_vma=False,
    )
```

```python
import functools

import jax
import jax.numpy as jnp
from jax import lax
from jax.experimental import pallas as pl
from jax.experimental.pallas import tpu as pltpu
from jax.sharding import PartitionSpec as P

ITERS = 3
UNROLL = 16
LANES = 4
DEPTH = 6
HIDE_FLOPS = 20_000_000_000
CORES = 2
VMEM_LIMIT = 24 * 1024 * 1024

NT = (((1,), (1,)), ((), ()))
NN = (((1,), (0,)), ((), ()))


def in_vmem():
    return pl.BlockSpec(memory_space=pltpu.VMEM)


def in_hbm():
    return pl.BlockSpec(memory_space=pltpu.HBM)


def in_smem():
    return pl.BlockSpec(memory_space=pltpu.SMEM)


def stay_in_hbm(array):
    return pltpu.with_memory_space_constraint(array, pltpu.HBM)


def params():
    return pltpu.CompilerParams(vmem_limit_bytes=VMEM_LIMIT)


def split(value):
    high = value.astype(jnp.bfloat16)
    low = (value - high.astype(jnp.float32)).astype(jnp.bfloat16)
    return high, low


def times_block(field, high, low):
    field_high, field_low = split(field)
    rhs = field.shape[0]
    both = jnp.concatenate([field_high, field_low], axis=0)
    first = lax.dot_general(both, high, NT, preferred_element_type=jnp.float32)
    second = lax.dot_general(field_high, low, NT, preferred_element_type=jnp.float32)
    return first[:rhs] + (first[rhs:] + second)


def partner(chip, shift, chips):
    if chips & (chips - 1) == 0:
        return chip ^ shift
    return (chip + shift) % chips


def halves(value, size):
    if size & (size - 1) == 0:
        return lax.shift_right_logical(value, size.bit_length() - 1), value & (size - 1)
    return lax.div(value, size), lax.rem(value, size)


def relative(mine, source, groups):
    if groups % 2:
        away = mine - source
        return jnp.where(away < 0, away + groups, away)
    other = (mine ^ source) & 1
    away = (mine ^ other) - source
    away = jnp.where(away < 0, away + groups, away)
    return other * (groups // 2) + lax.shift_right_logical(away, 1)


def gather_stages(groups, parts):
    every = range(parts)
    own = [(0, part) for part in every]
    if groups % 2:
        return [own, [(index, part) for index in range(1, groups) for part in every]]
    pairs = groups // 2
    early = range(parts - 1)
    far, forwarded = range(1, pairs), range(pairs + 1, groups)
    stages = [
        own,
        [(index, part) for part in early for index in far],
        [(pairs, part) for part in every] + [(index, parts - 1) for index in far]
        + [(index, part) for part in early for index in forwarded],
        [(index, parts - 1) for index in forwarded],
    ]
    return [stage for stage in stages if stage]


def ring(groups, step):
    return [(c, (c + step) % groups) for c in range(groups)]


def gather(whole, rounded, groups):
    sets = {(0, 0): whole}
    if groups % 2:
        for step in range(1, groups):
            sets[step, 0] = lax.ppermute(whole, "col", ring(groups, step))
        return sets
    for part, piece in enumerate(rounded):
        for step in range(1, groups // 2):
            sets[step, part] = lax.ppermute(piece, "col", ring(groups, 2 * step))
    sets[groups // 2, 0] = lax.ppermute(whole, "col", neighbours(groups))
    for step in range(1, groups // 2):
        across = [(c, ((c + 2 * step) % groups) ^ 1) for c in range(groups)]
        sets[groups // 2 + step, len(rounded) - 1] = lax.ppermute(rounded[-1], "col", across)
    return sets


def neighbours(count):
    return [(index, index ^ 1) for index in range(count)]


def hold_kernel(piece_ref, token_ref, out_ref):
    pass


def put_rounded(p, value, whole_ref, part_refs):
    part, inner = divmod(p, part_refs[0].shape[0])
    rounded = value.astype(jnp.bfloat16)
    whole_ref[p] = rounded
    part_refs[part][inner] = rounded


def start_kernel(precond_hbm, rhs_hbm, high_ref, low_ref, sol_ref, left_ref, whole_ref, *refs):
    part_refs, (precond_ref, sems) = refs[:-2], refs[-2:]
    owned = left_ref.shape[0]
    parts = sems.shape[0] - 1
    each = owned // parts
    loads = [pltpu.make_async_copy(rhs_hbm, left_ref, sems.at[parts])]
    for part in range(parts):
        at = pl.ds(part * each, each)
        loads.append(pltpu.make_async_copy(precond_hbm.at[at], precond_ref.at[at], sems.at[part]))
    for load in loads:
        load.start()
    loads[0].wait()
    for part in range(parts):
        loads[1 + part].wait()
        for p in range(part * each, (part + 1) * each):
            high, low = split(precond_ref[p])
            high_ref[p] = high
            low_ref[p] = low
            value = times_block(left_ref[p], high, low)
            sol_ref[p] = value
            put_rounded(p, value, whole_ref, part_refs)


def apply_kernel(part, parts, pieces, high_ref, low_ref, left_ref, sol_ref, base_ref, *refs):
    piece_refs, refs = refs[:pieces], refs[pieces:]
    earlier_refs, refs = refs[:-3 - (part == parts - 1)], refs[-3 - (part == parts - 1):]
    new_ref, new_left_ref, rounded_ref, *whole_refs = refs
    each = rounded_ref.shape[0]
    for whole_ref in whole_refs:
        for index, earlier_ref in enumerate(earlier_refs):
            whole_ref[pl.ds(index * each, each)] = earlier_ref[...]
    for inner in range(each):
        p = part * each + inner
        received = sum(piece_ref[p].astype(jnp.float32) for piece_ref in piece_refs)
        value = sol_ref[p] + times_block(base_ref[p] - received, high_ref[p], low_ref[p])
        new_ref[p] = value
        new_left_ref[p] = left_ref[p] - received
        for out_ref, at in [(rounded_ref, inner)] + [(whole_ref, p) for whole_ref in whole_refs]:
            out_ref[at] = value.astype(jnp.bfloat16)


def finish_kernel(pieces, high_ref, low_ref, sol_ref, base_ref, *refs):
    piece_refs, (out_hbm, value_ref, sems) = refs[:pieces], refs[pieces:]
    owned = sol_ref.shape[0]
    parts = sems.shape[0]
    each = owned // parts
    stores = []
    for part in range(parts):
        for p in range(part * each, (part + 1) * each):
            received = sum(piece_ref[p].astype(jnp.float32) for piece_ref in piece_refs)
            value_ref[p] = sol_ref[p] + times_block(base_ref[p] - received, high_ref[p], low_ref[p])
        at = pl.ds(part * each, each)
        stores.append(pltpu.make_async_copy(value_ref.at[at], out_hbm.at[at], sems.at[part]))
        stores[-1].start()
    for store in stores:
        store.wait()


def order_kernel(group, owned, groups, parts, stages, bits, count_ref, rows_hbm, cols_hbm, values_hbm,
                 list_out, total_out, values_out, token_ref, rows_ref, cols_ref, first_ref, base_ref, total_ref,
                 sems):
    token_ref[...] = jnp.zeros_like(token_ref)
    loads = [
        pltpu.make_async_copy(rows_hbm, rows_ref, sems.at[0]),
        pltpu.make_async_copy(cols_hbm, cols_ref, sems.at[1]),
        pltpu.make_async_copy(values_hbm, values_out, sems.at[2]),
    ]
    for load in loads:
        load.start()
    other = 1 - (lax.axis_index("row") & (CORES - 1))
    mine = lax.axis_index("col")
    row_bits, col_bits = bits
    lists = len(stages) * CORES
    each = owned // parts
    trash = (group // CORES) << col_bits
    places = {
        piece: (index * CORES, place * each) for index, stage in enumerate(stages) for place, piece in enumerate(stage)
    }
    own_rows = lax.axis_index("row") * owned
    for source in range(groups):
        piece = relative(mine, source, groups)
        for part in range(parts):
            first, base = places[0, part]
            for index in range(1, groups):
                first = jnp.where(piece == index, places[index, part][0], first)
                base = jnp.where(piece == index, places[index, part][1], base)
            at = halves(source * group + own_rows + part * each, each)[0]
            first_ref[at] = first
            base_ref[at] = base
    for index in range(lists + 1):
        total_ref[index] = 0
    for load in loads[:2]:
        load.wait()
    used = count_ref[0, 0]

    def place(chunk, carry):
        entries = []
        for lane in range(LANES):
            slot = chunk * LANES + lane
            owner, row_inner = halves(halves(rows_ref[0, 0, slot], group)[1], owned)
            at, inner = halves(cols_ref[0, 0, slot], each)
            half = (owner & (CORES - 1)) ^ other
            which = jnp.where(slot < used, first_ref[at] + half, lists)
            row = lax.shift_right_logical(owner, 1) * owned + row_inner
            col = base_ref[at] + inner
            entries.append((which, (((slot << row_bits) | row) << col_bits) | col))
        for which, entry in entries:
            at = total_ref[which]
            list_out[which, at] = entry
            total_ref[which] = at + 1
        return carry

    lax.fori_loop(0, lax.div(used + LANES - 1, LANES), place, 0)
    for index in range(lists):
        total_out[index] = total_ref[index]

    def close(index, carry):
        for extra in range(UNROLL):
            list_out[index, total_ref[index] + extra] = trash
        return carry

    lax.fori_loop(0, lists, close, 0)
    loads[2].wait()


def turn_kernel(total_ref, values_ref, base_ref, turned_ref, same_ref):
    used = sum(total_ref[index] for index in range(total_ref.shape[0]))

    def turn(chunk, carry):
        for lane in range(LANES):
            turned_ref[chunk * LANES + lane] = values_ref[chunk * LANES + lane].T
        return carry

    lax.fori_loop(0, lax.div(used + LANES - 1, LANES), turn, 0)


def add_products(which, bits, dims, list_ref, total_ref, values_ref, field_ref, total):
    row_bits, col_bits = bits

    def step(chunk, carry):
        terms = []

        def store(row, term):
            total[row] += term

        for lane in range(UNROLL):
            entry = list_ref[which, chunk * UNROLL + lane]
            col = entry & ((1 << col_bits) - 1)
            row = lax.shift_right_logical(entry, col_bits) & ((1 << row_bits) - 1)
            slot = lax.shift_right_logical(entry, col_bits + row_bits)
            term = lax.dot_general(field_ref[col], values_ref[slot], dims, preferred_element_type=jnp.float32)
            terms.append((row, term))
            if len(terms) > DEPTH:
                store(*terms.pop(0))
        for row, term in terms:
            store(row, term)
        return carry

    lax.fori_loop(0, lax.div(total_ref[which] + UNROLL - 1, UNROLL), step, 0)


def join(pieces, field):
    if len(pieces) == 1:
        return pieces[0]
    at = 0
    for piece in pieces:
        field[pl.ds(at, piece.shape[0])] = piece[...]
        at += piece.shape[0]
    return field


def swap_order(chips):
    return list(reversed(range(chips)))


def swapped_early(chips):
    return chips - 1


def swapped_rows(index, chips, owned, first_ref, rest_ref):
    early = swapped_early(chips)
    if index < early:
        return first_ref[pl.ds(index * owned, owned)]
    return rest_ref[pl.ds((index - early) * owned, owned)]


def first_kernel(pieces, steps, chips, bits, dims, list_ref, total_ref, values_ref, *refs):
    piece_refs, refs = refs[:pieces], refs[pieces:]
    out_refs, refs = refs[:2 * steps], refs[2 * steps:]
    in_refs, refs = refs[:2 * steps], refs[2 * steps:]
    sent_refs, totals, (token_ref, field) = refs[:-CORES - 2], refs[-CORES - 2:-2], refs[-2:]
    field_ref = join(piece_refs, field)
    token_ref[...] = jnp.zeros_like(token_ref)
    chip = lax.axis_index("row") // CORES
    for half, total in enumerate(totals):
        rows = total.shape[0] - 1
        owned = rows // chips
        if steps == 0:
            total[...] = jnp.zeros(total.shape, jnp.float32)
        else:
            for index, shift in enumerate(swap_order(chips)):
                swapped = in_refs if half else out_refs
                value = sum(
                    swapped_rows(index, chips, owned, *swapped[2 * step:2 * step + 2]).astype(jnp.float32)
                    for step in range(steps))
                if half == 0:
                    value = -value
                elif shift > 0:
                    for step in range(steps):
                        value -= sent_refs[step * (chips - 1) + index][...].astype(jnp.float32)
                total[pl.ds(partner(chip, shift, chips) * owned, owned)] = value
        add_products(half, bits, dims, list_ref, total_ref, values_ref, field_ref, total)


def stage_kernel(stage, bits, dims, pieces, list_ref, total_ref, values_ref, *refs):
    piece_refs, refs = refs[:pieces], refs[pieces + CORES:]
    totals, field = refs[:CORES], refs[-1]
    field_ref = join(piece_refs, field)
    for half, total in enumerate(totals):
        add_products(stage * CORES + half, bits, dims, list_ref, total_ref, values_ref, field_ref, total)


def last_kernel(stage, half, bits, dims, pieces, chips, list_ref, total_ref, values_ref, *refs):
    piece_refs, refs = refs[:pieces], refs[pieces + 1:]
    if half == 0:
        total, out_ref, field = refs
        other = total
    else:
        other, total, out_ref, field = refs
    field_ref = join(piece_refs, field)
    add_products(stage * CORES + half, bits, dims, list_ref, total_ref, values_ref, field_ref, total)
    chip = lax.axis_index("row") // CORES
    owned = (other.shape[0] - 1) // chips
    shifts, early = swap_order(chips), swapped_early(chips)
    for index, shift in enumerate(shifts[early:] if half else shifts[:early]):
        rows = other[pl.ds(partner(chip, shift, chips) * owned, owned)]
        out_ref[pl.ds(index * owned, owned)] = rows.astype(out_ref.dtype)


def chip_rows(index, chips, owned, own_ref, *other_refs):
    chip = lax.axis_index("row") // CORES
    at = pl.ds(partner(chip, swap_order(chips)[index], chips) * owned, owned)
    return own_ref[at] + swapped_rows(index, chips, owned, *other_refs).astype(jnp.float32)


def combine_first_kernel(chips, own_ref, first_ref, *send_refs):
    for index, send_ref in enumerate(send_refs):
        rows = chip_rows(index, chips, send_ref.shape[0], own_ref, first_ref, None)
        send_ref[...] = rows.astype(send_ref.dtype)


def combine_rest_kernel(chips, own_ref, rest_ref, left_ref, sol_ref, before_ref, base_ref, *send_refs):
    owned = base_ref.shape[0]
    for index, send_ref in enumerate(send_refs):
        rows = chip_rows(swapped_early(chips) + index, chips, owned, own_ref, None, rest_ref)
        send_ref[...] = rows.astype(send_ref.dtype)
    keep = chip_rows(chips - 1, chips, owned, own_ref, None, rest_ref)
    base_ref[...] = left_ref[...] - sol_ref[...] - keep


def per_device(block_values, block_rows, block_cols, block_counts, precond, right_side):
    owned, rhs, size = right_side.shape[1:]
    row_devices = lax.axis_size("row")
    groups = lax.axis_size("col")
    chips = row_devices // CORES
    group = owned * row_devices
    half_rows = chips * owned
    slots = block_values.shape[2]

    parts = 2 if owned % 2 == 0 else 1
    stages = gather_stages(groups, parts)
    final = len(stages) - 1
    lists_total = len(stages) * CORES
    widest = max(len(stage) for stage in stages) * owned // parts
    row_bits, col_bits = bits = half_rows.bit_length(), (widest - 1).bit_length()
    assert (slots - 1).bit_length() + row_bits + col_bits <= 31
    assert slots % LANES == 0

    field_type = jax.ShapeDtypeStruct((owned, rhs, size), jnp.float32)
    matrix_type = jax.ShapeDtypeStruct((owned, size, size), jnp.bfloat16)
    total_type = jax.ShapeDtypeStruct((half_rows + 1, rhs, size), jnp.float32)
    index_type = pltpu.SMEM(block_rows.shape, jnp.int32)
    token_type = jax.ShapeDtypeStruct((8, 128), jnp.float32)
    loads = next(count for count in (4, 2, 1) if owned % count == 0)
    rounded_type = jax.ShapeDtypeStruct((owned, rhs, size), jnp.bfloat16)
    part_type = jax.ShapeDtypeStruct((owned // parts, rhs, size), jnp.bfloat16)

    high, low, sol, left, whole, *rounded = pl.pallas_call(
        start_kernel,
        out_shape=[matrix_type] * 2 + [field_type] * 2 + [rounded_type] + [part_type] * parts,
        in_specs=[in_hbm()] * 2,
        out_specs=[in_vmem()] * (5 + parts),
        scratch_shapes=[
            pltpu.VMEM((owned, size, size), jnp.float32),
            pltpu.SemaphoreType.DMA((loads + 1,)),
        ],
        compiler_params=params(),
        name="start",
    )(stay_in_hbm(precond[0]), stay_in_hbm(right_side[0]))

    *lists, values, order_token = pl.pallas_call(
        functools.partial(order_kernel, group, owned, groups, parts, stages, bits),
        out_shape=[
            pltpu.SMEM((lists_total + 1, slots + UNROLL), jnp.int32),
            pltpu.SMEM((lists_total,), jnp.int32),
            pltpu.VMEM(block_values.shape[2:], block_values.dtype),
            token_type,
        ],
        in_specs=[in_smem()] + [in_hbm()] * 3,
        out_specs=[in_smem()] * 2 + [in_vmem()] * 2,
        scratch_shapes=[
            index_type, index_type,
            pltpu.SMEM((groups * row_devices * parts,), jnp.int32),
            pltpu.SMEM((groups * row_devices * parts,), jnp.int32),
            pltpu.SMEM((lists_total + 1,), jnp.int32),
            pltpu.SemaphoreType.DMA((3,)),
        ],
        compiler_params=params(),
        name="order",
    )(block_counts, *[stay_in_hbm(array) for array in (block_rows, block_cols, block_values[0, 0])])

    def turn(values, base):
        return pl.pallas_call(
            turn_kernel,
            out_shape=[pltpu.VMEM(values.shape, values.dtype), field_type],
            in_specs=[in_smem()] + [in_vmem()] * 2,
            out_specs=[in_vmem()] * 2,
            input_output_aliases={2: 1},
            compiler_params=params(),
            cost_estimate=pl.CostEstimate(flops=HIDE_FLOPS, bytes_accessed=0, transcendentals=0),
            name="turn",
        )(lists[1], values, base)

    def cost(share):
        return pl.CostEstimate(
            flops=int(slots * share) * 2 * rhs * size * size,
            bytes_accessed=int(slots * share) * 2 * size * size, transcendentals=0)

    def field_scratch(pieces):
        return pltpu.VMEM((sum(piece.shape[0] for piece in pieces), rhs, size), jnp.bfloat16)

    def product_first(values, dims, pieces, outs, ins, sent):
        return pl.pallas_call(
            functools.partial(first_kernel, len(pieces), len(outs) // 2, chips, bits, dims),
            out_shape=[total_type] * CORES + [token_type],
            in_specs=[in_smem()] * 2 + [in_vmem()] * (1 + len(pieces) + len(outs) + len(ins) + len(sent)),
            out_specs=[in_vmem()] * (CORES + 1),
            compiler_params=params(),
            scratch_shapes=[field_scratch(pieces)],
            cost_estimate=cost(len(stages[0]) / groups / parts),
            name="stage0",
        )(*lists, values, *pieces, *outs, *ins, *sent)

    def product_stage(values, dims, stage, pieces, totals):
        inputs = 3 + len(pieces)
        return pl.pallas_call(
            functools.partial(stage_kernel, stage, bits, dims, len(pieces)),
            out_shape=[total_type] * CORES,
            in_specs=[in_smem()] * 2 + [in_vmem()] * (1 + len(pieces) + CORES),
            out_specs=[in_vmem()] * CORES,
            scratch_shapes=[field_scratch(pieces)],
            input_output_aliases={inputs + half: half for half in range(CORES)},
            compiler_params=params(),
            cost_estimate=cost(len(stages[stage]) / groups / parts),
            name="stage%d" % stage,
        )(*lists, values, *pieces, *totals)

    def product_last(values, dims, half, pieces, total, *other):
        send_chips = chips - swapped_early(chips) if half else swapped_early(chips)
        return pl.pallas_call(
            functools.partial(last_kernel, final, half, bits, dims, len(pieces), chips),
            out_shape=[total_type, jax.ShapeDtypeStruct((send_chips * owned, rhs, size), jnp.bfloat16)],
            in_specs=[in_smem()] * 2 + [in_vmem()] * (2 + len(pieces) + len(other)),
            out_specs=[in_vmem()] * 2,
            scratch_shapes=[field_scratch(pieces)],
            input_output_aliases={3 + len(pieces): 0},
            compiler_params=params(),
            cost_estimate=pl.CostEstimate(
                flops=HIDE_FLOPS if half else 0, bytes_accessed=0, transcendentals=0),
            name="last%d" % half,
        )(*lists, values, *pieces, total, *other)

    def hold(piece, token):
        return pl.pallas_call(
            hold_kernel,
            out_shape=part_type,
            in_specs=[in_vmem()] * 2,
            out_specs=in_vmem(),
            input_output_aliases={0: 0},
            compiler_params=params(),
            name="hold",
        )(piece, token)

    early = swapped_early(chips)

    def combine_first(own, first):
        return pl.pallas_call(
            functools.partial(combine_first_kernel, chips),
            out_shape=[rounded_type] * early,
            in_specs=[in_vmem()] * 2,
            out_specs=[in_vmem()] * early,
            compiler_params=params(),
            name="combine0",
        )(own, first)

    def combine_rest(own, rest, left, sol, before):
        return pl.pallas_call(
            functools.partial(combine_rest_kernel, chips),
            out_shape=[field_type] + [rounded_type] * (chips - 1 - early),
            in_specs=[in_vmem()] * 5,
            out_specs=[in_vmem()] * (chips - early),
            compiler_params=params(),
            name="combine1",
        )(own, rest, left, sol, before)

    def apply(part, sol, left, base, pieces, earlier):
        last = part == parts - 1
        return pl.pallas_call(
            functools.partial(apply_kernel, part, parts, len(pieces)),
            out_shape=[field_type, field_type, part_type] + [rounded_type] * last,
            in_specs=[in_vmem()] * (5 + len(pieces) + len(earlier)),
            out_specs=[in_vmem()] * (3 + last),
            input_output_aliases={2: 1, 3: 0},
            compiler_params=params(),
            cost_estimate=pl.CostEstimate(flops=HIDE_FLOPS, bytes_accessed=0, transcendentals=0),
            name="apply%d" % part,
        )(high, low, left, sol, base, *pieces, *earlier)

    blocks = values, NT
    outs, ins, sent = [], [], []
    for step in range(ITERS):
        sets = gather(whole, rounded, groups)

        def stage_pieces(stage):
            return [sets[piece] for piece in stages[stage] if piece in sets]

        *totals, token = product_first(*blocks, stage_pieces(0), outs, ins, sent)
        if groups % 2 == 0:
            for part in range(parts - 1):
                for index in range(1, groups // 2):
                    sets[index, part] = hold(sets[index, part], token)
                    sets[groups // 2 + index, part] = lax.ppermute(sets[index, part], "col", neighbours(groups))
        for stage in range(1, final):
            totals = product_stage(*blocks, stage, stage_pieces(stage), totals)
        other, out_first = product_last(*blocks, 0, stage_pieces(final), totals[0])
        own, out_rest = product_last(*blocks, 1, stage_pieces(final), totals[1], other)
        outgoing = [out_first, out_rest]
        incoming = [lax.ppermute(rows, "row", neighbours(row_devices)) for rows in outgoing]
        outs += outgoing
        ins += incoming
        first = combine_first(own, incoming[0])
        base, *rest = combine_rest(own, incoming[1], left, sol, first[-1])
        sends = list(first) + rest
        sent += sends
        pieces = [
            lax.ppermute(send, "row", [
                (chip * CORES + core, partner(chip, shift, chips) * CORES + core)
                for chip in range(chips) for core in range(CORES)
            ])
            for shift, send in zip(swap_order(chips), sends)
        ]
        if step == 0:
            turned, base = turn(values, base)
            blocks = turned, NN
        if step < ITERS - 1:
            rounded = []
            for part in range(parts):
                sol, left, new, *done = apply(part, sol, left, base, pieces, rounded if part == parts - 1 else [])
                rounded.append(new)
            whole, = done
    return pl.pallas_call(
        functools.partial(finish_kernel, len(pieces)),
        out_shape=field_type,
        in_specs=[in_vmem()] * (4 + len(pieces)),
        out_specs=in_hbm(),
        scratch_shapes=[
            pltpu.VMEM((owned, rhs, size), jnp.float32),
            pltpu.SemaphoreType.DMA((2 if owned % 2 == 0 else 1,)),
        ],
        compiler_params=params(),
        name="finish",
    )(high, low, sol, base, *pieces)[None]


def solution(mesh):
    placed = (
        P("row", "col", None, None, None),
        P("row", "col", None),
        P("row", "col", None),
        P("row", "col"),
        P("col", "row", None, None),
        P("col", "row", None, None),
    )
    return jax.shard_map(
        per_device,
        mesh=mesh,
        in_specs=placed,
        out_specs=P("col", "row", None, None),
        check_vma=False,
    )
```

```python
import functools

import jax
import jax.numpy as jnp
from jax import lax
from jax.experimental import pallas as pl
from jax.experimental.pallas import tpu as pltpu
from jax.sharding import PartitionSpec as P

ITERS = 3
UNROLL = 16
LANES = 4
DEPTH = 6
HIDE_FLOPS = 20_000_000_000
CORES = 2
VMEM_LIMIT = 24 * 1024 * 1024

NT = (((1,), (1,)), ((), ()))
NN = (((1,), (0,)), ((), ()))


def in_vmem():
    return pl.BlockSpec(memory_space=pltpu.VMEM)


def in_hbm():
    return pl.BlockSpec(memory_space=pltpu.HBM)


def in_smem():
    return pl.BlockSpec(memory_space=pltpu.SMEM)


def stay_in_hbm(array):
    return pltpu.with_memory_space_constraint(array, pltpu.HBM)


def params():
    return pltpu.CompilerParams(vmem_limit_bytes=VMEM_LIMIT)


def split(value):
    high = value.astype(jnp.bfloat16)
    low = (value - high.astype(jnp.float32)).astype(jnp.bfloat16)
    return high, low


def times_block(field, high, low):
    field_high, field_low = split(field)
    rhs = field.shape[0]
    both = jnp.concatenate([field_high, field_low], axis=0)
    first = lax.dot_general(both, high, NT, preferred_element_type=jnp.float32)
    second = lax.dot_general(field_high, low, NT, preferred_element_type=jnp.float32)
    return first[:rhs] + (first[rhs:] + second)


def partner(chip, shift, chips):
    if chips & (chips - 1) == 0:
        return chip ^ shift
    return (chip + shift) % chips


def halves(value, size):
    if size & (size - 1) == 0:
        return lax.shift_right_logical(value, size.bit_length() - 1), value & (size - 1)
    return lax.div(value, size), lax.rem(value, size)


def relative(mine, source, groups):
    if groups % 2:
        away = mine - source
        return jnp.where(away < 0, away + groups, away)
    other = (mine ^ source) & 1
    away = (mine ^ other) - source
    away = jnp.where(away < 0, away + groups, away)
    return other * (groups // 2) + lax.shift_right_logical(away, 1)


def gather_stages(groups, parts):
    every = range(parts)
    own = [(0, part) for part in every]
    if groups % 2:
        return [own, [(index, part) for index in range(1, groups) for part in every]]
    pairs = groups // 2
    early = range(parts - 1)
    far, forwarded = range(1, pairs), range(pairs + 1, groups)
    stages = [
        own + [(index, part) for part in early for index in far],
        [(index, parts - 1) for index in far],
        [(pairs, part) for part in every] + [(index, part) for part in early for index in forwarded],
        [(index, parts - 1) for index in forwarded],
    ]
    return [stage for stage in stages if stage]


def ring(groups, step):
    return [(c, (c + step) % groups) for c in range(groups)]


def gather(whole, rounded, groups):
    sets = {(0, 0): whole}
    if groups % 2:
        for step in range(1, groups):
            sets[step, 0] = lax.ppermute(whole, "col", ring(groups, step))
        return sets
    for part, piece in enumerate(rounded):
        for step in range(1, groups // 2):
            sets[step, part] = lax.ppermute(piece, "col", ring(groups, 2 * step))
    sets[groups // 2, 0] = lax.ppermute(whole, "col", neighbours(groups))
    for step in range(1, groups // 2):
        across = [(c, ((c + 2 * step) % groups) ^ 1) for c in range(groups)]
        sets[groups // 2 + step, len(rounded) - 1] = lax.ppermute(rounded[-1], "col", across)
    return sets


def neighbours(count):
    return [(index, index ^ 1) for index in range(count)]


def hold_kernel(piece_ref, token_ref, out_ref):
    pass


def put_rounded(p, value, whole_ref, part_refs):
    part, inner = divmod(p, part_refs[0].shape[0])
    rounded = value.astype(jnp.bfloat16)
    whole_ref[p] = rounded
    part_refs[part][inner] = rounded


def start_kernel(precond_hbm, rhs_hbm, high_ref, low_ref, sol_ref, left_ref, whole_ref, *refs):
    part_refs, (precond_ref, sems) = refs[:-2], refs[-2:]
    owned = left_ref.shape[0]
    parts = sems.shape[0] - 1
    each = owned // parts
    loads = [pltpu.make_async_copy(rhs_hbm, left_ref, sems.at[parts])]
    for part in range(parts):
        at = pl.ds(part * each, each)
        loads.append(pltpu.make_async_copy(precond_hbm.at[at], precond_ref.at[at], sems.at[part]))
    for load in loads:
        load.start()
    loads[0].wait()
    for part in range(parts):
        loads[1 + part].wait()
        for p in range(part * each, (part + 1) * each):
            high, low = split(precond_ref[p])
            high_ref[p] = high
            low_ref[p] = low
            value = times_block(left_ref[p], high, low)
            sol_ref[p] = value
            put_rounded(p, value, whole_ref, part_refs)


def apply_kernel(part, parts, pieces, high_ref, low_ref, left_ref, sol_ref, base_ref, *refs):
    piece_refs, refs = refs[:pieces], refs[pieces:]
    earlier_refs, refs = refs[:-3 - (part == parts - 1)], refs[-3 - (part == parts - 1):]
    new_ref, new_left_ref, rounded_ref, *whole_refs = refs
    each = rounded_ref.shape[0]
    for whole_ref in whole_refs:
        for index, earlier_ref in enumerate(earlier_refs):
            whole_ref[pl.ds(index * each, each)] = earlier_ref[...]
    for inner in range(each):
        p = part * each + inner
        received = sum(piece_ref[p].astype(jnp.float32) for piece_ref in piece_refs)
        value = sol_ref[p] + times_block(base_ref[p] - received, high_ref[p], low_ref[p])
        new_ref[p] = value
        new_left_ref[p] = left_ref[p] - received
        for out_ref, at in [(rounded_ref, inner)] + [(whole_ref, p) for whole_ref in whole_refs]:
            out_ref[at] = value.astype(jnp.bfloat16)


def finish_kernel(pieces, high_ref, low_ref, sol_ref, base_ref, *refs):
    piece_refs, (out_hbm, value_ref, sems) = refs[:pieces], refs[pieces:]
    owned = sol_ref.shape[0]
    parts = sems.shape[0]
    each = owned // parts
    stores = []
    for part in range(parts):
        for p in range(part * each, (part + 1) * each):
            received = sum(piece_ref[p].astype(jnp.float32) for piece_ref in piece_refs)
            value_ref[p] = sol_ref[p] + times_block(base_ref[p] - received, high_ref[p], low_ref[p])
        at = pl.ds(part * each, each)
        stores.append(pltpu.make_async_copy(value_ref.at[at], out_hbm.at[at], sems.at[part]))
        stores[-1].start()
    for store in stores:
        store.wait()


def order_kernel(group, owned, groups, parts, stages, bits, count_ref, rows_hbm, cols_hbm, values_hbm,
                 list_out, total_out, values_out, token_ref, rows_ref, cols_ref, first_ref, base_ref, total_ref,
                 sems):
    token_ref[...] = jnp.zeros_like(token_ref)
    loads = [
        pltpu.make_async_copy(rows_hbm, rows_ref, sems.at[0]),
        pltpu.make_async_copy(cols_hbm, cols_ref, sems.at[1]),
        pltpu.make_async_copy(values_hbm, values_out, sems.at[2]),
    ]
    for load in loads:
        load.start()
    other = 1 - (lax.axis_index("row") & (CORES - 1))
    mine = lax.axis_index("col")
    row_bits, col_bits = bits
    lists = len(stages) * CORES
    each = owned // parts
    trash = (group // CORES) << col_bits
    places = {
        piece: (index * CORES, place * each) for index, stage in enumerate(stages) for place, piece in enumerate(stage)
    }
    own_rows = lax.axis_index("row") * owned
    for source in range(groups):
        piece = relative(mine, source, groups)
        for part in range(parts):
            first, base = places[0, part]
            for index in range(1, groups):
                first = jnp.where(piece == index, places[index, part][0], first)
                base = jnp.where(piece == index, places[index, part][1], base)
            at = halves(source * group + own_rows + part * each, each)[0]
            first_ref[at] = first
            base_ref[at] = base
    for index in range(lists + 1):
        total_ref[index] = 0
    for load in loads[:2]:
        load.wait()
    used = count_ref[0, 0]

    def place(chunk, carry):
        entries = []
        for lane in range(LANES):
            slot = chunk * LANES + lane
            owner, row_inner = halves(halves(rows_ref[0, 0, slot], group)[1], owned)
            at, inner = halves(cols_ref[0, 0, slot], each)
            half = (owner & (CORES - 1)) ^ other
            which = jnp.where(slot < used, first_ref[at] + half, lists)
            row = lax.shift_right_logical(owner, 1) * owned + row_inner
            col = base_ref[at] + inner
            entries.append((which, (((slot << row_bits) | row) << col_bits) | col))
        for which, entry in entries:
            at = total_ref[which]
            list_out[which, at] = entry
            total_ref[which] = at + 1
        return carry

    lax.fori_loop(0, lax.div(used + LANES - 1, LANES), place, 0)
    for index in range(lists):
        total_out[index] = total_ref[index]

    def close(index, carry):
        for extra in range(UNROLL):
            list_out[index, total_ref[index] + extra] = trash
        return carry

    lax.fori_loop(0, lists, close, 0)
    loads[2].wait()


def turn_kernel(total_ref, values_ref, base_ref, turned_ref, same_ref):
    used = sum(total_ref[index] for index in range(total_ref.shape[0]))

    def turn(chunk, carry):
        for lane in range(LANES):
            turned_ref[chunk * LANES + lane] = values_ref[chunk * LANES + lane].T
        return carry

    lax.fori_loop(0, lax.div(used + LANES - 1, LANES), turn, 0)


def add_products(which, bits, dims, list_ref, total_ref, values_ref, field_ref, total):
    row_bits, col_bits = bits

    def step(chunk, carry):
        terms = []

        def store(row, term):
            total[row] += term

        for lane in range(UNROLL):
            entry = list_ref[which, chunk * UNROLL + lane]
            col = entry & ((1 << col_bits) - 1)
            row = lax.shift_right_logical(entry, col_bits) & ((1 << row_bits) - 1)
            slot = lax.shift_right_logical(entry, col_bits + row_bits)
            term = lax.dot_general(field_ref[col], values_ref[slot], dims, preferred_element_type=jnp.float32)
            terms.append((row, term))
            if len(terms) > DEPTH:
                store(*terms.pop(0))
        for row, term in terms:
            store(row, term)
        return carry

    lax.fori_loop(0, lax.div(total_ref[which] + UNROLL - 1, UNROLL), step, 0)


def join(pieces, field):
    if len(pieces) == 1:
        return pieces[0]
    at = 0
    for piece in pieces:
        field[pl.ds(at, piece.shape[0])] = piece[...]
        at += piece.shape[0]
    return field


def swap_order(chips):
    return list(reversed(range(chips)))


def swapped_early(chips):
    return chips - 1


def swapped_rows(index, chips, owned, first_ref, rest_ref):
    early = swapped_early(chips)
    if index < early:
        return first_ref[pl.ds(index * owned, owned)]
    return rest_ref[pl.ds((index - early) * owned, owned)]


def first_kernel(pieces, steps, chips, bits, dims, list_ref, total_ref, values_ref, *refs):
    piece_refs, refs = refs[:pieces], refs[pieces:]
    out_refs, refs = refs[:2 * steps], refs[2 * steps:]
    in_refs, refs = refs[:2 * steps], refs[2 * steps:]
    sent_refs, totals, (token_ref, field) = refs[:-CORES - 2], refs[-CORES - 2:-2], refs[-2:]
    field_ref = join(piece_refs, field)
    token_ref[...] = jnp.zeros_like(token_ref)
    chip = lax.axis_index("row") // CORES
    for half, total in enumerate(totals):
        rows = total.shape[0] - 1
        owned = rows // chips
        if steps == 0:
            total[...] = jnp.zeros(total.shape, jnp.float32)
        else:
            for index, shift in enumerate(swap_order(chips)):
                swapped = in_refs if half else out_refs
                value = sum(
                    swapped_rows(index, chips, owned, *swapped[2 * step:2 * step + 2]).astype(jnp.float32)
                    for step in range(steps))
                if half == 0:
                    value = -value
                elif shift > 0:
                    for step in range(steps):
                        value -= sent_refs[step * (chips - 1) + index][...].astype(jnp.float32)
                total[pl.ds(partner(chip, shift, chips) * owned, owned)] = value
        add_products(half, bits, dims, list_ref, total_ref, values_ref, field_ref, total)


def stage_kernel(stage, bits, dims, pieces, list_ref, total_ref, values_ref, *refs):
    piece_refs, refs = refs[:pieces], refs[pieces + CORES:]
    totals, field = refs[:CORES], refs[-1]
    field_ref = join(piece_refs, field)
    for half, total in enumerate(totals):
        add_products(stage * CORES + half, bits, dims, list_ref, total_ref, values_ref, field_ref, total)


def last_kernel(stage, half, bits, dims, pieces, chips, list_ref, total_ref, values_ref, *refs):
    piece_refs, refs = refs[:pieces], refs[pieces + 1:]
    if half == 0:
        total, out_ref, field = refs
        other = total
    else:
        other, total, out_ref, field = refs
    field_ref = join(piece_refs, field)
    add_products(stage * CORES + half, bits, dims, list_ref, total_ref, values_ref, field_ref, total)
    chip = lax.axis_index("row") // CORES
    owned = (other.shape[0] - 1) // chips
    shifts, early = swap_order(chips), swapped_early(chips)
    for index, shift in enumerate(shifts[early:] if half else shifts[:early]):
        rows = other[pl.ds(partner(chip, shift, chips) * owned, owned)]
        out_ref[pl.ds(index * owned, owned)] = rows.astype(out_ref.dtype)


def chip_rows(index, chips, owned, own_ref, *other_refs):
    chip = lax.axis_index("row") // CORES
    at = pl.ds(partner(chip, swap_order(chips)[index], chips) * owned, owned)
    return own_ref[at] + swapped_rows(index, chips, owned, *other_refs).astype(jnp.float32)


def combine_first_kernel(chips, own_ref, first_ref, *send_refs):
    for index, send_ref in enumerate(send_refs):
        rows = chip_rows(index, chips, send_ref.shape[0], own_ref, first_ref, None)
        send_ref[...] = rows.astype(send_ref.dtype)


def combine_rest_kernel(chips, own_ref, rest_ref, left_ref, sol_ref, before_ref, base_ref, *send_refs):
    owned = base_ref.shape[0]
    for index, send_ref in enumerate(send_refs):
        rows = chip_rows(swapped_early(chips) + index, chips, owned, own_ref, None, rest_ref)
        send_ref[...] = rows.astype(send_ref.dtype)
    keep = chip_rows(chips - 1, chips, owned, own_ref, None, rest_ref)
    base_ref[...] = left_ref[...] - sol_ref[...] - keep


def per_device(block_values, block_rows, block_cols, block_counts, precond, right_side):
    owned, rhs, size = right_side.shape[1:]
    row_devices = lax.axis_size("row")
    groups = lax.axis_size("col")
    chips = row_devices // CORES
    group = owned * row_devices
    half_rows = chips * owned
    slots = block_values.shape[2]

    parts = 2 if owned % 2 == 0 else 1
    stages = gather_stages(groups, parts)
    final = len(stages) - 1
    lists_total = len(stages) * CORES
    widest = max(len(stage) for stage in stages) * owned // parts
    row_bits, col_bits = bits = half_rows.bit_length(), (widest - 1).bit_length()
    assert (slots - 1).bit_length() + row_bits + col_bits <= 31
    assert slots % LANES == 0

    field_type = jax.ShapeDtypeStruct((owned, rhs, size), jnp.float32)
    matrix_type = jax.ShapeDtypeStruct((owned, size, size), jnp.bfloat16)
    total_type = jax.ShapeDtypeStruct((half_rows + 1, rhs, size), jnp.float32)
    index_type = pltpu.SMEM(block_rows.shape, jnp.int32)
    token_type = jax.ShapeDtypeStruct((8, 128), jnp.float32)
    loads = next(count for count in (4, 2, 1) if owned % count == 0)
    rounded_type = jax.ShapeDtypeStruct((owned, rhs, size), jnp.bfloat16)
    part_type = jax.ShapeDtypeStruct((owned // parts, rhs, size), jnp.bfloat16)

    high, low, sol, left, whole, *rounded = pl.pallas_call(
        start_kernel,
        out_shape=[matrix_type] * 2 + [field_type] * 2 + [rounded_type] + [part_type] * parts,
        in_specs=[in_hbm()] * 2,
        out_specs=[in_vmem()] * (5 + parts),
        scratch_shapes=[
            pltpu.VMEM((owned, size, size), jnp.float32),
            pltpu.SemaphoreType.DMA((loads + 1,)),
        ],
        compiler_params=params(),
        name="start",
    )(stay_in_hbm(precond[0]), stay_in_hbm(right_side[0]))

    *lists, values, order_token = pl.pallas_call(
        functools.partial(order_kernel, group, owned, groups, parts, stages, bits),
        out_shape=[
            pltpu.SMEM((lists_total + 1, slots + UNROLL), jnp.int32),
            pltpu.SMEM((lists_total,), jnp.int32),
            pltpu.VMEM(block_values.shape[2:], block_values.dtype),
            token_type,
        ],
        in_specs=[in_smem()] + [in_hbm()] * 3,
        out_specs=[in_smem()] * 2 + [in_vmem()] * 2,
        scratch_shapes=[
            index_type, index_type,
            pltpu.SMEM((groups * row_devices * parts,), jnp.int32),
            pltpu.SMEM((groups * row_devices * parts,), jnp.int32),
            pltpu.SMEM((lists_total + 1,), jnp.int32),
            pltpu.SemaphoreType.DMA((3,)),
        ],
        compiler_params=params(),
        name="order",
    )(block_counts, *[stay_in_hbm(array) for array in (block_rows, block_cols, block_values[0, 0])])

    def turn(values, base):
        return pl.pallas_call(
            turn_kernel,
            out_shape=[pltpu.VMEM(values.shape, values.dtype), field_type],
            in_specs=[in_smem()] + [in_vmem()] * 2,
            out_specs=[in_vmem()] * 2,
            input_output_aliases={2: 1},
            compiler_params=params(),
            cost_estimate=pl.CostEstimate(flops=HIDE_FLOPS, bytes_accessed=0, transcendentals=0),
            name="turn",
        )(lists[1], values, base)

    def cost(share):
        return pl.CostEstimate(
            flops=int(slots * share) * 2 * rhs * size * size,
            bytes_accessed=int(slots * share) * 2 * size * size, transcendentals=0)

    def field_scratch(pieces):
        return pltpu.VMEM((sum(piece.shape[0] for piece in pieces), rhs, size), jnp.bfloat16)

    def product_first(values, dims, pieces, outs, ins, sent):
        return pl.pallas_call(
            functools.partial(first_kernel, len(pieces), len(outs) // 2, chips, bits, dims),
            out_shape=[total_type] * CORES + [token_type],
            in_specs=[in_smem()] * 2 + [in_vmem()] * (1 + len(pieces) + len(outs) + len(ins) + len(sent)),
            out_specs=[in_vmem()] * (CORES + 1),
            compiler_params=params(),
            scratch_shapes=[field_scratch(pieces)],
            cost_estimate=cost(len(stages[0]) / groups / parts),
            name="stage0",
        )(*lists, values, *pieces, *outs, *ins, *sent)

    def product_stage(values, dims, stage, pieces, totals):
        inputs = 3 + len(pieces)
        return pl.pallas_call(
            functools.partial(stage_kernel, stage, bits, dims, len(pieces)),
            out_shape=[total_type] * CORES,
            in_specs=[in_smem()] * 2 + [in_vmem()] * (1 + len(pieces) + CORES),
            out_specs=[in_vmem()] * CORES,
            scratch_shapes=[field_scratch(pieces)],
            input_output_aliases={inputs + half: half for half in range(CORES)},
            compiler_params=params(),
            cost_estimate=cost(len(stages[stage]) / groups / parts),
            name="stage%d" % stage,
        )(*lists, values, *pieces, *totals)

    def product_last(values, dims, half, pieces, total, *other):
        send_chips = chips - swapped_early(chips) if half else swapped_early(chips)
        return pl.pallas_call(
            functools.partial(last_kernel, final, half, bits, dims, len(pieces), chips),
            out_shape=[total_type, jax.ShapeDtypeStruct((send_chips * owned, rhs, size), jnp.bfloat16)],
            in_specs=[in_smem()] * 2 + [in_vmem()] * (2 + len(pieces) + len(other)),
            out_specs=[in_vmem()] * 2,
            scratch_shapes=[field_scratch(pieces)],
            input_output_aliases={3 + len(pieces): 0},
            compiler_params=params(),
            cost_estimate=pl.CostEstimate(
                flops=HIDE_FLOPS if half else 0, bytes_accessed=0, transcendentals=0),
            name="last%d" % half,
        )(*lists, values, *pieces, total, *other)

    def hold(piece, token):
        return pl.pallas_call(
            hold_kernel,
            out_shape=part_type,
            in_specs=[in_vmem()] * 2,
            out_specs=in_vmem(),
            input_output_aliases={0: 0},
            compiler_params=params(),
            name="hold",
        )(piece, token)

    early = swapped_early(chips)

    def combine_first(own, first):
        return pl.pallas_call(
            functools.partial(combine_first_kernel, chips),
            out_shape=[rounded_type] * early,
            in_specs=[in_vmem()] * 2,
            out_specs=[in_vmem()] * early,
            compiler_params=params(),
            name="combine0",
        )(own, first)

    def combine_rest(own, rest, left, sol, before):
        return pl.pallas_call(
            functools.partial(combine_rest_kernel, chips),
            out_shape=[field_type] + [rounded_type] * (chips - 1 - early),
            in_specs=[in_vmem()] * 5,
            out_specs=[in_vmem()] * (chips - early),
            compiler_params=params(),
            name="combine1",
        )(own, rest, left, sol, before)

    def apply(part, sol, left, base, pieces, earlier):
        last = part == parts - 1
        return pl.pallas_call(
            functools.partial(apply_kernel, part, parts, len(pieces)),
            out_shape=[field_type, field_type, part_type] + [rounded_type] * last,
            in_specs=[in_vmem()] * (5 + len(pieces) + len(earlier)),
            out_specs=[in_vmem()] * (3 + last),
            input_output_aliases={2: 1, 3: 0},
            compiler_params=params(),
            cost_estimate=pl.CostEstimate(flops=HIDE_FLOPS, bytes_accessed=0, transcendentals=0),
            name="apply%d" % part,
        )(high, low, left, sol, base, *pieces, *earlier)

    blocks = values, NT
    outs, ins, sent = [], [], []
    for step in range(ITERS):
        sets = gather(whole, rounded, groups)

        def stage_pieces(stage):
            return [sets[piece] for piece in stages[stage] if piece in sets]

        def forward(part, token=None):
            for index in range(1, groups // 2):
                if token is not None:
                    sets[index, part] = hold(sets[index, part], token)
                sets[groups // 2 + index, part] = lax.ppermute(sets[index, part], "col", neighbours(groups))

        if groups % 2 == 0:
            for part in range(parts - 1):
                forward(part, order_token if step == 0 else None)
        *totals, _ = product_first(*blocks, stage_pieces(0), outs, ins, sent)

        for stage in range(1, final):
            totals = product_stage(*blocks, stage, stage_pieces(stage), totals)
        other, out_first = product_last(*blocks, 0, stage_pieces(final), totals[0])
        own, out_rest = product_last(*blocks, 1, stage_pieces(final), totals[1], other)
        outgoing = [out_first, out_rest]
        incoming = [lax.ppermute(rows, "row", neighbours(row_devices)) for rows in outgoing]
        outs += outgoing
        ins += incoming
        first = combine_first(own, incoming[0])
        base, *rest = combine_rest(own, incoming[1], left, sol, first[-1])
        sends = list(first) + rest
        sent += sends
        pieces = [
            lax.ppermute(send, "row", [
                (chip * CORES + core, partner(chip, shift, chips) * CORES + core)
                for chip in range(chips) for core in range(CORES)
            ])
            for shift, send in zip(swap_order(chips), sends)
        ]
        if step == 0:
            turned, base = turn(values, base)
            blocks = turned, NN
        if step < ITERS - 1:
            rounded = []
            for part in range(parts):
                sol, left, new, *done = apply(part, sol, left, base, pieces, rounded if part == parts - 1 else [])
                rounded.append(new)
            whole, = done
    return pl.pallas_call(
        functools.partial(finish_kernel, len(pieces)),
        out_shape=field_type,
        in_specs=[in_vmem()] * (4 + len(pieces)),
        out_specs=in_hbm(),
        scratch_shapes=[
            pltpu.VMEM((owned, rhs, size), jnp.float32),
            pltpu.SemaphoreType.DMA((4 if owned % 4 == 0 else 1,)),
        ],
        compiler_params=params(),
        name="finish",
    )(high, low, sol, base, *pieces)[None]


def solution(mesh):
    placed = (
        P("row", "col", None, None, None),
        P("row", "col", None),
        P("row", "col", None),
        P("row", "col"),
        P("col", "row", None, None),
        P("col", "row", None, None),
    )
    return jax.shard_map(
        per_device,
        mesh=mesh,
        in_specs=placed,
        out_specs=P("col", "row", None, None),
        check_vma=False,
    )
```

```python
import functools

import jax
import jax.numpy as jnp
from jax import lax
from jax.experimental import pallas as pl
from jax.experimental.pallas import tpu as pltpu
from jax.sharding import PartitionSpec as P

ITERS = 3
UNROLL = 8
LANES = 4
DEPTH = 6
HIDE_FLOPS = 20_000_000_000
CORES = 2
VMEM_LIMIT = 24 * 1024 * 1024

NT = (((1,), (1,)), ((), ()))
NN = (((1,), (0,)), ((), ()))


def in_vmem():
    return pl.BlockSpec(memory_space=pltpu.VMEM)


def in_hbm():
    return pl.BlockSpec(memory_space=pltpu.HBM)


def in_smem():
    return pl.BlockSpec(memory_space=pltpu.SMEM)


def stay_in_hbm(array):
    return pltpu.with_memory_space_constraint(array, pltpu.HBM)


def params():
    return pltpu.CompilerParams(vmem_limit_bytes=VMEM_LIMIT)


def split(value):
    high = value.astype(jnp.bfloat16)
    low = (value - high.astype(jnp.float32)).astype(jnp.bfloat16)
    return high, low


def times_block(field, high, low):
    field_high, field_low = split(field)
    rhs = field.shape[0]
    both = jnp.concatenate([field_high, field_low], axis=0)
    first = lax.dot_general(both, high, NT, preferred_element_type=jnp.float32)
    second = lax.dot_general(field_high, low, NT, preferred_element_type=jnp.float32)
    return first[:rhs] + (first[rhs:] + second)


def partner(chip, shift, chips):
    if chips & (chips - 1) == 0:
        return chip ^ shift
    return (chip + shift) % chips


def halves(value, size):
    if size & (size - 1) == 0:
        return lax.shift_right_logical(value, size.bit_length() - 1), value & (size - 1)
    return lax.div(value, size), lax.rem(value, size)


def relative(mine, source, groups):
    if groups % 2:
        away = mine - source
        return jnp.where(away < 0, away + groups, away)
    other = (mine ^ source) & 1
    away = (mine ^ other) - source
    away = jnp.where(away < 0, away + groups, away)
    return other * (groups // 2) + lax.shift_right_logical(away, 1)


def gather_stages(groups, parts):
    every = range(parts)
    own = [(0, part) for part in every]
    if groups % 2:
        return [own, [(index, part) for index in range(1, groups) for part in every]]
    pairs = groups // 2
    early = range(parts - 1)
    far, forwarded = range(1, pairs), range(pairs + 1, groups)
    stages = [
        own + [(index, part) for part in early for index in far],
        [(index, parts - 1) for index in far],
        [(pairs, part) for part in every] + [(index, part) for part in early for index in forwarded],
        [(index, parts - 1) for index in forwarded],
    ]
    return [stage for stage in stages if stage]


def ring(groups, step):
    return [(c, (c + step) % groups) for c in range(groups)]


def gather(whole, rounded, groups):
    sets = {(0, 0): whole}
    if groups % 2:
        for step in range(1, groups):
            sets[step, 0] = lax.ppermute(whole, "col", ring(groups, step))
        return sets
    for part, piece in enumerate(rounded):
        for step in range(1, groups // 2):
            sets[step, part] = lax.ppermute(piece, "col", ring(groups, 2 * step))
    sets[groups // 2, 0] = lax.ppermute(whole, "col", neighbours(groups))
    for step in range(1, groups // 2):
        across = [(c, ((c + 2 * step) % groups) ^ 1) for c in range(groups)]
        sets[groups // 2 + step, len(rounded) - 1] = lax.ppermute(rounded[-1], "col", across)
    return sets


def neighbours(count):
    return [(index, index ^ 1) for index in range(count)]


def hold_kernel(piece_ref, token_ref, out_ref):
    pass


def put_rounded(p, value, whole_ref, part_refs):
    part, inner = divmod(p, part_refs[0].shape[0])
    rounded = value.astype(jnp.bfloat16)
    whole_ref[p] = rounded
    part_refs[part][inner] = rounded


def start_kernel(precond_hbm, rhs_hbm, high_ref, low_ref, sol_ref, left_ref, whole_ref, *refs):
    part_refs, (precond_ref, sems) = refs[:-2], refs[-2:]
    owned = left_ref.shape[0]
    parts = sems.shape[0] - 1
    each = owned // parts
    loads = [pltpu.make_async_copy(rhs_hbm, left_ref, sems.at[parts])]
    for part in range(parts):
        at = pl.ds(part * each, each)
        loads.append(pltpu.make_async_copy(precond_hbm.at[at], precond_ref.at[at], sems.at[part]))
    for load in loads:
        load.start()
    loads[0].wait()
    for part in range(parts):
        loads[1 + part].wait()
        for p in range(part * each, (part + 1) * each):
            high, low = split(precond_ref[p])
            high_ref[p] = high
            low_ref[p] = low
            value = times_block(left_ref[p], high, low)
            sol_ref[p] = value
            put_rounded(p, value, whole_ref, part_refs)


def apply_kernel(part, parts, pieces, high_ref, low_ref, left_ref, sol_ref, base_ref, *refs):
    piece_refs, refs = refs[:pieces], refs[pieces:]
    earlier_refs, refs = refs[:-3 - (part == parts - 1)], refs[-3 - (part == parts - 1):]
    new_ref, new_left_ref, rounded_ref, *whole_refs = refs
    each = rounded_ref.shape[0]
    for whole_ref in whole_refs:
        for index, earlier_ref in enumerate(earlier_refs):
            whole_ref[pl.ds(index * each, each)] = earlier_ref[...]
    for inner in range(each):
        p = part * each + inner
        received = sum(piece_ref[p].astype(jnp.float32) for piece_ref in piece_refs)
        value = sol_ref[p] + times_block(base_ref[p] - received, high_ref[p], low_ref[p])
        new_ref[p] = value
        new_left_ref[p] = left_ref[p] - received
        for out_ref, at in [(rounded_ref, inner)] + [(whole_ref, p) for whole_ref in whole_refs]:
            out_ref[at] = value.astype(jnp.bfloat16)


def finish_kernel(pieces, high_ref, low_ref, sol_ref, base_ref, *refs):
    piece_refs, (out_hbm, value_ref, sems) = refs[:pieces], refs[pieces:]
    owned = sol_ref.shape[0]
    parts = sems.shape[0]
    each = owned // parts
    stores = []
    for part in range(parts):
        for p in range(part * each, (part + 1) * each):
            received = sum(piece_ref[p].astype(jnp.float32) for piece_ref in piece_refs)
            value_ref[p] = sol_ref[p] + times_block(base_ref[p] - received, high_ref[p], low_ref[p])
        at = pl.ds(part * each, each)
        stores.append(pltpu.make_async_copy(value_ref.at[at], out_hbm.at[at], sems.at[part]))
        stores[-1].start()
    for store in stores:
        store.wait()


def order_kernel(group, owned, groups, parts, stages, bits, count_ref, rows_hbm, cols_hbm, values_hbm,
                 list_out, total_out, values_out, token_ref, rows_ref, cols_ref, first_ref, base_ref, total_ref,
                 sems):
    token_ref[...] = jnp.zeros_like(token_ref)
    loads = [
        pltpu.make_async_copy(rows_hbm, rows_ref, sems.at[0]),
        pltpu.make_async_copy(cols_hbm, cols_ref, sems.at[1]),
        pltpu.make_async_copy(values_hbm, values_out, sems.at[2]),
    ]
    for load in loads:
        load.start()
    other = 1 - (lax.axis_index("row") & (CORES - 1))
    mine = lax.axis_index("col")
    row_bits, col_bits = bits
    lists = len(stages) * CORES
    each = owned // parts
    trash = (group // CORES) << col_bits
    places = {
        piece: (index * CORES, place * each) for index, stage in enumerate(stages) for place, piece in enumerate(stage)
    }
    own_rows = lax.axis_index("row") * owned
    for source in range(groups):
        piece = relative(mine, source, groups)
        for part in range(parts):
            first, base = places[0, part]
            for index in range(1, groups):
                first = jnp.where(piece == index, places[index, part][0], first)
                base = jnp.where(piece == index, places[index, part][1], base)
            at = halves(source * group + own_rows + part * each, each)[0]
            first_ref[at] = first
            base_ref[at] = base
    for index in range(lists + 1):
        total_ref[index] = 0
    for load in loads[:2]:
        load.wait()
    used = count_ref[0, 0]

    def place(chunk, carry):
        entries = []
        for lane in range(LANES):
            slot = chunk * LANES + lane
            owner, row_inner = halves(halves(rows_ref[0, 0, slot], group)[1], owned)
            at, inner = halves(cols_ref[0, 0, slot], each)
            half = (owner & (CORES - 1)) ^ other
            which = jnp.where(slot < used, first_ref[at] + half, lists)
            row = lax.shift_right_logical(owner, 1) * owned + row_inner
            col = base_ref[at] + inner
            entries.append((which, (((slot << row_bits) | row) << col_bits) | col))
        for which, entry in entries:
            at = total_ref[which]
            list_out[which, at] = entry
            total_ref[which] = at + 1
        return carry

    lax.fori_loop(0, lax.div(used + LANES - 1, LANES), place, 0)
    for index in range(lists):
        total_out[index] = total_ref[index]

    def close(index, carry):
        for extra in range(UNROLL):
            list_out[index, total_ref[index] + extra] = trash
        return carry

    lax.fori_loop(0, lists, close, 0)
    loads[2].wait()


def turn_kernel(total_ref, values_ref, base_ref, turned_ref, same_ref):
    used = sum(total_ref[index] for index in range(total_ref.shape[0]))

    def turn(chunk, carry):
        for lane in range(LANES):
            turned_ref[chunk * LANES + lane] = values_ref[chunk * LANES + lane].T
        return carry

    lax.fori_loop(0, lax.div(used + LANES - 1, LANES), turn, 0)


def add_products(which, bits, dims, list_ref, total_ref, values_ref, field_ref, total):
    row_bits, col_bits = bits

    def step(chunk, carry):
        terms = []

        def store(row, term):
            total[row] += term

        for lane in range(UNROLL):
            entry = list_ref[which, chunk * UNROLL + lane]
            col = entry & ((1 << col_bits) - 1)
            row = lax.shift_right_logical(entry, col_bits) & ((1 << row_bits) - 1)
            slot = lax.shift_right_logical(entry, col_bits + row_bits)
            term = lax.dot_general(field_ref[col], values_ref[slot], dims, preferred_element_type=jnp.float32)
            terms.append((row, term))
            if len(terms) > DEPTH:
                store(*terms.pop(0))
        for row, term in terms:
            store(row, term)
        return carry

    lax.fori_loop(0, lax.div(total_ref[which] + UNROLL - 1, UNROLL), step, 0)


def join(pieces, field):
    if len(pieces) == 1:
        return pieces[0]
    at = 0
    for piece in pieces:
        field[pl.ds(at, piece.shape[0])] = piece[...]
        at += piece.shape[0]
    return field


def swap_order(chips):
    return list(reversed(range(chips)))


def swapped_early(chips):
    return chips - 1


def swapped_rows(index, chips, owned, first_ref, rest_ref):
    early = swapped_early(chips)
    if index < early:
        return first_ref[pl.ds(index * owned, owned)]
    return rest_ref[pl.ds((index - early) * owned, owned)]


def first_kernel(pieces, steps, chips, bits, dims, list_ref, total_ref, values_ref, *refs):
    piece_refs, refs = refs[:pieces], refs[pieces:]
    out_refs, refs = refs[:2 * steps], refs[2 * steps:]
    in_refs, refs = refs[:2 * steps], refs[2 * steps:]
    sent_refs, totals, (token_ref, field) = refs[:-CORES - 2], refs[-CORES - 2:-2], refs[-2:]
    field_ref = join(piece_refs, field)
    token_ref[...] = jnp.zeros_like(token_ref)
    chip = lax.axis_index("row") // CORES
    for half, total in enumerate(totals):
        rows = total.shape[0] - 1
        owned = rows // chips
        if steps == 0:
            total[...] = jnp.zeros(total.shape, jnp.float32)
        else:
            for index, shift in enumerate(swap_order(chips)):
                swapped = in_refs if half else out_refs
                value = sum(
                    swapped_rows(index, chips, owned, *swapped[2 * step:2 * step + 2]).astype(jnp.float32)
                    for step in range(steps))
                if half == 0:
                    value = -value
                elif shift > 0:
                    for step in range(steps):
                        value -= sent_refs[step * (chips - 1) + index][...].astype(jnp.float32)
                total[pl.ds(partner(chip, shift, chips) * owned, owned)] = value
        add_products(half, bits, dims, list_ref, total_ref, values_ref, field_ref, total)


def stage_kernel(stage, bits, dims, pieces, list_ref, total_ref, values_ref, *refs):
    piece_refs, refs = refs[:pieces], refs[pieces + CORES:]
    totals, field = refs[:CORES], refs[-1]
    field_ref = join(piece_refs, field)
    for half, total in enumerate(totals):
        add_products(stage * CORES + half, bits, dims, list_ref, total_ref, values_ref, field_ref, total)


def last_kernel(stage, half, bits, dims, pieces, chips, list_ref, total_ref, values_ref, *refs):
    piece_refs, refs = refs[:pieces], refs[pieces + 1:]
    if half == 0:
        total, out_ref, field = refs
        other = total
    else:
        other, total, out_ref, field = refs
    field_ref = join(piece_refs, field)
    add_products(stage * CORES + half, bits, dims, list_ref, total_ref, values_ref, field_ref, total)
    chip = lax.axis_index("row") // CORES
    owned = (other.shape[0] - 1) // chips
    shifts, early = swap_order(chips), swapped_early(chips)
    for index, shift in enumerate(shifts[early:] if half else shifts[:early]):
        rows = other[pl.ds(partner(chip, shift, chips) * owned, owned)]
        out_ref[pl.ds(index * owned, owned)] = rows.astype(out_ref.dtype)


def chip_rows(index, chips, owned, own_ref, *other_refs):
    chip = lax.axis_index("row") // CORES
    at = pl.ds(partner(chip, swap_order(chips)[index], chips) * owned, owned)
    return own_ref[at] + swapped_rows(index, chips, owned, *other_refs).astype(jnp.float32)


def combine_first_kernel(chips, own_ref, first_ref, *send_refs):
    for index, send_ref in enumerate(send_refs):
        rows = chip_rows(index, chips, send_ref.shape[0], own_ref, first_ref, None)
        send_ref[...] = rows.astype(send_ref.dtype)


def combine_rest_kernel(chips, own_ref, rest_ref, left_ref, sol_ref, before_ref, base_ref, *send_refs):
    owned = base_ref.shape[0]
    for index, send_ref in enumerate(send_refs):
        rows = chip_rows(swapped_early(chips) + index, chips, owned, own_ref, None, rest_ref)
        send_ref[...] = rows.astype(send_ref.dtype)
    keep = chip_rows(chips - 1, chips, owned, own_ref, None, rest_ref)
    base_ref[...] = left_ref[...] - sol_ref[...] - keep


def per_device(block_values, block_rows, block_cols, block_counts, precond, right_side):
    owned, rhs, size = right_side.shape[1:]
    row_devices = lax.axis_size("row")
    groups = lax.axis_size("col")
    chips = row_devices // CORES
    group = owned * row_devices
    half_rows = chips * owned
    slots = block_values.shape[2]

    parts = 2 if owned % 2 == 0 else 1
    stages = gather_stages(groups, parts)
    final = len(stages) - 1
    lists_total = len(stages) * CORES
    widest = max(len(stage) for stage in stages) * owned // parts
    row_bits, col_bits = bits = half_rows.bit_length(), (widest - 1).bit_length()
    assert (slots - 1).bit_length() + row_bits + col_bits <= 31
    assert slots % LANES == 0

    field_type = jax.ShapeDtypeStruct((owned, rhs, size), jnp.float32)
    matrix_type = jax.ShapeDtypeStruct((owned, size, size), jnp.bfloat16)
    total_type = jax.ShapeDtypeStruct((half_rows + 1, rhs, size), jnp.float32)
    index_type = pltpu.SMEM(block_rows.shape, jnp.int32)
    token_type = jax.ShapeDtypeStruct((8, 128), jnp.float32)
    loads = next(count for count in (4, 2, 1) if owned % count == 0)
    rounded_type = jax.ShapeDtypeStruct((owned, rhs, size), jnp.bfloat16)
    part_type = jax.ShapeDtypeStruct((owned // parts, rhs, size), jnp.bfloat16)

    high, low, sol, left, whole, *rounded = pl.pallas_call(
        start_kernel,
        out_shape=[matrix_type] * 2 + [field_type] * 2 + [rounded_type] + [part_type] * parts,
        in_specs=[in_hbm()] * 2,
        out_specs=[in_vmem()] * (5 + parts),
        scratch_shapes=[
            pltpu.VMEM((owned, size, size), jnp.float32),
            pltpu.SemaphoreType.DMA((loads + 1,)),
        ],
        compiler_params=params(),
        name="start",
    )(stay_in_hbm(precond[0]), stay_in_hbm(right_side[0]))

    *lists, values, order_token = pl.pallas_call(
        functools.partial(order_kernel, group, owned, groups, parts, stages, bits),
        out_shape=[
            pltpu.SMEM((lists_total + 1, slots + UNROLL), jnp.int32),
            pltpu.SMEM((lists_total,), jnp.int32),
            pltpu.VMEM(block_values.shape[2:], block_values.dtype),
            token_type,
        ],
        in_specs=[in_smem()] + [in_hbm()] * 3,
        out_specs=[in_smem()] * 2 + [in_vmem()] * 2,
        scratch_shapes=[
            index_type, index_type,
            pltpu.SMEM((groups * row_devices * parts,), jnp.int32),
            pltpu.SMEM((groups * row_devices * parts,), jnp.int32),
            pltpu.SMEM((lists_total + 1,), jnp.int32),
            pltpu.SemaphoreType.DMA((3,)),
        ],
        compiler_params=params(),
        name="order",
    )(block_counts, *[stay_in_hbm(array) for array in (block_rows, block_cols, block_values[0, 0])])

    def turn(values, base):
        return pl.pallas_call(
            turn_kernel,
            out_shape=[pltpu.VMEM(values.shape, values.dtype), field_type],
            in_specs=[in_smem()] + [in_vmem()] * 2,
            out_specs=[in_vmem()] * 2,
            input_output_aliases={2: 1},
            compiler_params=params(),
            cost_estimate=pl.CostEstimate(flops=HIDE_FLOPS, bytes_accessed=0, transcendentals=0),
            name="turn",
        )(lists[1], values, base)

    def cost(share):
        return pl.CostEstimate(
            flops=int(slots * share) * 2 * rhs * size * size,
            bytes_accessed=int(slots * share) * 2 * size * size, transcendentals=0)

    def field_scratch(pieces):
        return pltpu.VMEM((sum(piece.shape[0] for piece in pieces), rhs, size), jnp.bfloat16)

    def product_first(values, dims, pieces, outs, ins, sent):
        return pl.pallas_call(
            functools.partial(first_kernel, len(pieces), len(outs) // 2, chips, bits, dims),
            out_shape=[total_type] * CORES + [token_type],
            in_specs=[in_smem()] * 2 + [in_vmem()] * (1 + len(pieces) + len(outs) + len(ins) + len(sent)),
            out_specs=[in_vmem()] * (CORES + 1),
            compiler_params=params(),
            scratch_shapes=[field_scratch(pieces)],
            cost_estimate=cost(len(stages[0]) / groups / parts),
            name="stage0",
        )(*lists, values, *pieces, *outs, *ins, *sent)

    def product_stage(values, dims, stage, pieces, totals):
        inputs = 3 + len(pieces)
        return pl.pallas_call(
            functools.partial(stage_kernel, stage, bits, dims, len(pieces)),
            out_shape=[total_type] * CORES,
            in_specs=[in_smem()] * 2 + [in_vmem()] * (1 + len(pieces) + CORES),
            out_specs=[in_vmem()] * CORES,
            scratch_shapes=[field_scratch(pieces)],
            input_output_aliases={inputs + half: half for half in range(CORES)},
            compiler_params=params(),
            cost_estimate=cost(len(stages[stage]) / groups / parts),
            name="stage%d" % stage,
        )(*lists, values, *pieces, *totals)

    def product_last(values, dims, half, pieces, total, *other):
        send_chips = chips - swapped_early(chips) if half else swapped_early(chips)
        return pl.pallas_call(
            functools.partial(last_kernel, final, half, bits, dims, len(pieces), chips),
            out_shape=[total_type, jax.ShapeDtypeStruct((send_chips * owned, rhs, size), jnp.bfloat16)],
            in_specs=[in_smem()] * 2 + [in_vmem()] * (2 + len(pieces) + len(other)),
            out_specs=[in_vmem()] * 2,
            scratch_shapes=[field_scratch(pieces)],
            input_output_aliases={3 + len(pieces): 0},
            compiler_params=params(),
            cost_estimate=pl.CostEstimate(
                flops=HIDE_FLOPS if half else 0, bytes_accessed=0, transcendentals=0),
            name="last%d" % half,
        )(*lists, values, *pieces, total, *other)

    def hold(piece, token):
        return pl.pallas_call(
            hold_kernel,
            out_shape=part_type,
            in_specs=[in_vmem()] * 2,
            out_specs=in_vmem(),
            input_output_aliases={0: 0},
            compiler_params=params(),
            name="hold",
        )(piece, token)

    early = swapped_early(chips)

    def combine_first(own, first):
        return pl.pallas_call(
            functools.partial(combine_first_kernel, chips),
            out_shape=[rounded_type] * early,
            in_specs=[in_vmem()] * 2,
            out_specs=[in_vmem()] * early,
            compiler_params=params(),
            name="combine0",
        )(own, first)

    def combine_rest(own, rest, left, sol, before):
        return pl.pallas_call(
            functools.partial(combine_rest_kernel, chips),
            out_shape=[field_type] + [rounded_type] * (chips - 1 - early),
            in_specs=[in_vmem()] * 5,
            out_specs=[in_vmem()] * (chips - early),
            compiler_params=params(),
            name="combine1",
        )(own, rest, left, sol, before)

    def apply(part, sol, left, base, pieces, earlier):
        last = part == parts - 1
        return pl.pallas_call(
            functools.partial(apply_kernel, part, parts, len(pieces)),
            out_shape=[field_type, field_type, part_type] + [rounded_type] * last,
            in_specs=[in_vmem()] * (5 + len(pieces) + len(earlier)),
            out_specs=[in_vmem()] * (3 + last),
            input_output_aliases={2: 1, 3: 0},
            compiler_params=params(),
            cost_estimate=pl.CostEstimate(flops=HIDE_FLOPS, bytes_accessed=0, transcendentals=0),
            name="apply%d" % part,
        )(high, low, left, sol, base, *pieces, *earlier)

    blocks = values, NT
    outs, ins, sent = [], [], []
    for step in range(ITERS):
        sets = gather(whole, rounded, groups)

        def stage_pieces(stage):
            return [sets[piece] for piece in stages[stage] if piece in sets]

        def forward(part, token=None):
            for index in range(1, groups // 2):
                if token is not None:
                    sets[index, part] = hold(sets[index, part], token)
                sets[groups // 2 + index, part] = lax.ppermute(sets[index, part], "col", neighbours(groups))

        if groups % 2 == 0:
            for part in range(parts - 1):
                forward(part, order_token if step == 0 else None)
        *totals, _ = product_first(*blocks, stage_pieces(0), outs, ins, sent)

        for stage in range(1, final):
            totals = product_stage(*blocks, stage, stage_pieces(stage), totals)
        other, out_first = product_last(*blocks, 0, stage_pieces(final), totals[0])
        own, out_rest = product_last(*blocks, 1, stage_pieces(final), totals[1], other)
        outgoing = [out_first, out_rest]
        incoming = [lax.ppermute(rows, "row", neighbours(row_devices)) for rows in outgoing]
        outs += outgoing
        ins += incoming
        first = combine_first(own, incoming[0])
        base, *rest = combine_rest(own, incoming[1], left, sol, first[-1])
        sends = list(first) + rest
        sent += sends
        pieces = [
            lax.ppermute(send, "row", [
                (chip * CORES + core, partner(chip, shift, chips) * CORES + core)
                for chip in range(chips) for core in range(CORES)
            ])
            for shift, send in zip(swap_order(chips), sends)
        ]
        if step == 0:
            turned, base = turn(values, base)
            blocks = turned, NN
        if step < ITERS - 1:
            rounded = []
            for part in range(parts):
                sol, left, new, *done = apply(part, sol, left, base, pieces, rounded if part == parts - 1 else [])
                rounded.append(new)
            whole, = done
    return pl.pallas_call(
        functools.partial(finish_kernel, len(pieces)),
        out_shape=field_type,
        in_specs=[in_vmem()] * (4 + len(pieces)),
        out_specs=in_hbm(),
        scratch_shapes=[
            pltpu.VMEM((owned, rhs, size), jnp.float32),
            pltpu.SemaphoreType.DMA((4 if owned % 4 == 0 else 1,)),
        ],
        compiler_params=params(),
        name="finish",
    )(high, low, sol, base, *pieces)[None]


def solution(mesh):
    placed = (
        P("row", "col", None, None, None),
        P("row", "col", None),
        P("row", "col", None),
        P("row", "col"),
        P("col", "row", None, None),
        P("col", "row", None, None),
    )
    return jax.shard_map(
        per_device,
        mesh=mesh,
        in_specs=placed,
        out_specs=P("col", "row", None, None),
        check_vma=False,
    )
```
